32 devices in a mesh: seq: 8 (over z, y), head: 4 (over x, core).
Axes of the slice: x: 2, y: 2, z: 4, core: 2. Of those that a mesh axis runs over, the one named last changes fastest.
Arguments:
- queries: bfloat16 [2048, 8, 1024], P('seq', 'head')
- keys: bfloat16 [2048, 8, 128], P('seq', 'head')
- values: bfloat16 [2048, 8, 128], P('seq', 'head'), may hold values from -6 to 6
- retrieval_ids: int32 [4], replicated, may hold values from 0 to 7, as said below
- vertical_blocks: int32 [16, 8, 16], P('seq'), may hold values from 0 to 15, as said below
- slash_offsets: int32 [16, 8, 16], P('seq'), may hold values from 0 to 15, as said below
- sink_blocks: int32 [8], replicated, may hold values from 1 to 2
- window_blocks: int32 [8], replicated, may hold values from 1 to 5
Outputs:
- attended: bfloat16 [2048, 8, 1024], P('seq', 'head')
The draws below stay inside these ranges and needn't reach their ends.
Inputs may be any that keep to these rules, and one draw needn't show every extreme that they name: `retrieval_ids`: 4 different KV head numbers in increasing order. `vertical_blocks`: each entry is at most the index of its query block (dimension 0). `slash_offsets`: each entry is at most the index of its query block (dimension 0).
All inputs are finite; a program needn't handle non-finite values.
Results may differ from the reference program's by a relative error of at most 0.0044.
Values may be sent and summed in bfloat16 or wider, within the bound.
No kernel may reach another device: no remote copies, remote signals or barrier semaphores. Data moves between devices by JAX's collectives and lax.ppermute only.
A program may use at most 128 MiB of HBM per device.

```python
import jax
import jax.numpy as jnp
from jax import lax

KV_HEADS = 8
GROUP = 8
HEAD_DIM = 128
BLOCK = 128
VERT = 16
SLASH = 16
RETR = 4
SINK_MAX = 2
WIN_MAX = 5
TOKENS = 2048
QBLOCKS = 16


def pick_retrieval(key):
    order = jax.random.permutation(jax.random.fold_in(key, 101), KV_HEADS)
    return jnp.sort(order[:RETR]).astype(jnp.int32)


def running_pick(key, salt):
    chosen_ids = pick_retrieval(key)
    flags = jnp.any(jnp.arange(KV_HEADS)[:, None] == chosen_ids[None, :], axis=1).astype(jnp.int32)
    order = jax.random.permutation(jax.random.fold_in(key, salt), KV_HEADS)
    ranking = jnp.arange(KV_HEADS, dtype=jnp.int32) + KV_HEADS * flags[order]
    return order[jnp.argmin(ranking)]


def draw_retrieval_ids(key, part):
    return pick_retrieval(key)


def draw_window_blocks(key, part):
    base_draw = jax.random.randint(jax.random.fold_in(key, 201), (KV_HEADS,), 1, WIN_MAX + 1)
    widest = running_pick(key, 202)
    return jnp.where(jnp.arange(KV_HEADS) == widest, WIN_MAX, base_draw).astype(jnp.int32)


def draw_sink_blocks(key, part):
    base_draw = jax.random.randint(jax.random.fold_in(key, 301), (KV_HEADS,), 1, SINK_MAX + 1)
    widest = running_pick(key, 302)
    return jnp.where(jnp.arange(KV_HEADS) == widest, SINK_MAX, base_draw).astype(jnp.int32)


def draw_vertical_blocks(key, part):
    upper = jnp.arange(QBLOCKS, dtype=jnp.int32)[:, None, None] + 1
    return jax.random.randint(jax.random.fold_in(key, 401), (QBLOCKS, KV_HEADS, VERT), 0, upper).astype(jnp.int32)


def draw_slash_offsets(key, part):
    upper = jnp.arange(QBLOCKS, dtype=jnp.int32)[:, None, None] + 1
    return jax.random.randint(jax.random.fold_in(key, 501), (QBLOCKS, KV_HEADS, SLASH), 0, upper).astype(jnp.int32)


def draw_queries(key, part):
    base_draw = jax.random.normal(jax.random.fold_in(key, 601), (TOKENS, KV_HEADS, GROUP * HEAD_DIM), jnp.float32)
    return base_draw.astype(jnp.bfloat16)


def draw_keys(key, part):
    base_draw = jax.random.normal(jax.random.fold_in(key, 611), (TOKENS, KV_HEADS, HEAD_DIM), jnp.float32)
    return base_draw.astype(jnp.bfloat16)


def levels(key, shape, shards, least, largest):
    def one(dim, parts):
        steps = jax.random.uniform(jax.random.fold_in(jax.random.fold_in(key, 6), dim), (parts,), jnp.float32, least / len(shards), largest / len(shards))
        return jnp.repeat(jnp.exp(steps), shape[dim] // parts).reshape((-1,) + (1,) * (len(shape) - dim - 1))

    loudness = one(*shards[0])
    for cut in shards[1:]:
        loudness = loudness * one(*cut)
    return loudness


def normal_values(rng, extent, scale, bound, shards=(), kind=jnp.bfloat16):
    factor_of = levels(rng, extent, shards, -0.22, 0.18) if shards else 1.0
    values = jax.random.normal(rng, extent, jnp.float32) * scale * factor_of
    return jnp.minimum(jnp.maximum(values, -bound), bound).astype(kind)


def setup_inputs(seed: int = 0) -> dict:
    key_of = jax.random.split(jax.random.key(seed), 9)
    queries = draw_queries(jax.random.fold_in(key_of[8], 71), 0)
    keys = draw_keys(jax.random.fold_in(key_of[8], 71), 0)
    values = normal_values(key_of[2], (TOKENS, KV_HEADS, HEAD_DIM), 1.0, 6.0, ((0, 8), (1, 4)))
    retrieval_ids = draw_retrieval_ids(jax.random.fold_in(key_of[8], 71), 0)
    vertical_blocks = draw_vertical_blocks(jax.random.fold_in(key_of[8], 71), 0)
    slash_offsets = draw_slash_offsets(jax.random.fold_in(key_of[8], 71), 0)
    sink_blocks = draw_sink_blocks(jax.random.fold_in(key_of[8], 71), 0)
    window_blocks = draw_window_blocks(jax.random.fold_in(key_of[8], 71), 0)
    return {"queries": queries, "keys": keys, "values": values, "retrieval_ids": retrieval_ids, "vertical_blocks": vertical_blocks, "slash_offsets": slash_offsets, "sink_blocks": sink_blocks, "window_blocks": window_blocks}


masked_score = -1.0e30


def candidate_blocks(head_id, query_block, is_retrieval, vertical_blocks, slash_offsets, sink_blocks, window_blocks):
    listed = jnp.concatenate([
        jnp.reshape(query_block, (1,)).astype(jnp.int32),
        vertical_blocks[query_block, head_id].astype(jnp.int32),
        (query_block - slash_offsets[query_block, head_id]).astype(jnp.int32)])
    width_all = listed.shape[0]
    earlier = jnp.arange(width_all)[:, None] > jnp.arange(width_all)[None, :]
    repeated = jnp.any(earlier & (listed[:, None] == listed[None, :]), axis=1)
    listed_ok = jnp.logical_not(repeated) & (listed <= query_block) & (listed >= 0)
    sink_ids = jnp.arange(SINK_MAX, dtype=jnp.int32)
    window_ids = (query_block - jnp.arange(WIN_MAX, dtype=jnp.int32)).astype(jnp.int32)
    sink_ok = (sink_ids < sink_blocks[head_id]) & (sink_ids <= query_block)
    window_ok = (window_ids > query_block - window_blocks[head_id]) & (window_ids >= sink_blocks[head_id]) & (window_ids >= 0)
    padding = width_all - SINK_MAX - WIN_MAX
    read = jnp.concatenate([sink_ids, window_ids, jnp.zeros((padding,), jnp.int32)])
    read_ok = jnp.concatenate([sink_ok, window_ok, jnp.zeros((padding,), bool)])
    chosen = jnp.where(is_retrieval, listed, read)
    usable = jnp.where(is_retrieval, listed_ok, read_ok)
    return chosen, usable


def reference(queries, keys, values, retrieval_ids, vertical_blocks, slash_offsets, sink_blocks, window_blocks):
    score_scale = HEAD_DIM ** -0.5
    key_tiles = keys.astype(jnp.float32).reshape(QBLOCKS, BLOCK, KV_HEADS, HEAD_DIM)
    value_tiles = values.astype(jnp.float32).reshape(QBLOCKS, BLOCK, KV_HEADS, HEAD_DIM)
    query_tiles = queries.astype(jnp.float32).reshape(QBLOCKS, BLOCK, KV_HEADS, GROUP, HEAD_DIM)
    retrieval_flags = jnp.any(jnp.arange(KV_HEADS, dtype=jnp.int32)[:, None] == retrieval_ids[None, :], axis=1)
    offsets = jnp.arange(BLOCK, dtype=jnp.int32)

    def per_head(head_id):
        is_retrieval = retrieval_flags[head_id]
        head_keys = jnp.take(key_tiles, head_id, axis=2)
        head_values = jnp.take(value_tiles, head_id, axis=2)
        head_queries = jnp.take(query_tiles, head_id, axis=2)

        def per_block(query_block):
            chosen, usable = candidate_blocks(head_id, query_block, is_retrieval, vertical_blocks, slash_offsets, sink_blocks, window_blocks)
            safe_ids = jnp.clip(chosen, 0, QBLOCKS - 1)
            key_rows = head_keys[safe_ids]
            value_rows = head_values[safe_ids]
            query_rows = head_queries[query_block]
            scores = jnp.einsum('tgd,csd->gtcs', query_rows, key_rows) * score_scale
            query_pos = query_block * BLOCK + offsets
            key_pos = chosen[:, None] * BLOCK + offsets[None, :]
            visible = usable[None, :, None] & (key_pos[None, :, :] <= query_pos[:, None, None])
            scores = jnp.where(visible[None], scores, masked_score)
            row_peak = jnp.max(scores, axis=(2, 3), keepdims=True)
            expo = jnp.exp(scores - row_peak)
            row_total = jnp.sum(expo, axis=(2, 3))
            rounded = lax.optimization_barrier(expo.astype(jnp.bfloat16)).astype(jnp.float32)
            mixed = jnp.einsum('gtcs,csd->tgd', rounded, value_rows) / jnp.transpose(row_total)[:, :, None]
            return mixed.reshape(BLOCK, GROUP * HEAD_DIM)

        return lax.map(per_block, jnp.arange(QBLOCKS, dtype=jnp.int32))

    result = lax.map(per_head, jnp.arange(KV_HEADS, dtype=jnp.int32))
    return jnp.transpose(result, (1, 2, 0, 3)).reshape(TOKENS, KV_HEADS, GROUP * HEAD_DIM).astype(jnp.bfloat16)
```

```python
import functools
import math

import jax
import jax.numpy as jnp
from jax import lax
from jax.experimental import pallas as pl
from jax.experimental.pallas import tpu as pltpu
from jax.sharding import PartitionSpec as P

KV_HEADS = 8
BLOCK = 128
INNER = 2
ROW_TILE = 256
HIDDEN = -1e30
SAFE_TOTAL = 1e30


def allowed_blocks(
    vertical_blocks, slash_offsets, retrieval_ids, sink_blocks, window_blocks, first_block,
    first_head, heads, block_total,
):
    blocks_here = vertical_blocks.shape[0]
    vert = lax.dynamic_slice_in_dim(vertical_blocks, first_head, heads, axis=1)
    slash = lax.dynamic_slice_in_dim(slash_offsets, first_head, heads, axis=1)
    sinks = lax.dynamic_slice_in_dim(sink_blocks, first_head, heads)
    windows = lax.dynamic_slice_in_dim(window_blocks, first_head, heads)
    head_ids = first_head + jnp.arange(heads, dtype=jnp.int32)
    is_retr = jnp.any(head_ids[:, None] == retrieval_ids[None, :], axis=1)
    query_block = first_block + jnp.arange(blocks_here, dtype=jnp.int32)[:, None, None]
    key_block = jnp.arange(block_total, dtype=jnp.int32)[None, None, :]
    listed = jnp.any(vert[..., None] == key_block[:, :, None, :], axis=2)
    listed |= jnp.any(query_block[..., None] - slash[..., None] == key_block[:, :, None, :], axis=2)
    listed |= key_block == query_block
    read = (key_block < sinks[None, :, None]) | (key_block > query_block - windows[None, :, None])
    allowed = jnp.where(is_retr[None, :, None], listed, read) & (key_block <= query_block)
    return jnp.transpose(allowed, (1, 0, 2)).astype(jnp.int32)


def attend_kernel(
    n_slots, group, heads, blocks_here, block_total, score_scale, pos_ref, allowed_ref, q_ref, *refs
):
    piece_refs = refs[:n_slots]
    out_ref, kv, block_list, peak, total, acc, out_rows, sems = refs[n_slots:]
    outer = n_slots // INNER
    rows_unit = BLOCK * group
    seq_pos = pos_ref[0]
    first_block = seq_pos * blocks_here
    factor = score_scale * math.log2(math.e)

    copies = [
        pltpu.make_async_copy(piece_refs[i], kv.at[i], sems.at[i]) for i in range(n_slots)
    ]
    for copy in copies:
        copy.start()

    def place(c):
        owner = c // blocks_here
        away = seq_pos // INNER - owner // INNER
        other_column = (owner % INNER) != (seq_pos % INNER)
        slot = jnp.where(other_column, outer + away, away)
        return slot, pl.multiple_of((c % blocks_here) * BLOCK, BLOCK)

    def load(which, c):
        slot, row = place(c)
        return kv[slot, which, pl.ds(row, BLOCK), :]

    def both(which, c0, c1):
        return jnp.concatenate([load(which, c0), load(which, c1)], axis=0)

    for copy in copies:
        copy.wait()

    def unit(u, carry):
        h = u // blocks_here
        b = u % blocks_here
        query_block = first_block + b

        def collect(c, n):
            block_list[n] = c
            return n + allowed_ref[h, b, c]

        n = lax.fori_loop(0, query_block, collect, jnp.int32(0))
        has_other = n % 2
        n_pairs = n // 2
        other = jnp.where(has_other == 1, block_list[jnp.maximum(n - 1, 0)], query_block)

        def q_tile(r):
            start = pl.multiple_of(b * rows_unit + r * ROW_TILE, ROW_TILE)
            return q_ref[h, pl.ds(start, ROW_TILE), :]

        def scores(r, keys):
            s = lax.dot_general(
                q_tile(r), keys, (((1,), (1,)), ((), ())), preferred_element_type=jnp.float32
            )
            return s * factor

        tiles = range(rows_unit // ROW_TILE)

        def first_scores(r, keys):
            s = scores(r, keys)
            token = (r * ROW_TILE + lax.broadcasted_iota(jnp.int32, s.shape, 0)) // group
            column = lax.broadcasted_iota(jnp.int32, s.shape, 1)
            seen = ((column < BLOCK) & (has_other == 1)) | (
                (column >= BLOCK) & (column - BLOCK <= token)
            )
            return jnp.where(seen, s, HIDDEN)

        def add(r, s, vals, first):
            rows = pl.ds(r * ROW_TILE, ROW_TILE)
            m = peak[rows, :]
            p = jnp.exp2(s - jnp.concatenate([m, m], axis=1))
            part = p[:, :BLOCK] + p[:, BLOCK:]
            mixed = jnp.dot(p.astype(jnp.bfloat16), vals, preferred_element_type=jnp.float32)
            if first:
                total[rows, :] = part
                acc[rows, :] = mixed
            else:
                total[rows, :] += part
                acc[rows, :] += mixed

        def first_chunk(set_peak):
            keys = both(h, other, query_block)
            vals = both(heads + h, other, query_block)
            for r in tiles:
                s = first_scores(r, keys)
                if set_peak:
                    m = jnp.max(s, axis=1, keepdims=True)
                    peak[pl.ds(r * ROW_TILE, ROW_TILE), :] = jnp.broadcast_to(
                        m, (ROW_TILE, BLOCK)
                    )
                add(r, s, vals, True)

        def pair(i, c):
            c0, c1 = block_list[2 * i], block_list[2 * i + 1]
            keys = both(h, c0, c1)
            vals = both(heads + h, c0, c1)
            for r in tiles:
                add(r, scores(r, keys), vals, False)
            return c

        first_chunk(True)
        lax.fori_loop(0, n_pairs, pair, 0)
        row_total = jnp.sum(total[...], axis=1, keepdims=True)
        largest = jnp.max(row_total)

        @pl.when(jnp.logical_not(largest < SAFE_TOTAL))
        def _():
            def widen(i, c):
                keys = both(h, block_list[2 * i], block_list[2 * i + 1])
                for r in tiles:
                    rows = pl.ds(r * ROW_TILE, ROW_TILE)
                    m = jnp.max(scores(r, keys), axis=1, keepdims=True)
                    peak[rows, :] = jnp.maximum(peak[rows, :], m)
                return c

            lax.fori_loop(0, n_pairs, widen, 0)
            first_chunk(False)
            lax.fori_loop(0, n_pairs, pair, 0)

        row_total = jnp.sum(total[...], axis=1, keepdims=True)
        out_rows[pl.ds(b * rows_unit * heads + h, rows_unit, stride=heads), :] = (
            acc[...] / row_total
        )
        return carry

    lax.fori_loop(0, heads * blocks_here, unit, 0)
    out_ref[...] = out_rows[...].astype(out_ref.dtype)


def attend(pos, allowed, q, pieces, score_scale):
    n_slots = len(pieces)
    heads, blocks_here, block_total = allowed.shape
    rows, head_dim = q.shape[1:]
    group = rows // (blocks_here * BLOCK)
    body = functools.partial(
        attend_kernel, n_slots, group, heads, blocks_here, block_total, score_scale
    )
    smem = pl.BlockSpec(memory_space=pltpu.SMEM)
    vmem = pl.BlockSpec(memory_space=pltpu.VMEM)
    rows_unit = BLOCK * group
    return pl.pallas_call(
        body,
        out_shape=jax.ShapeDtypeStruct((rows * heads, head_dim), jnp.bfloat16),
        in_specs=[smem, smem, vmem] + [pl.BlockSpec(memory_space=pl.ANY)] * n_slots,
        out_specs=vmem,
        scratch_shapes=[
            pltpu.VMEM((n_slots,) + pieces[0].shape, jnp.bfloat16),
            pltpu.SMEM((block_total + 1,), jnp.int32),
            pltpu.VMEM((rows_unit, head_dim), jnp.float32),
            pltpu.VMEM((rows_unit, head_dim), jnp.float32),
            pltpu.VMEM((rows_unit, head_dim), jnp.float32),
            pltpu.VMEM((rows * heads, head_dim), jnp.float32),
            pltpu.SemaphoreType.DMA((n_slots,)),
        ],
        compiler_params=pltpu.CompilerParams(vmem_limit_bytes=48 * 1024 * 1024),
    )(pos, allowed, q, *pieces)


def per_device(
    n_seq, queries, keys, values, retrieval_ids, vertical_blocks, slash_offsets, sink_blocks,
    window_blocks,
):
    tokens_here, heads, width = queries.shape
    head_dim = keys.shape[2]
    group = width // head_dim
    blocks_here = tokens_here // BLOCK
    outer = n_seq // INNER
    seq_pos = lax.axis_index("seq")

    own = jnp.concatenate(
        [jnp.transpose(keys, (1, 0, 2)), jnp.transpose(values, (1, 0, 2))], axis=0
    )
    column = [own]
    for step in range(1, outer):
        pairs = [(s, s + INNER) for s in range(n_seq - INNER) if s // INNER >= step - 1]
        column.append(lax.ppermute(column[-1], "seq", pairs))
    crossed = []
    for step in range(outer):
        pairs = [
            (s, s ^ 1) for s in range(n_seq)
            if s // INNER >= step and (step > 0 or s % INNER == 0)
        ]
        crossed.append(lax.ppermute(column[step], "seq", pairs))

    allowed = allowed_blocks(
        vertical_blocks, slash_offsets, retrieval_ids, sink_blocks, window_blocks,
        seq_pos * blocks_here, lax.axis_index("head") * heads, heads, n_seq * blocks_here,
    )
    q = queries.reshape(tokens_here, heads, group, head_dim)
    q = jnp.transpose(q, (1, 0, 2, 3)).reshape(heads, tokens_here * group, head_dim)
    pos = jnp.reshape(seq_pos, (1,)).astype(jnp.int32)
    out = attend(pos, allowed, q, column + crossed, head_dim ** -0.5)
    out = out.reshape(tokens_here, group, heads, head_dim)
    return jnp.transpose(out, (0, 2, 1, 3)).reshape(tokens_here, heads, width)


def solution(mesh):
    in_specs = (
        P("seq", "head", None),
        P("seq", "head", None),
        P("seq", "head", None),
        P(),
        P("seq", None, None),
        P("seq", None, None),
        P(),
        P(),
    )
    out_specs = P("seq", "head", None)
    return jax.shard_map(
        functools.partial(per_device, mesh.shape["seq"]),
        mesh=mesh, in_specs=in_specs, out_specs=out_specs, check_vma=False,
    )
```

```python
import functools
import math

import jax
import jax.numpy as jnp
from jax import lax
from jax.experimental import pallas as pl
from jax.experimental.pallas import tpu as pltpu
from jax.sharding import PartitionSpec as P

KV_HEADS = 8
BLOCK = 128
INNER = 2
ROW_TILE = 256
HIDDEN = -1e30
PENALTY = 1e30
SAFE_TOTAL = 1e30


def allowed_blocks(
    vertical_blocks, slash_offsets, retrieval_ids, sink_blocks, window_blocks, first_block,
    first_head, heads, block_total,
):
    blocks_here = vertical_blocks.shape[0]
    vert = lax.dynamic_slice_in_dim(vertical_blocks, first_head, heads, axis=1)
    slash = lax.dynamic_slice_in_dim(slash_offsets, first_head, heads, axis=1)
    sinks = lax.dynamic_slice_in_dim(sink_blocks, first_head, heads)
    windows = lax.dynamic_slice_in_dim(window_blocks, first_head, heads)
    head_ids = first_head + jnp.arange(heads, dtype=jnp.int32)
    is_retr = jnp.any(head_ids[:, None] == retrieval_ids[None, :], axis=1)
    query_block = first_block + jnp.arange(blocks_here, dtype=jnp.int32)[:, None, None]
    key_block = jnp.arange(block_total, dtype=jnp.int32)[None, None, :]
    listed = jnp.any(vert[..., None] == key_block[:, :, None, :], axis=2)
    listed |= jnp.any(query_block[..., None] - slash[..., None] == key_block[:, :, None, :], axis=2)
    listed |= key_block == query_block
    read = (key_block < sinks[None, :, None]) | (key_block > query_block - windows[None, :, None])
    allowed = jnp.where(is_retr[None, :, None], listed, read) & (key_block <= query_block)
    return jnp.transpose(allowed, (1, 0, 2)).astype(jnp.int32)


class Shape:
    def __init__(self, heads, blocks_here, block_total, group, head_dim):
        self.heads = heads
        self.blocks_here = blocks_here
        self.block_total = block_total
        self.group = group
        self.head_dim = head_dim
        self.rows_unit = BLOCK * group
        self.rows = blocks_here * self.rows_unit
        self.factor = head_dim ** -0.5 * math.log2(math.e)


def owner_of(seq_pos, crossed, away):
    line = seq_pos // INNER - away
    place = seq_pos % INNER
    return line * INNER + (1 - place if crossed else place)


def scores(q, keys):
    return lax.dot_general(q, keys, (((1,), (1,)), ((), ())), preferred_element_type=jnp.float32)


def with_ones(vals):
    return jnp.concatenate([vals, jnp.ones_like(vals)], axis=1)


def tiles_of(shape):
    return [(b, r * ROW_TILE) for b in range(shape.blocks_here)
            for r in range(shape.rows_unit // ROW_TILE)]


def first_kernel(shape, pos_ref, allowed_ref, q_ref, own_ref, peak_ref, acc_ref):
    first_block = pos_ref[0] * shape.blocks_here

    def head(h, carry):
        for b, start in tiles_of(shape):
            rows = pl.ds(b * shape.rows_unit + start, ROW_TILE)
            width = (b + 1) * BLOCK
            s = scores(q_ref[h, rows, :], own_ref[h, :width, :]) * shape.factor
            columns = []
            for j in range(b):
                seen = allowed_ref[h, b, first_block + j] > 0
                columns.append(s[:, j * BLOCK:(j + 1) * BLOCK] - jnp.where(seen, 0.0, PENALTY))
            diagonal = s[:, b * BLOCK:]
            row = start + lax.broadcasted_iota(jnp.int32, diagonal.shape, 0)
            column = lax.broadcasted_iota(jnp.int32, diagonal.shape, 1)
            columns.append(jnp.where(column * shape.group <= row, diagonal, HIDDEN))
            s = jnp.concatenate(columns, axis=1)
            m = jnp.max(s, axis=1, keepdims=True)
            peak_ref[h, rows, :] = jnp.broadcast_to(m, (ROW_TILE, BLOCK))
            p = jnp.exp2(s - m).astype(jnp.bfloat16)
            vals = with_ones(own_ref[shape.heads + h, :width, :])
            acc_ref[h, rows, :] = jnp.dot(p, vals, preferred_element_type=jnp.float32)
        return carry

    lax.fori_loop(0, shape.heads, head, 0)


def add_pieces(shape, slots, pos_ref, allowed_ref, q_ref, peak_ref, piece_refs, acc_ref):
    seq_pos = pos_ref[0]
    owners = [owner_of(seq_pos, crossed, away) for crossed, away in slots]

    def head(h, carry):
        flags = []
        for b in range(shape.blocks_here):
            row = []
            for owner in owners:
                there = (owner >= 0) & (owner < seq_pos)
                base = jnp.where(there, owner, 0) * shape.blocks_here
                for j in range(shape.blocks_here):
                    row.append(there & (allowed_ref[h, b, base + j] > 0))
            flags.append(row)
        some = functools.reduce(jnp.logical_or, [f for row in flags for f in row])

        @pl.when(some)
        def _():
            keys = jnp.concatenate([ref[h] for ref in piece_refs], axis=0)
            vals = with_ones(
                jnp.concatenate([ref[shape.heads + h] for ref in piece_refs], axis=0)
            )
            for b, start in tiles_of(shape):
                rows = pl.ds(b * shape.rows_unit + start, ROW_TILE)
                s = scores(q_ref[h, rows, :], keys) * shape.factor
                m = peak_ref[h, rows, :]
                shift = jnp.concatenate(
                    [m + jnp.where(f, 0.0, PENALTY) for f in flags[b]], axis=1
                )
                p = jnp.exp2(s - shift).astype(jnp.bfloat16)
                acc_ref[h, rows, :] += jnp.dot(p, vals, preferred_element_type=jnp.float32)

        return carry

    lax.fori_loop(0, shape.heads, head, 0)


def middle_kernel(shape, slots, pos_ref, allowed_ref, q_ref, peak_ref, acc_in, *refs):
    del acc_in
    add_pieces(
        shape, slots, pos_ref, allowed_ref, q_ref, peak_ref, refs[:len(slots)], refs[len(slots)]
    )


def last_kernel(
    shape, slots, all_slots, pos_ref, allowed_ref, q_ref, peak_ref, acc_in, *refs
):
    del acc_in
    n, n_all = len(slots), len(all_slots)
    piece_refs, all_refs = refs[:n], refs[n:n + n_all]
    out_ref, acc_ref, out_rows, kv, owner_list, sems = refs[n + n_all:]
    seq_pos = pos_ref[0]
    first_block = seq_pos * shape.blocks_here
    add_pieces(shape, slots, pos_ref, allowed_ref, q_ref, peak_ref, piece_refs, acc_ref)

    def finish():
        worst = jnp.zeros((8, shape.head_dim), jnp.float32)
        for h in range(shape.heads):
            for start in range(0, shape.rows, ROW_TILE):
                sums = acc_ref[h, pl.ds(start, ROW_TILE), :]
                total = sums[:, shape.head_dim:]
                bad = jnp.where(total < SAFE_TOTAL, 0.0, 1.0)
                worst = jnp.maximum(
                    worst, jnp.max(bad.reshape(ROW_TILE // 8, 8, shape.head_dim), axis=0)
                )
                out_rows[pl.ds(start * shape.heads + h, ROW_TILE, stride=shape.heads), :] = (
                    sums[:, :shape.head_dim] / total
                )
        out_ref[...] = out_rows[...].astype(out_ref.dtype)
        return worst

    worst = finish()

    @pl.when(jnp.max(worst) > 0.0)
    def _():
        copies = [pltpu.make_async_copy(all_refs[i], kv.at[i], sems.at[i]) for i in range(n_all)]
        for copy in copies:
            copy.start()
        for i, (crossed, away) in enumerate(all_slots):
            owner_list[i] = owner_of(seq_pos, crossed, away)
        for copy in copies:
            copy.wait()

        def every_tile(step):
            def slot_step(i, carry):
                owner = owner_list[i]

                @pl.when((owner >= 0) & (owner <= seq_pos))
                def _():
                    for h in range(shape.heads):
                        for b, start in tiles_of(shape):
                            rows = pl.ds(b * shape.rows_unit + start, ROW_TILE)
                            s = scores(q_ref[h, rows, :], kv[i, h]) * shape.factor
                            columns = []
                            for j in range(shape.blocks_here):
                                block = owner * shape.blocks_here + j
                                part = s[:, j * BLOCK:(j + 1) * BLOCK]
                                row = start + lax.broadcasted_iota(jnp.int32, part.shape, 0)
                                column = lax.broadcasted_iota(jnp.int32, part.shape, 1)
                                ahead = (first_block + b - block) * BLOCK
                                part = jnp.where(
                                    (column - ahead) * shape.group <= row, part, HIDDEN
                                )
                                seen = allowed_ref[h, b, block] > 0
                                columns.append(part - jnp.where(seen, 0.0, PENALTY))
                            step(h, rows, jnp.concatenate(columns, axis=1), i)

                return carry

            lax.fori_loop(0, n_all, slot_step, 0)

        def widen(h, rows, s, i):
            m = jnp.max(s, axis=1, keepdims=True)
            peak_ref[h, rows, :] = jnp.maximum(peak_ref[h, rows, :], m)

        def collect(h, rows, s, i):
            m = peak_ref[h, rows, :]
            shift = jnp.concatenate([m] * shape.blocks_here, axis=1)
            p = jnp.exp2(s - shift).astype(jnp.bfloat16)
            acc_ref[h, rows, :] += jnp.dot(
                p, with_ones(kv[i, shape.heads + h]), preferred_element_type=jnp.float32
            )

        every_tile(widen)
        acc_ref[...] = jnp.zeros_like(acc_ref)
        every_tile(collect)
        finish()


def per_device(
    n_seq, queries, keys, values, retrieval_ids, vertical_blocks, slash_offsets, sink_blocks,
    window_blocks,
):
    tokens_here, heads, width = queries.shape
    head_dim = keys.shape[2]
    group = width // head_dim
    blocks_here = tokens_here // BLOCK
    outer = n_seq // INNER
    seq_pos = lax.axis_index("seq")
    shape = Shape(heads, blocks_here, n_seq * blocks_here, group, head_dim)

    own = jnp.concatenate(
        [jnp.transpose(keys, (1, 0, 2)), jnp.transpose(values, (1, 0, 2))], axis=0
    )
    column = [own]
    crossed = []
    for step in range(outer):
        pairs = [
            (s, s ^ 1) for s in range(n_seq)
            if s // INNER >= step and (step > 0 or s % INNER == 0)
        ]
        crossed.append(lax.ppermute(column[step], "seq", pairs))
        if step + 1 < outer:
            pairs = [(s, s + INNER) for s in range(n_seq - INNER) if s // INNER >= step]
            column.append(lax.ppermute(column[step], "seq", pairs))

    allowed = allowed_blocks(
        vertical_blocks, slash_offsets, retrieval_ids, sink_blocks, window_blocks,
        seq_pos * blocks_here, lax.axis_index("head") * heads, heads, shape.block_total,
    )
    q = queries.reshape(tokens_here, heads, group, head_dim)
    q = jnp.transpose(q, (1, 0, 2, 3)).reshape(heads, tokens_here * group, head_dim)
    pos = jnp.reshape(seq_pos, (1,)).astype(jnp.int32)

    smem = pl.BlockSpec(memory_space=pltpu.SMEM)
    vmem = pl.BlockSpec(memory_space=pltpu.VMEM)
    anywhere = pl.BlockSpec(memory_space=pl.ANY)
    peak_shape = jax.ShapeDtypeStruct((heads, shape.rows, head_dim), jnp.float32)
    acc_shape = jax.ShapeDtypeStruct((heads, shape.rows, 2 * head_dim), jnp.float32)
    params = pltpu.CompilerParams(vmem_limit_bytes=16 * 1024 * 1024)

    def cost(key_count):
        pairs = heads * shape.rows * key_count
        return pl.CostEstimate(
            flops=6 * pairs * head_dim, transcendentals=pairs, bytes_accessed=1 << 20
        )

    peak, acc = pl.pallas_call(
        functools.partial(first_kernel, shape),
        out_shape=(peak_shape, acc_shape),
        in_specs=[smem, smem, vmem, vmem],
        out_specs=(vmem, vmem),
        compiler_params=params,
        cost_estimate=cost(tokens_here),
    )(pos, allowed, q, own)

    for step in range(1, outer):
        slots = [(False, step), (True, step - 1)]
        acc = pl.pallas_call(
            functools.partial(middle_kernel, shape, slots),
            out_shape=acc_shape,
            in_specs=[smem, smem, vmem, vmem, vmem, vmem, vmem],
            out_specs=vmem,
            input_output_aliases={4: 0},
            compiler_params=params,
            cost_estimate=cost(2 * tokens_here),
        )(pos, allowed, q, peak, acc, column[step], crossed[step - 1])

    slots = [(True, outer - 1)]
    all_slots = [(False, a) for a in range(outer)] + [(True, a) for a in range(outer)]
    n_all = len(all_slots)
    out, _, _ = pl.pallas_call(
        functools.partial(last_kernel_aliased, shape, slots, all_slots),
        out_shape=(
            jax.ShapeDtypeStruct((heads * shape.rows, head_dim), jnp.bfloat16),
            peak_shape,
            acc_shape,
        ),
        in_specs=[smem, smem, vmem, vmem, vmem, vmem] + [anywhere] * n_all,
        out_specs=(vmem, vmem, vmem),
        input_output_aliases={3: 1, 4: 2},
        scratch_shapes=[
            pltpu.VMEM((heads * shape.rows, head_dim), jnp.float32),
            pltpu.VMEM((n_all,) + own.shape, jnp.bfloat16),
            pltpu.SMEM((n_all,), jnp.int32),
            pltpu.SemaphoreType.DMA((n_all,)),
        ],
        compiler_params=pltpu.CompilerParams(
            vmem_limit_bytes=(16 << 20) + 2 * n_all * own.size
        ),
        cost_estimate=cost(tokens_here),
    )(pos, allowed, q, peak, acc, crossed[outer - 1], *column, *crossed)
    out = out.reshape(tokens_here, group, heads, head_dim)
    return jnp.transpose(out, (0, 2, 1, 3)).reshape(tokens_here, heads, width)


def last_kernel_aliased(
    shape, slots, all_slots, pos_ref, allowed_ref, q_ref, peak_in, acc_in, *refs
):
    del peak_in
    n_in = len(slots) + len(all_slots)
    out_ref, peak_ref, acc_ref = refs[n_in:n_in + 3]
    last_kernel(
        shape, slots, all_slots, pos_ref, allowed_ref, q_ref, peak_ref, acc_in,
        *refs[:n_in], out_ref, acc_ref, *refs[n_in + 3:],
    )


def solution(mesh):
    in_specs = (
        P("seq", "head", None),
        P("seq", "head", None),
        P("seq", "head", None),
        P(),
        P("seq", None, None),
        P("seq", None, None),
        P(),
        P(),
    )
    out_specs = P("seq", "head", None)
    return jax.shard_map(
        functools.partial(per_device, mesh.shape["seq"]),
        mesh=mesh, in_specs=in_specs, out_specs=out_specs, check_vma=False,
    )
```

```python
import functools
import math

import jax
import jax.numpy as jnp
from jax import lax
from jax.experimental import pallas as pl
from jax.experimental.pallas import tpu as pltpu
from jax.sharding import PartitionSpec as P

KV_HEADS = 8
BLOCK = 128
INNER = 2
ROW_TILE = 256
HIDDEN = -1e30
PENALTY = 1e30
SAFE_TOTAL = 1e30


class Shape:
    def __init__(self, heads, blocks_here, block_total, group, head_dim):
        self.heads = heads
        self.blocks_here = blocks_here
        self.block_total = block_total
        self.group = group
        self.head_dim = head_dim
        self.rows_unit = BLOCK * group
        self.rows = blocks_here * self.rows_unit
        self.factor = head_dim ** -0.5 * math.log2(math.e)


def owner_of(seq_pos, crossed, away):
    line = seq_pos // INNER - away
    place = seq_pos % INNER
    return line * INNER + (1 - place if crossed else place)


def scores(q, keys):
    return lax.dot_general(q, keys, (((1,), (1,)), ((), ())), preferred_element_type=jnp.float32)


def with_ones(vals):
    return jnp.concatenate([vals, jnp.ones_like(vals)], axis=1)


def tiles_of(shape):
    return [(b, r * ROW_TILE) for b in range(shape.blocks_here)
            for r in range(shape.rows_unit // ROW_TILE)]


def mark_allowed(
    shape, pos_ref, retr_ref, vert_ref, slash_ref, sink_ref, window_ref, allowed_ref
):
    first_block = pos_ref[0] * shape.blocks_here
    first_head = pos_ref[1] * shape.heads
    n_retr = retr_ref.shape[0]
    for h in range(shape.heads):
        head_id = first_head + h
        is_retr = functools.reduce(
            jnp.logical_or, [retr_ref[i] == head_id for i in range(n_retr)]
        )
        for b in range(shape.blocks_here):
            query_block = first_block + b
            sinks = jnp.where(is_retr, 0, sink_ref[head_id])
            lowest = query_block - jnp.where(is_retr, 1, window_ref[head_id])

            def clear(c, carry):
                read = ((c < sinks) | (c > lowest)) & (c <= query_block)
                allowed_ref[h, b, c] = read.astype(jnp.int32)
                return carry

            lax.fori_loop(0, shape.block_total, clear, 0)
            for j in range(vert_ref.shape[2]):
                c = vert_ref[b, head_id, j]
                allowed_ref[h, b, jnp.where(is_retr, c, query_block)] = 1
            for j in range(slash_ref.shape[2]):
                c = query_block - slash_ref[b, head_id, j]
                allowed_ref[h, b, jnp.where(is_retr, c, query_block)] = 1


def first_kernel(shape, pos_ref, *refs):
    list_refs, q_raw_ref, own_refs = refs[:5], refs[5], refs[6:6 + shape.heads]
    allowed_ref, q_ref, peak_ref, acc_ref, wide, *lists, sems = refs[6 + shape.heads:]
    first_block = pos_ref[0] * shape.blocks_here
    copies = [pltpu.make_async_copy(list_refs[i], lists[i], sems.at[i]) for i in range(5)]
    for copy in copies:
        copy.start()
    wide[...] = q_raw_ref[...].astype(jnp.float32)
    for h in range(shape.heads):
        q_ref[h] = wide[pl.ds(h, shape.rows, stride=shape.heads), :].astype(q_ref.dtype)
    for copy in copies:
        copy.wait()
    mark_allowed(shape, pos_ref, *lists, allowed_ref)
    for h in range(shape.heads):
        for b, start in tiles_of(shape):
            rows = pl.ds(b * shape.rows_unit + start, ROW_TILE)
            width = (b + 1) * BLOCK
            s = scores(q_ref[h, rows, :], own_refs[h][0, :width, :]) * shape.factor
            columns = []
            for j in range(b):
                seen = allowed_ref[h, b, first_block + j] > 0
                columns.append(s[:, j * BLOCK:(j + 1) * BLOCK] - jnp.where(seen, 0.0, PENALTY))
            diagonal = s[:, b * BLOCK:]
            row = start + lax.broadcasted_iota(jnp.int32, diagonal.shape, 0)
            column = lax.broadcasted_iota(jnp.int32, diagonal.shape, 1)
            columns.append(jnp.where(column * shape.group <= row, diagonal, HIDDEN))
            s = jnp.concatenate(columns, axis=1)
            m = jnp.max(s, axis=1, keepdims=True)
            peak_ref[h, rows, :] = jnp.broadcast_to(m, (ROW_TILE, BLOCK))
            p = jnp.exp2(s - m).astype(jnp.bfloat16)
            vals = with_ones(own_refs[h][1, :width, :])
            acc_ref[h, rows, :] = jnp.dot(p, vals, preferred_element_type=jnp.float32)


def seen_flags(shape, slots, h, seq_pos, allowed_ref):
    flags = []
    for b in range(shape.blocks_here):
        row = []
        for crossed, away in slots:
            owner = owner_of(seq_pos, crossed, away)
            there = (owner >= 0) & (owner < seq_pos)
            base = jnp.where(there, owner, 0) * shape.blocks_here
            for j in range(shape.blocks_here):
                row.append(there & (allowed_ref[h, b, base + j] > 0))
        flags.append(row)
    return flags


def mixed_tiles(shape, h, flags, q_ref, peak_ref, piece_refs):
    keys = jnp.concatenate([ref[0] for ref in piece_refs], axis=0)
    vals = with_ones(jnp.concatenate([ref[1] for ref in piece_refs], axis=0))
    for b, start in tiles_of(shape):
        rows = pl.ds(b * shape.rows_unit + start, ROW_TILE)
        s = scores(q_ref[h, rows, :], keys) * shape.factor
        m = peak_ref[h, rows, :]
        shift = jnp.concatenate([m + jnp.where(f, 0.0, PENALTY) for f in flags[b]], axis=1)
        p = jnp.exp2(s - shift).astype(jnp.bfloat16)
        yield rows, jnp.dot(p, vals, preferred_element_type=jnp.float32)


def middle_kernel(shape, slots, pos_ref, allowed_ref, q_ref, peak_ref, acc_in, *refs):
    del acc_in
    n = len(slots)
    acc_ref = refs[-1]
    for h in range(shape.heads):
        flags = seen_flags(shape, slots, h, pos_ref[0], allowed_ref)

        @pl.when(functools.reduce(jnp.logical_or, [f for row in flags for f in row]))
        def _():
            for rows, mixed in mixed_tiles(
                shape, h, flags, q_ref, peak_ref, refs[h * n:(h + 1) * n]
            ):
                acc_ref[h, rows, :] += mixed


def last_kernel(
    shape, slots, all_slots, pos_ref, allowed_ref, q_ref, peak_ref, acc_ref, *refs
):
    n, n_all, heads = len(slots), len(all_slots), shape.heads
    piece_refs, all_refs = refs[:n * heads], refs[n * heads:(n + n_all) * heads]
    out_ref, out_rows, kv, owner_list, sems = refs[(n + n_all) * heads:]
    seq_pos = pos_ref[0]
    first_block = seq_pos * shape.blocks_here
    head_dim = shape.head_dim

    def finish(h, rows, sums):
        total = sums[:, head_dim:]
        out_rows[pl.ds(rows.start * heads + h, ROW_TILE, stride=heads), :] = (
            sums[:, :head_dim] / total
        )
        bad = jnp.where(total < SAFE_TOTAL, 0.0, 1.0)
        return jnp.max(bad.reshape(ROW_TILE // 8, 8, head_dim), axis=0)

    worst = jnp.zeros((8, head_dim), jnp.float32)
    for h in range(heads):
        flags = seen_flags(shape, slots, h, seq_pos, allowed_ref)
        for rows, mixed in mixed_tiles(
            shape, h, flags, q_ref, peak_ref, piece_refs[h * n:(h + 1) * n]
        ):
            worst = jnp.maximum(worst, finish(h, rows, acc_ref[h, rows, :] + mixed))
    out_ref[...] = out_rows[...].astype(out_ref.dtype)

    @pl.when(jnp.max(worst) > 0.0)
    def _():
        copies = [
            pltpu.make_async_copy(all_refs[h * n_all + i], kv.at[i, h], sems.at[i, h])
            for h in range(heads) for i in range(n_all)
        ]
        for copy in copies:
            copy.start()
        for i, (crossed, away) in enumerate(all_slots):
            owner_list[i] = owner_of(seq_pos, crossed, away)
        for copy in copies:
            copy.wait()

        def every_tile(step):
            def slot_step(i, carry):
                owner = owner_list[i]

                @pl.when((owner >= 0) & (owner <= seq_pos))
                def _():
                    for h in range(heads):
                        for b, start in tiles_of(shape):
                            rows = pl.ds(b * shape.rows_unit + start, ROW_TILE)
                            s = scores(q_ref[h, rows, :], kv[i, h, 0]) * shape.factor
                            columns = []
                            for j in range(shape.blocks_here):
                                block = owner * shape.blocks_here + j
                                part = s[:, j * BLOCK:(j + 1) * BLOCK]
                                row = start + lax.broadcasted_iota(jnp.int32, part.shape, 0)
                                column = lax.broadcasted_iota(jnp.int32, part.shape, 1)
                                ahead = (first_block + b - block) * BLOCK
                                part = jnp.where(
                                    (column - ahead) * shape.group <= row, part, HIDDEN
                                )
                                seen = allowed_ref[h, b, block] > 0
                                columns.append(part - jnp.where(seen, 0.0, PENALTY))
                            step(h, rows, jnp.concatenate(columns, axis=1), i)

                return carry

            lax.fori_loop(0, n_all, slot_step, 0)

        def widen(h, rows, s, i):
            m = jnp.max(s, axis=1, keepdims=True)
            peak_ref[h, rows, :] = jnp.maximum(peak_ref[h, rows, :], m)

        def collect(h, rows, s, i):
            m = peak_ref[h, rows, :]
            shift = jnp.concatenate([m] * shape.blocks_here, axis=1)
            p = jnp.exp2(s - shift).astype(jnp.bfloat16)
            acc_ref[h, rows, :] += jnp.dot(
                p, with_ones(kv[i, h, 1]), preferred_element_type=jnp.float32
            )

        every_tile(widen)
        acc_ref[...] = jnp.zeros_like(acc_ref)
        every_tile(collect)
        for h in range(heads):
            for b, start in tiles_of(shape):
                rows = pl.ds(b * shape.rows_unit + start, ROW_TILE)
                finish(h, rows, acc_ref[h, rows, :])
        out_ref[...] = out_rows[...].astype(out_ref.dtype)


def last_kernel_in_place(
    shape, slots, all_slots, pos_ref, allowed_ref, q_ref, peak_in, acc_in, *refs
):
    del peak_in, acc_in
    n_in = (len(slots) + len(all_slots)) * shape.heads
    out_ref, peak_ref, acc_ref = refs[n_in:n_in + 3]
    last_kernel(
        shape, slots, all_slots, pos_ref, allowed_ref, q_ref, peak_ref, acc_ref,
        *refs[:n_in], out_ref, *refs[n_in + 3:],
    )


def per_device(
    n_seq, queries, keys, values, retrieval_ids, vertical_blocks, slash_offsets, sink_blocks,
    window_blocks,
):
    tokens_here, heads, width = queries.shape
    head_dim = keys.shape[2]
    group = width // head_dim
    blocks_here = tokens_here // BLOCK
    outer = n_seq // INNER
    shape = Shape(heads, blocks_here, n_seq * blocks_here, group, head_dim)

    own = [jnp.stack([keys[:, h], values[:, h]]) for h in range(heads)]

    q_raw = queries.reshape(tokens_here, heads, group, head_dim)
    q_raw = jnp.transpose(q_raw, (0, 2, 1, 3)).reshape(heads * shape.rows, head_dim)
    pos = jnp.stack([lax.axis_index("seq"), lax.axis_index("head")]).astype(jnp.int32)

    smem = pl.BlockSpec(memory_space=pltpu.SMEM)
    vmem = pl.BlockSpec(memory_space=pltpu.VMEM)
    anywhere = pl.BlockSpec(memory_space=pl.ANY)
    allowed_shape = jax.ShapeDtypeStruct((heads, blocks_here, shape.block_total), jnp.int32)
    q_shape = jax.ShapeDtypeStruct((heads, shape.rows, head_dim), jnp.bfloat16)
    peak_shape = jax.ShapeDtypeStruct((heads, shape.rows, head_dim), jnp.float32)
    acc_shape = jax.ShapeDtypeStruct((heads, shape.rows, 2 * head_dim), jnp.float32)
    params = pltpu.CompilerParams(vmem_limit_bytes=16 << 20)
    cost = pl.CostEstimate(flops=1 << 20, transcendentals=0, bytes_accessed=1 << 10)

    lists = (retrieval_ids, vertical_blocks, slash_offsets, sink_blocks, window_blocks)
    allowed, q, peak, acc = pl.pallas_call(
        functools.partial(first_kernel, shape),
        out_shape=(allowed_shape, q_shape, peak_shape, acc_shape),
        in_specs=[smem] + [anywhere] * 5 + [vmem] * (1 + heads),
        out_specs=(smem, vmem, vmem, vmem),
        scratch_shapes=[pltpu.VMEM((heads * shape.rows, head_dim), jnp.float32)]
        + [pltpu.SMEM(x.shape, jnp.int32) for x in lists]
        + [pltpu.SemaphoreType.DMA((5,))],
        compiler_params=params,
        cost_estimate=cost,
    )(pos, *lists, q_raw, *own)

    column, crossed = [own], []
    for step in range(outer):
        across = [
            (s, s ^ 1) for s in range(n_seq)
            if s // INNER >= step and (step > 0 or s % INNER == 0)
        ]
        along = [(s, s + INNER) for s in range(n_seq - INNER) if s // INNER >= step]
        crossed.append([])
        if step + 1 < outer:
            column.append([])
        for h in range(heads):
            if step + 1 < outer:
                column[step + 1].append(lax.ppermute(column[step][h], "seq", along))
            crossed[step].append(lax.ppermute(column[step][h], "seq", across))
        if step + 1 == outer:
            break
        if step > 0:
            slots = [(False, step), (True, step - 1)]
            pieces = [p for h in range(heads) for p in (column[step][h], crossed[step - 1][h])]
            acc = pl.pallas_call(
                functools.partial(middle_kernel, shape, slots),
                out_shape=acc_shape,
                in_specs=[smem, smem] + [vmem] * (3 + len(pieces)),
                out_specs=vmem,
                input_output_aliases={4: 0},
                compiler_params=params,
                cost_estimate=cost,
            )(pos, allowed, q, peak, acc, *pieces)
        column[step + 1][0], acc = lax.optimization_barrier((column[step + 1][0], acc))

    step = outer - 1
    slots = [(False, step), (True, step - 1)]
    pieces = [p for h in range(heads) for p in (column[step][h], crossed[step - 1][h])]
    acc = pl.pallas_call(
        functools.partial(middle_kernel, shape, slots),
        out_shape=acc_shape,
        in_specs=[smem, smem] + [vmem] * (3 + len(pieces)),
        out_specs=vmem,
        input_output_aliases={4: 0},
        compiler_params=params,
        cost_estimate=cost,
    )(pos, allowed, q, peak, acc, *pieces)

    slots = [(True, outer - 1)]
    all_slots = [(False, a) for a in range(outer)] + [(True, a) for a in range(outer)]
    n_all = len(all_slots)
    everything = [piece[h] for h in range(heads) for piece in column + crossed]
    out, _, _ = pl.pallas_call(
        functools.partial(last_kernel_in_place, shape, slots, all_slots),
        out_shape=(
            jax.ShapeDtypeStruct((heads * shape.rows, head_dim), jnp.bfloat16),
            peak_shape,
            acc_shape,
        ),
        in_specs=[smem, smem] + [vmem] * (3 + heads) + [anywhere] * len(everything),
        out_specs=(vmem, vmem, vmem),
        input_output_aliases={3: 1, 4: 2},
        scratch_shapes=[
            pltpu.VMEM((heads * shape.rows, head_dim), jnp.float32),
            pltpu.VMEM((n_all, heads) + own[0].shape, jnp.bfloat16),
            pltpu.SMEM((n_all,), jnp.int32),
            pltpu.SemaphoreType.DMA((n_all, heads)),
        ],
        compiler_params=pltpu.CompilerParams(
            vmem_limit_bytes=(16 << 20) + 2 * n_all * heads * own[0].size
        ),
        cost_estimate=cost,
    )(pos, allowed, q, peak, acc, *crossed[outer - 1], *everything)
    out = out.reshape(tokens_here, group, heads, head_dim)
    return jnp.transpose(out, (0, 2, 1, 3)).reshape(tokens_here, heads, width)


def solution(mesh):
    in_specs = (
        P("seq", "head", None),
        P("seq", "head", None),
        P("seq", "head", None),
        P(),
        P("seq", None, None),
        P("seq", None, None),
        P(),
        P(),
    )
    out_specs = P("seq", "head", None)
    return jax.shard_map(
        functools.partial(per_device, mesh.shape["seq"]),
        mesh=mesh, in_specs=in_specs, out_specs=out_specs, check_vma=False,
    )
```

```python
import functools
import math

import jax
import jax.numpy as jnp
from jax import lax
from jax.experimental import pallas as pl
from jax.experimental.pallas import tpu as pltpu
from jax.sharding import PartitionSpec as P

KV_HEADS = 8
BLOCK = 128
INNER = 2
ROW_TILE = 256
HIDDEN = -1e30
SAFE_TOTAL = 1e30


class Shape:
    def __init__(self, heads, blocks_here, block_total, group, head_dim, n_slots):
        self.heads = heads
        self.n_slots = n_slots
        self.blocks_here = blocks_here
        self.block_total = block_total
        self.group = group
        self.head_dim = head_dim
        self.rows_unit = BLOCK * group
        self.rows = blocks_here * self.rows_unit
        self.factor = head_dim ** -0.5 * math.log2(math.e)


def owner_of(shape, seq_pos, slot):
    outer = shape.n_slots // INNER
    crossed = slot >= outer
    line = seq_pos // INNER - jnp.where(crossed, slot - outer, slot)
    place = seq_pos % INNER
    return line * INNER + jnp.where(crossed, 1 - place, place)


def scores(q, keys):
    return lax.dot_general(q, keys, (((1,), (1,)), ((), ())), preferred_element_type=jnp.float32)


def with_ones(vals):
    return jnp.concatenate([vals, jnp.ones_like(vals)], axis=1)


def tiles_of(shape):
    return [(b, r * ROW_TILE) for b in range(shape.blocks_here)
            for r in range(shape.rows_unit // ROW_TILE)]


def mark_allowed(
    shape, pos_ref, retr_ref, vert_ref, slash_ref, sink_ref, window_ref, allowed_ref
):
    first_block = pos_ref[0] * shape.blocks_here
    first_head = pos_ref[1] * shape.heads
    n_retr = retr_ref.shape[0]
    for h in range(shape.heads):
        head_id = first_head + h
        is_retr = functools.reduce(
            jnp.logical_or, [retr_ref[i] == head_id for i in range(n_retr)]
        )
        for b in range(shape.blocks_here):
            query_block = first_block + b
            sinks = jnp.where(is_retr, 0, sink_ref[head_id])
            lowest = query_block - jnp.where(is_retr, 1, window_ref[head_id])

            def clear(c, carry):
                read = ((c < sinks) | (c > lowest)) & (c <= query_block)
                allowed_ref[h, b, c] = read.astype(jnp.int32)
                return carry

            lax.fori_loop(0, shape.block_total, clear, 0)
            for j in range(vert_ref.shape[2]):
                c = vert_ref[b, head_id, j]
                allowed_ref[h, b, jnp.where(is_retr, c, query_block)] = 1
            for j in range(slash_ref.shape[2]):
                c = query_block - slash_ref[b, head_id, j]
                allowed_ref[h, b, jnp.where(is_retr, c, query_block)] = 1


def read_lists(list_refs, lists, sems):
    return [pltpu.make_async_copy(list_refs[i], lists[i], sems.at[i]) for i in range(len(lists))]


def first_kernel(shape, n_lists, pos_ref, *refs):
    list_refs, q_raw_ref, own_ref = refs[:n_lists], refs[n_lists], refs[n_lists + 1]
    mask_ref, q_ref, peak_ref, acc_ref, *scratch = refs[n_lists + 2:]
    q_raw, wide, allowed_ref, lists, sems = *scratch[:3], scratch[3:-1], scratch[-1]
    seq_pos = pos_ref[0]
    first_block = seq_pos * shape.blocks_here
    q_copy = pltpu.make_async_copy(q_raw_ref, q_raw, sems.at[n_lists])
    q_copy.start()
    copies = read_lists(list_refs, lists, sems)
    for copy in copies:
        copy.start()
    for copy in copies:
        copy.wait()
    mark_allowed(shape, pos_ref, *lists, allowed_ref)

    def fill_masks(slot, carry):
        owner = owner_of(shape, seq_pos, slot)
        there = (owner >= 0) & (owner < seq_pos)
        base = jnp.where(there, owner, 0) * shape.blocks_here
        for h in range(shape.heads):
            for b in range(shape.blocks_here):
                for j in range(shape.blocks_here):
                    seen = there & (allowed_ref[h, b, base + j] > 0)
                    mask_ref[h, b, pl.ds(slot * shape.blocks_here + j, 1), :] = jnp.full(
                        (1, shape.head_dim), jnp.where(seen, 1.0, 0.0), jnp.float32
                    )
        return carry

    lax.fori_loop(0, shape.n_slots, fill_masks, 0)
    q_copy.wait()
    wide[...] = q_raw[...].astype(jnp.float32)
    for h in range(shape.heads):
        q_ref[h] = wide[pl.ds(h, shape.rows, stride=shape.heads), :].astype(q_ref.dtype)
    for h in range(shape.heads):
        for b, start in tiles_of(shape):
            rows = pl.ds(b * shape.rows_unit + start, ROW_TILE)
            width = (b + 1) * BLOCK
            s = scores(q_ref[h, rows, :], own_ref[h, :width, :]) * shape.factor
            columns = []
            for j in range(b):
                seen = allowed_ref[h, b, first_block + j] > 0
                columns.append(
                    s[:, j * BLOCK:(j + 1) * BLOCK] + jnp.where(seen, 0.0, HIDDEN)
                )
            diagonal = s[:, b * BLOCK:]
            row = start + lax.broadcasted_iota(jnp.int32, diagonal.shape, 0)
            column = lax.broadcasted_iota(jnp.int32, diagonal.shape, 1)
            columns.append(jnp.where(column * shape.group <= row, diagonal, HIDDEN))
            s = jnp.concatenate(columns, axis=1)
            m = jnp.max(s, axis=1, keepdims=True)
            peak_ref[h, rows, :] = jnp.broadcast_to(m, (ROW_TILE, BLOCK))
            p = jnp.exp2(s - m).astype(jnp.bfloat16)
            vals = with_ones(own_ref[shape.heads + h, :width, :])
            acc_ref[h, rows, :] = jnp.dot(p, vals, preferred_element_type=jnp.float32)


def mixed_tiles(shape, slots, h, mask_ref, q_ref, peak_ref, piece_refs):
    keys = jnp.concatenate([ref[h] for ref in piece_refs], axis=0)
    vals = jnp.concatenate([ref[shape.heads + h] for ref in piece_refs], axis=0)
    seen_vals = []
    for b in range(shape.blocks_here):
        masks = jnp.concatenate(
            [
                jnp.broadcast_to(
                    mask_ref[h, b, pl.ds(slot * shape.blocks_here + j, 1), :],
                    (BLOCK, shape.head_dim),
                )
                for slot in slots for j in range(shape.blocks_here)
            ],
            axis=0,
        ).astype(jnp.bfloat16)
        seen_vals.append(jnp.concatenate([vals * masks, masks], axis=1))
    for b, start in tiles_of(shape):
        rows = pl.ds(b * shape.rows_unit + start, ROW_TILE)
        s = scores(q_ref[h, rows, :], keys) * shape.factor
        m = peak_ref[h, rows, :]
        p = jnp.exp2(s - jnp.concatenate([m] * (s.shape[1] // m.shape[1]), axis=1))
        yield rows, jnp.dot(
            p.astype(jnp.bfloat16), seen_vals[b], preferred_element_type=jnp.float32
        )


def middle_kernel(shape, slots, mask_ref, q_ref, peak_ref, acc_in, *refs):
    del acc_in
    piece_refs, acc_ref = refs[:-1], refs[-1]
    for h in range(shape.heads):
        for rows, mixed in mixed_tiles(
            shape, slots, h, mask_ref, q_ref, peak_ref, piece_refs
        ):
            acc_ref[h, rows, :] += mixed


def last_kernel(shape, slots, n_lists, mask_ref, q_ref, peak_in, acc_in, *refs):
    del peak_in, acc_in
    n, n_all, heads, head_dim = len(slots), shape.n_slots, shape.heads, shape.head_dim
    piece_refs, all_refs, list_refs = refs[:n], refs[n:n + n_all], refs[n + n_all:][:n_lists + 1]
    out_ref, peak_ref, acc_ref, *scratch = refs[n + n_all + n_lists + 1:]
    out_rows, kv, allowed_ref, lists, sems = *scratch[:3], scratch[3:-1], scratch[-1]

    def finish(h, rows, sums):
        total = sums[:, head_dim:]
        out_rows[pl.ds(rows.start * heads + h, ROW_TILE, stride=heads), :] = (
            sums[:, :head_dim] / total
        )
        bad = jnp.where(total < SAFE_TOTAL, 0.0, 1.0)
        return jnp.max(bad.reshape(ROW_TILE // 8, 8, head_dim), axis=0)

    worst = jnp.zeros((8, head_dim), jnp.float32)
    for h in range(heads):
        for rows, mixed in mixed_tiles(
            shape, slots, h, mask_ref, q_ref, peak_ref, piece_refs
        ):
            worst = jnp.maximum(worst, finish(h, rows, acc_ref[h, rows, :] + mixed))
    out_ref[...] = out_rows[...].astype(out_ref.dtype)

    @pl.when(jnp.max(worst) > 0.0)
    def _():
        copies = read_lists(list_refs, lists, sems) + [
            pltpu.make_async_copy(all_refs[i], kv.at[i], sems.at[n_lists + 1 + i])
            for i in range(n_all)
        ]
        for copy in copies:
            copy.start()
        for copy in copies:
            copy.wait()
        pos_ref = lists[0]
        seq_pos = pos_ref[0]
        first_block = seq_pos * shape.blocks_here
        mark_allowed(shape, pos_ref, *lists[1:], allowed_ref)

        def every_tile(step):
            def slot_step(i, carry):
                owner = owner_of(shape, seq_pos, i)

                @pl.when((owner >= 0) & (owner <= seq_pos))
                def _():
                    for h in range(heads):
                        for b, start in tiles_of(shape):
                            rows = pl.ds(b * shape.rows_unit + start, ROW_TILE)
                            s = scores(q_ref[h, rows, :], kv[i, h]) * shape.factor
                            columns = []
                            for j in range(shape.blocks_here):
                                block = owner * shape.blocks_here + j
                                part = s[:, j * BLOCK:(j + 1) * BLOCK]
                                row = start + lax.broadcasted_iota(jnp.int32, part.shape, 0)
                                column = lax.broadcasted_iota(jnp.int32, part.shape, 1)
                                ahead = (first_block + b - block) * BLOCK
                                part = jnp.where(
                                    (column - ahead) * shape.group <= row, part, HIDDEN
                                )
                                seen = allowed_ref[h, b, block] > 0
                                columns.append(part + jnp.where(seen, 0.0, HIDDEN))
                            step(h, rows, jnp.concatenate(columns, axis=1), i)

                return carry

            lax.fori_loop(0, n_all, slot_step, 0)

        def widen(h, rows, s, i):
            m = jnp.max(s, axis=1, keepdims=True)
            peak_ref[h, rows, :] = jnp.maximum(peak_ref[h, rows, :], m)

        def collect(h, rows, s, i):
            m = peak_ref[h, rows, :]
            p = jnp.exp2(s - jnp.concatenate([m] * shape.blocks_here, axis=1))
            acc_ref[h, rows, :] += jnp.dot(
                p.astype(jnp.bfloat16), with_ones(kv[i, heads + h]),
                preferred_element_type=jnp.float32,
            )

        every_tile(widen)
        acc_ref[...] = jnp.zeros_like(acc_ref)
        every_tile(collect)
        for h in range(heads):
            for b, start in tiles_of(shape):
                rows = pl.ds(b * shape.rows_unit + start, ROW_TILE)
                finish(h, rows, acc_ref[h, rows, :])
        out_ref[...] = out_rows[...].astype(out_ref.dtype)


def per_device(
    n_seq, queries, keys, values, retrieval_ids, vertical_blocks, slash_offsets, sink_blocks,
    window_blocks,
):
    tokens_here, heads, width = queries.shape
    head_dim = keys.shape[2]
    group = width // head_dim
    blocks_here = tokens_here // BLOCK
    outer = n_seq // INNER
    shape = Shape(heads, blocks_here, n_seq * blocks_here, group, head_dim, n_seq)

    own = jnp.concatenate(
        [jnp.transpose(keys, (1, 0, 2)), jnp.transpose(values, (1, 0, 2))], axis=0
    )
    q_raw = queries.reshape(tokens_here, heads, group, head_dim)
    q_raw = jnp.transpose(q_raw, (0, 2, 1, 3)).reshape(heads * shape.rows, head_dim)
    pos = jnp.stack([lax.axis_index("seq"), lax.axis_index("head")]).astype(jnp.int32)

    smem = pl.BlockSpec(memory_space=pltpu.SMEM)
    vmem = pl.BlockSpec(memory_space=pltpu.VMEM)
    hbm = pl.BlockSpec(memory_space=pltpu.HBM)
    anywhere = pl.BlockSpec(memory_space=pl.ANY)
    mask_shape = jax.ShapeDtypeStruct(
        (heads, blocks_here, shape.block_total, head_dim), jnp.float32
    )
    q_shape = jax.ShapeDtypeStruct((heads, shape.rows, head_dim), jnp.bfloat16)
    peak_shape = jax.ShapeDtypeStruct((heads, shape.rows, head_dim), jnp.float32)
    acc_shape = jax.ShapeDtypeStruct((heads, shape.rows, 2 * head_dim), jnp.float32)
    allowed_scratch = pltpu.SMEM((heads, blocks_here, shape.block_total), jnp.int32)
    params = pltpu.CompilerParams(vmem_limit_bytes=16 << 20)
    cost = pl.CostEstimate(flops=1 << 20, transcendentals=0, bytes_accessed=1 << 10)

    lists = tuple(
        pltpu.with_memory_space_constraint(x, pltpu.HBM)
        for x in (retrieval_ids, vertical_blocks, slash_offsets, sink_blocks, window_blocks)
    )
    q_raw = pltpu.with_memory_space_constraint(q_raw, pltpu.HBM)
    n_lists = len(lists)
    list_scratch = [pltpu.SMEM(x.shape, jnp.int32) for x in lists]
    mask, q, peak, acc = pl.pallas_call(
        functools.partial(first_kernel, shape, n_lists),
        out_shape=(mask_shape, q_shape, peak_shape, acc_shape),
        in_specs=[smem] + [hbm] * (n_lists + 1) + [vmem],
        out_specs=(vmem, vmem, vmem, vmem),
        scratch_shapes=[
            pltpu.VMEM((heads * shape.rows, head_dim), jnp.bfloat16),
            pltpu.VMEM((heads * shape.rows, head_dim), jnp.float32),
            allowed_scratch,
            *list_scratch,
            pltpu.SemaphoreType.DMA((n_lists + 1,)),
        ],
        compiler_params=params,
        cost_estimate=cost,
    )(pos, *lists, q_raw, own)

    def add(acc, step):
        slots = [step, outer + step - 1]
        return pl.pallas_call(
            functools.partial(middle_kernel, shape, slots),
            out_shape=acc_shape,
            in_specs=[vmem] * 6,
            out_specs=vmem,
            input_output_aliases={3: 0},
            compiler_params=params,
            cost_estimate=cost,
        )(mask, q, peak, acc, column[step], crossed[step - 1])

    column, crossed = [own], []
    for step in range(outer):
        across = [
            (s, s ^ 1) for s in range(n_seq)
            if s // INNER >= step and (step > 0 or s % INNER == 0)
        ]
        along = [(s, s + INNER) for s in range(n_seq - INNER) if s // INNER >= step]
        if along:
            column.append(lax.ppermute(column[step], "seq", along))
        crossed.append(lax.ppermute(column[step], "seq", across))
        if step > 0:
            acc = add(acc, step)
        if along:
            column[step + 1], acc = lax.optimization_barrier((column[step + 1], acc))

    out, _, _ = pl.pallas_call(
        functools.partial(last_kernel, shape, [n_seq - 1], n_lists),
        out_shape=(
            jax.ShapeDtypeStruct((heads * shape.rows, head_dim), jnp.bfloat16),
            peak_shape,
            acc_shape,
        ),
        in_specs=[vmem] * 5 + [anywhere] * n_seq + [anywhere] + [hbm] * n_lists,
        out_specs=(vmem, vmem, vmem),
        input_output_aliases={2: 1, 3: 2},
        scratch_shapes=[
            pltpu.VMEM((heads * shape.rows, head_dim), jnp.float32),
            pltpu.VMEM((n_seq,) + own.shape, jnp.bfloat16),
            allowed_scratch,
            pltpu.SMEM(pos.shape, jnp.int32),
            *list_scratch,
            pltpu.SemaphoreType.DMA((n_lists + 1 + n_seq,)),
        ],
        compiler_params=pltpu.CompilerParams(
            vmem_limit_bytes=(16 << 20) + 2 * n_seq * own.size
        ),
        cost_estimate=cost,
    )(mask, q, peak, acc, crossed[outer - 1], *column, *crossed, pos, *lists)
    out = out.reshape(tokens_here, group, heads, head_dim)
    return jnp.transpose(out, (0, 2, 1, 3)).reshape(tokens_here, heads, width)


def solution(mesh):
    in_specs = (
        P("seq", "head", None),
        P("seq", "head", None),
        P("seq", "head", None),
        P(),
        P("seq", None, None),
        P("seq", None, None),
        P(),
        P(),
    )
    out_specs = P("seq", "head", None)
    return jax.shard_map(
        functools.partial(per_device, mesh.shape["seq"]),
        mesh=mesh, in_specs=in_specs, out_specs=out_specs, check_vma=False,
    )
```

```python
import functools
import math

import jax
import jax.numpy as jnp
from jax import lax
from jax.experimental import pallas as pl
from jax.experimental.pallas import tpu as pltpu
from jax.sharding import PartitionSpec as P

KV_HEADS = 8
BLOCK = 128
INNER = 2
ROW_TILE = 256
PIECES_AT_ONCE = 2
HIDDEN = -1e30
SAFE_TOTAL = 1e30


class Shape:
    def __init__(self, heads, blocks_here, block_total, group, head_dim, n_slots):
        self.heads = heads
        self.blocks_here = blocks_here
        self.block_total = block_total
        self.group = group
        self.head_dim = head_dim
        self.n_slots = n_slots
        self.outer = n_slots // INNER
        self.rows_unit = BLOCK * group
        self.rows = blocks_here * self.rows_unit
        self.factor = head_dim ** -0.5 * math.log2(math.e)

    def away(self, slot):
        return slot % self.outer


def owner_of(shape, seq_pos, slot):
    crossed = slot >= shape.outer
    line = seq_pos // INNER - jnp.where(crossed, slot - shape.outer, slot)
    place = seq_pos % INNER
    return line * INNER + jnp.where(crossed, 1 - place, place)


def scores(q, keys):
    return lax.dot_general(q, keys, (((1,), (1,)), ((), ())), preferred_element_type=jnp.float32)


def with_ones(vals):
    return jnp.concatenate([vals, jnp.ones_like(vals)], axis=1)


def tiles_of(shape):
    return [(b, r * ROW_TILE) for b in range(shape.blocks_here)
            for r in range(shape.rows_unit // ROW_TILE)]


def mark_allowed(shape, retr_ref, vert_ref, slash_ref, sink_ref, window_ref, allowed_ref):
    first_block = lax.axis_index("seq") * shape.blocks_here
    first_head = lax.axis_index("head") * shape.heads
    n_retr = retr_ref.shape[0]
    for h in range(shape.heads):
        head_id = first_head + h
        is_retr = functools.reduce(
            jnp.logical_or, [retr_ref[i] == head_id for i in range(n_retr)]
        )
        for b in range(shape.blocks_here):
            query_block = first_block + b
            sinks = jnp.where(is_retr, 0, sink_ref[head_id])
            lowest = query_block - jnp.where(is_retr, 1, window_ref[head_id])

            def clear(c, carry):
                read = ((c < sinks) | (c > lowest)) & (c <= query_block)
                allowed_ref[h, b, c] = read.astype(jnp.int32)
                return carry

            lax.fori_loop(0, shape.block_total, clear, 0)
            for j in range(vert_ref.shape[2]):
                c = vert_ref[b, head_id, j]
                allowed_ref[h, b, jnp.where(is_retr, c, query_block)] = 1
            for j in range(slash_ref.shape[2]):
                c = query_block - slash_ref[b, head_id, j]
                allowed_ref[h, b, jnp.where(is_retr, c, query_block)] = 1


def read_lists(list_refs, lists, sems):
    return [pltpu.make_async_copy(list_refs[i], lists[i], sems.at[i]) for i in range(len(lists))]


def prepare_kernel(shape, n_lists, *refs):
    list_refs, q_raw_ref, mask_ref, q_ref = refs[:n_lists], *refs[n_lists:n_lists + 3]
    q_raw, wide, allowed_ref, *lists, sems = refs[n_lists + 3:]
    seq_pos = lax.axis_index("seq")
    copies = read_lists(list_refs, lists, sems)
    for copy in copies:
        copy.start()
    q_copy = pltpu.make_async_copy(q_raw_ref, q_raw, sems.at[n_lists])
    q_copy.start()
    for copy in copies:
        copy.wait()
    mark_allowed(shape, *lists, allowed_ref)

    def fill_masks(slot, carry):
        owner = owner_of(shape, seq_pos, slot)
        there = (owner >= 0) & (owner <= seq_pos)
        base = jnp.where(there, owner, 0) * shape.blocks_here
        for h in range(shape.heads):
            for b in range(shape.blocks_here):
                for j in range(shape.blocks_here):
                    seen = there & (allowed_ref[h, b, base + j] > 0)
                    mask_ref[h, b, pl.ds(slot * shape.blocks_here + j, 1), :] = jnp.full(
                        (1, shape.head_dim), jnp.where(seen, 1.0, 0.0), jnp.float32
                    )
        return carry

    lax.fori_loop(0, shape.n_slots, fill_masks, 0)
    q_copy.wait()
    wide[...] = q_raw[...].astype(jnp.float32)
    for h in range(shape.heads):
        q_ref[h] = wide[pl.ds(h, shape.rows, stride=shape.heads), :].astype(q_ref.dtype)


def own_kernel(shape, mask_ref, q_ref, own_ref, peak_ref, acc_ref):
    for h in range(shape.heads):
        for b, start in tiles_of(shape):
            rows = pl.ds(b * shape.rows_unit + start, ROW_TILE)
            width = (b + 1) * BLOCK
            s = scores(q_ref[h, rows, :], own_ref[h, :width, :]) * shape.factor
            columns = []
            for j in range(b):
                seen = mask_ref[h, b, pl.ds(j, 1), :]
                columns.append(jnp.where(seen > 0.0, s[:, j * BLOCK:(j + 1) * BLOCK], HIDDEN))
            diagonal = s[:, b * BLOCK:]
            row = start + lax.broadcasted_iota(jnp.int32, diagonal.shape, 0)
            column = lax.broadcasted_iota(jnp.int32, diagonal.shape, 1)
            columns.append(jnp.where(column * shape.group <= row, diagonal, HIDDEN))
            s = jnp.concatenate(columns, axis=1)
            m = jnp.max(s, axis=1, keepdims=True)
            peak_ref[h, rows, :] = jnp.broadcast_to(m, (ROW_TILE, BLOCK))
            p = jnp.exp2(s - m).astype(jnp.bfloat16)
            vals = with_ones(own_ref[shape.heads + h, :width, :])
            acc_ref[h, rows, :] = jnp.dot(p, vals, preferred_element_type=jnp.float32)


def mixed_tiles(shape, slots, h, mask_ref, q_ref, peak_ref, piece_refs):
    parts = []
    for at in range(0, len(slots), PIECES_AT_ONCE):
        some_slots = slots[at:at + PIECES_AT_ONCE]
        some_refs = piece_refs[at:at + PIECES_AT_ONCE]
        vals = jnp.concatenate([ref[shape.heads + h] for ref in some_refs], axis=0)
        seen_vals = []
        for b in range(shape.blocks_here):
            masks = jnp.concatenate(
                [
                    jnp.broadcast_to(
                        mask_ref[h, b, pl.ds(slot * shape.blocks_here + j, 1), :],
                        (BLOCK, shape.head_dim),
                    )
                    for slot in some_slots for j in range(shape.blocks_here)
                ],
                axis=0,
            ).astype(jnp.bfloat16)
            seen_vals.append(jnp.concatenate([vals * masks, masks], axis=1))
        parts.append((jnp.concatenate([ref[h] for ref in some_refs], axis=0), seen_vals))
    for b, start in tiles_of(shape):
        rows = pl.ds(b * shape.rows_unit + start, ROW_TILE)
        q = q_ref[h, rows, :]
        m = peak_ref[h, rows, :]
        mixed = None
        for keys, seen_vals in parts:
            s = scores(q, keys) * shape.factor
            p = jnp.exp2(s - jnp.concatenate([m] * (s.shape[1] // m.shape[1]), axis=1))
            part = jnp.dot(
                p.astype(jnp.bfloat16), seen_vals[b], preferred_element_type=jnp.float32
            )
            mixed = part if mixed is None else mixed + part
        yield rows, mixed


def middle_kernel(shape, slots, mask_ref, q_ref, peak_ref, acc_in, *refs):
    del acc_in
    piece_refs, acc_ref = refs[:-1], refs[-1]
    nearest = min(shape.away(slot) for slot in slots)

    @pl.when(lax.axis_index("seq") // INNER >= nearest)
    def _():
        for h in range(shape.heads):
            for rows, mixed in mixed_tiles(
                shape, slots, h, mask_ref, q_ref, peak_ref, piece_refs
            ):
                acc_ref[h, rows, :] += mixed


def last_kernel(shape, slots, n_lists, mask_ref, q_ref, peak_in, acc_in, *refs):
    del peak_in, acc_in
    heads, head_dim = shape.heads, shape.head_dim
    n, n_all = len(slots), shape.n_slots
    piece_refs, all_refs, list_refs = refs[:n], refs[n:n + n_all], refs[n + n_all:][:n_lists]
    out_ref, peak_ref, acc_ref, *scratch = refs[n + n_all + n_lists:]
    out_rows, worst, kv, allowed_ref, *lists, sems = scratch
    seq_pos = lax.axis_index("seq")
    first_block = seq_pos * shape.blocks_here
    line = seq_pos // INNER

    def finish(h, rows, sums):
        total = sums[:, head_dim:]
        out_rows[pl.ds(rows.start * heads + h, ROW_TILE, stride=heads), :] = (
            sums[:, :head_dim] / total
        )
        bad = jnp.where(total < SAFE_TOTAL, 0.0, 1.0)
        worst[...] = jnp.maximum(
            worst[...], jnp.max(bad.reshape(ROW_TILE // 8, 8, head_dim), axis=0)
        )

    def finish_all():
        for h in range(heads):
            for b, start in tiles_of(shape):
                rows = pl.ds(b * shape.rows_unit + start, ROW_TILE)
                finish(h, rows, acc_ref[h, rows, :])

    worst[...] = jnp.zeros_like(worst)
    steps = sorted({shape.away(slot) for slot in slots}) + [shape.outer]
    for least, below in zip([0] + steps, steps):
        here = [i for i, slot in enumerate(slots) if shape.away(slot) <= least]

        @pl.when((line >= least) & (line < below))
        def _(here=here):
            if not here:
                finish_all()
                return
            for h in range(heads):
                for rows, mixed in mixed_tiles(
                    shape, [slots[i] for i in here], h, mask_ref, q_ref, peak_ref,
                    [piece_refs[i] for i in here],
                ):
                    finish(h, rows, acc_ref[h, rows, :] + mixed)

    out_ref[...] = out_rows[...].astype(out_ref.dtype)

    @pl.when(jnp.max(worst[...]) > 0.0)
    def _():
        copies = read_lists(list_refs, lists, sems) + [
            pltpu.make_async_copy(all_refs[i], kv.at[i], sems.at[n_lists + i])
            for i in range(n_all)
        ]
        for copy in copies:
            copy.start()
        for copy in copies:
            copy.wait()
        mark_allowed(shape, *lists, allowed_ref)

        def every_tile(step):
            def slot_step(i, carry):
                owner = owner_of(shape, seq_pos, i)

                @pl.when((owner >= 0) & (owner <= seq_pos))
                def _():
                    for h in range(heads):
                        for b, start in tiles_of(shape):
                            rows = pl.ds(b * shape.rows_unit + start, ROW_TILE)
                            s = scores(q_ref[h, rows, :], kv[i, h]) * shape.factor
                            columns = []
                            for j in range(shape.blocks_here):
                                block = owner * shape.blocks_here + j
                                part = s[:, j * BLOCK:(j + 1) * BLOCK]
                                row = start + lax.broadcasted_iota(jnp.int32, part.shape, 0)
                                column = lax.broadcasted_iota(jnp.int32, part.shape, 1)
                                ahead = (first_block + b - block) * BLOCK
                                part = jnp.where(
                                    (column - ahead) * shape.group <= row, part, HIDDEN
                                )
                                seen = allowed_ref[h, b, block] > 0
                                columns.append(part + jnp.where(seen, 0.0, HIDDEN))
                            step(h, rows, jnp.concatenate(columns, axis=1), i)

                return carry

            lax.fori_loop(0, n_all, slot_step, 0)

        def widen(h, rows, s, i):
            m = jnp.max(s, axis=1, keepdims=True)
            peak_ref[h, rows, :] = jnp.maximum(peak_ref[h, rows, :], m)

        def collect(h, rows, s, i):
            m = peak_ref[h, rows, :]
            p = jnp.exp2(s - jnp.concatenate([m] * shape.blocks_here, axis=1))
            acc_ref[h, rows, :] += jnp.dot(
                p.astype(jnp.bfloat16), with_ones(kv[i, heads + h]),
                preferred_element_type=jnp.float32,
            )

        every_tile(widen)
        acc_ref[...] = jnp.zeros_like(acc_ref)
        every_tile(collect)
        finish_all()
        out_ref[...] = out_rows[...].astype(out_ref.dtype)


def per_device(
    n_seq, queries, keys, values, retrieval_ids, vertical_blocks, slash_offsets, sink_blocks,
    window_blocks,
):
    tokens_here, heads, width = queries.shape
    head_dim = keys.shape[2]
    group = width // head_dim
    blocks_here = tokens_here // BLOCK
    shape = Shape(heads, blocks_here, n_seq * blocks_here, group, head_dim, n_seq)
    outer = shape.outer

    vmem = pl.BlockSpec(memory_space=pltpu.VMEM)
    hbm = pl.BlockSpec(memory_space=pltpu.HBM)
    anywhere = pl.BlockSpec(memory_space=pl.ANY)
    mask_shape = jax.ShapeDtypeStruct(
        (heads, blocks_here, shape.block_total, head_dim), jnp.float32
    )
    q_shape = jax.ShapeDtypeStruct((heads, shape.rows, head_dim), jnp.bfloat16)
    peak_shape = jax.ShapeDtypeStruct((heads, shape.rows, head_dim), jnp.float32)
    acc_shape = jax.ShapeDtypeStruct((heads, shape.rows, 2 * head_dim), jnp.float32)
    allowed_scratch = pltpu.SMEM((heads, blocks_here, shape.block_total), jnp.int32)
    params = pltpu.CompilerParams(vmem_limit_bytes=16 << 20)
    cost = pl.CostEstimate(flops=1 << 20, transcendentals=0, bytes_accessed=1 << 10)

    own = jnp.concatenate(
        [jnp.transpose(keys, (1, 0, 2)), jnp.transpose(values, (1, 0, 2))], axis=0
    )
    q_raw = queries.reshape(tokens_here, heads, group, head_dim)
    q_raw = jnp.transpose(q_raw, (0, 2, 1, 3)).reshape(heads * shape.rows, head_dim)
    q_raw = pltpu.with_memory_space_constraint(q_raw, pltpu.HBM)
    lists = tuple(
        pltpu.with_memory_space_constraint(x, pltpu.HBM)
        for x in (retrieval_ids, vertical_blocks, slash_offsets, sink_blocks, window_blocks)
    )
    n_lists = len(lists)
    list_scratch = [pltpu.SMEM(x.shape, jnp.int32) for x in lists]

    def prepare():
        return pl.pallas_call(
            functools.partial(prepare_kernel, shape, n_lists),
            out_shape=(mask_shape, q_shape),
            in_specs=[hbm] * (n_lists + 1),
            out_specs=(vmem, vmem),
            scratch_shapes=[
                pltpu.VMEM((heads * shape.rows, head_dim), jnp.bfloat16),
                pltpu.VMEM((heads * shape.rows, head_dim), jnp.float32),
                allowed_scratch,
                *list_scratch,
                pltpu.SemaphoreType.DMA((n_lists + 1,)),
            ],
            compiler_params=params,
            cost_estimate=cost,
        )(*lists, q_raw)

    def start_sums():
        return pl.pallas_call(
            functools.partial(own_kernel, shape),
            out_shape=(peak_shape, acc_shape),
            in_specs=[vmem] * 3,
            out_specs=(vmem, vmem),
            compiler_params=params,
            cost_estimate=cost,
        )(mask, q, own)

    def add(acc, slots):
        return pl.pallas_call(
            functools.partial(middle_kernel, shape, slots),
            out_shape=acc_shape,
            in_specs=[vmem] * (4 + len(slots)),
            out_specs=vmem,
            input_output_aliases={3: 0},
            compiler_params=params,
            cost_estimate=cost,
        )(mask, q, peak, acc, *[piece[slot] for slot in slots])

    def send(x, pairs):
        return lax.ppermute(x, "seq", pairs)

    def along(x, least, step=1, most=outer):
        return send(x, [
            (s, s + step * INNER) for s in range(n_seq)
            if least <= s // INNER < min(most, outer - step)
        ])

    def across(x, least):
        return send(x, [
            (s, s ^ 1) for s in range(n_seq)
            if s // INNER >= least and (least > 0 or s % INNER == 0)
        ])

    piece = {0: own}
    if outer == 4:
        piece[1] = along(own, 0)
        piece[4] = send(own, [(s, s ^ 1) for s in range(n_seq) if s % INNER == 0 or s == 1])
        far = along(own, 0, step=2, most=1)
        mask, q = prepare()
        piece[1], q = lax.optimization_barrier((piece[1], q))
        second = along(piece[1], 2)
        piece[5] = across(piece[1], 1)
        piece[3] = along(far, 2)
        piece[7] = along(piece[4], 0, step=3, most=1)
        peak, acc = start_sums()
        second, acc = lax.optimization_barrier((second, acc))
        piece[2] = far + second
        piece[6] = across(piece[2], 2)
        acc = add(acc, [1, 4, 5, 2])
        last_slots = [6, 3, 7]
    else:
        mask, q = prepare()
        peak, acc = start_sums()
        for step in range(outer):
            if step + 1 < outer:
                piece[step + 1] = along(piece[step], step)
            piece[outer + step] = across(piece[step], step)
            if step > 0:
                acc = add(acc, [step, outer + step - 1])
            if step + 1 < outer:
                piece[step + 1], acc = lax.optimization_barrier((piece[step + 1], acc))
        last_slots = [n_seq - 1]

    out, _, _ = pl.pallas_call(
        functools.partial(last_kernel, shape, last_slots, n_lists),
        out_shape=(
            jax.ShapeDtypeStruct((heads * shape.rows, head_dim), jnp.bfloat16),
            peak_shape,
            acc_shape,
        ),
        in_specs=[vmem] * (4 + len(last_slots)) + [anywhere] * n_seq + [hbm] * n_lists,
        out_specs=(vmem, vmem, vmem),
        input_output_aliases={2: 1, 3: 2},
        scratch_shapes=[
            pltpu.VMEM((heads * shape.rows, head_dim), jnp.float32),
            pltpu.VMEM((8, head_dim), jnp.float32),
            pltpu.VMEM((n_seq,) + own.shape, jnp.bfloat16),
            allowed_scratch,
            *list_scratch,
            pltpu.SemaphoreType.DMA((n_lists + n_seq,)),
        ],
        compiler_params=pltpu.CompilerParams(
            vmem_limit_bytes=(16 << 20) + 2 * n_seq * own.size
        ),
        cost_estimate=cost,
    )(
        mask, q, peak, acc, *[piece[slot] for slot in last_slots],
        *[piece[slot] for slot in range(n_seq)], *lists,
    )
    out = out.reshape(tokens_here, group, heads, head_dim)
    return jnp.transpose(out, (0, 2, 1, 3)).reshape(tokens_here, heads, width)


def solution(mesh):
    in_specs = (
        P("seq", "head", None),
        P("seq", "head", None),
        P("seq", "head", None),
        P(),
        P("seq", None, None),
        P("seq", None, None),
        P(),
        P(),
    )
    out_specs = P("seq", "head", None)
    return jax.shard_map(
        functools.partial(per_device, mesh.shape["seq"]),
        mesh=mesh, in_specs=in_specs, out_specs=out_specs, check_vma=False,
    )
```

```python
import functools
import math

import jax
import jax.numpy as jnp
from jax import lax
from jax.experimental import pallas as pl
from jax.experimental.pallas import tpu as pltpu
from jax.sharding import PartitionSpec as P

KV_HEADS = 8
BLOCK = 128
INNER = 2
ROW_TILE = 256
PIECES_AT_ONCE = 2
HIDDEN = -1e30
SAFE_TOTAL = 1e30


class Shape:
    def __init__(self, heads, blocks_here, block_total, group, head_dim, n_slots):
        self.heads = heads
        self.blocks_here = blocks_here
        self.block_total = block_total
        self.group = group
        self.head_dim = head_dim
        self.n_slots = n_slots
        self.outer = n_slots // INNER
        self.rows_unit = BLOCK * group
        self.rows = blocks_here * self.rows_unit
        self.factor = head_dim ** -0.5 * math.log2(math.e)

    def away(self, slot):
        return slot % self.outer


def owner_of(shape, seq_pos, slot):
    crossed = slot >= shape.outer
    line = seq_pos // INNER - jnp.where(crossed, slot - shape.outer, slot)
    place = seq_pos % INNER
    return line * INNER + jnp.where(crossed, 1 - place, place)


def scores(q, keys):
    return lax.dot_general(q, keys, (((1,), (1,)), ((), ())), preferred_element_type=jnp.float32)


def with_ones(vals):
    return jnp.concatenate([vals, jnp.ones_like(vals)], axis=1)


def tiles_of(shape):
    return [(b, r * ROW_TILE) for b in range(shape.blocks_here)
            for r in range(shape.rows_unit // ROW_TILE)]


def mark_allowed(shape, retr_ref, vert_ref, slash_ref, sink_ref, window_ref, allowed_ref):
    first_block = lax.axis_index("seq") * shape.blocks_here
    first_head = lax.axis_index("head") * shape.heads
    n_retr = retr_ref.shape[0]
    for h in range(shape.heads):
        head_id = first_head + h
        is_retr = functools.reduce(
            jnp.logical_or, [retr_ref[i] == head_id for i in range(n_retr)]
        )
        for b in range(shape.blocks_here):
            query_block = first_block + b
            sinks = jnp.where(is_retr, 0, sink_ref[head_id])
            lowest = query_block - jnp.where(is_retr, 1, window_ref[head_id])

            def clear(c, carry):
                read = ((c < sinks) | (c > lowest)) & (c <= query_block)
                allowed_ref[h, b, c] = read.astype(jnp.int32)
                return carry

            lax.fori_loop(0, shape.block_total, clear, 0)
            for j in range(vert_ref.shape[2]):
                c = vert_ref[b, head_id, j]
                allowed_ref[h, b, jnp.where(is_retr, c, query_block)] = 1
            for j in range(slash_ref.shape[2]):
                c = query_block - slash_ref[b, head_id, j]
                allowed_ref[h, b, jnp.where(is_retr, c, query_block)] = 1


def read_lists(list_refs, lists, sems):
    return [pltpu.make_async_copy(list_refs[i], lists[i], sems.at[i]) for i in range(len(lists))]


def prepare_kernel(shape, n_lists, *refs):
    list_refs, q_raw_ref, mask_ref, q_ref = refs[:n_lists], *refs[n_lists:n_lists + 3]
    q_raw, wide, allowed_ref, *lists, sems = refs[n_lists + 3:]
    seq_pos = lax.axis_index("seq")
    copies = read_lists(list_refs, lists, sems)
    for copy in copies:
        copy.start()
    q_copy = pltpu.make_async_copy(q_raw_ref, q_raw, sems.at[n_lists])
    q_copy.start()
    for copy in copies:
        copy.wait()
    mark_allowed(shape, *lists, allowed_ref)

    def fill_masks(slot, carry):
        owner = owner_of(shape, seq_pos, slot)
        there = (owner >= 0) & (owner <= seq_pos)
        base = jnp.where(there, owner, 0) * shape.blocks_here
        for h in range(shape.heads):
            for b in range(shape.blocks_here):
                for j in range(shape.blocks_here):
                    seen = there & (allowed_ref[h, b, base + j] > 0)
                    mask_ref[h, b, pl.ds(slot * shape.blocks_here + j, 1), :] = jnp.full(
                        (1, shape.head_dim), jnp.where(seen, 1.0, 0.0), jnp.float32
                    )
        return carry

    lax.fori_loop(0, shape.n_slots, fill_masks, 0)
    q_copy.wait()
    wide[...] = q_raw[...].astype(jnp.float32)
    for h in range(shape.heads):
        q_ref[h] = wide[pl.ds(h, shape.rows, stride=shape.heads), :].astype(q_ref.dtype)


def own_kernel(shape, mask_ref, q_ref, own_ref, peak_ref, acc_ref):
    for h in range(shape.heads):
        for b, start in tiles_of(shape):
            rows = pl.ds(b * shape.rows_unit + start, ROW_TILE)
            width = (b + 1) * BLOCK
            s = scores(q_ref[h, rows, :], own_ref[h, :width, :]) * shape.factor
            columns = []
            for j in range(b):
                seen = mask_ref[h, b, pl.ds(j, 1), :]
                columns.append(jnp.where(seen > 0.0, s[:, j * BLOCK:(j + 1) * BLOCK], HIDDEN))
            diagonal = s[:, b * BLOCK:]
            row = start + lax.broadcasted_iota(jnp.int32, diagonal.shape, 0)
            column = lax.broadcasted_iota(jnp.int32, diagonal.shape, 1)
            columns.append(jnp.where(column * shape.group <= row, diagonal, HIDDEN))
            s = jnp.concatenate(columns, axis=1)
            m = jnp.max(s, axis=1, keepdims=True)
            peak_ref[h, rows, :] = jnp.broadcast_to(m, (ROW_TILE, BLOCK))
            p = jnp.exp2(s - m).astype(jnp.bfloat16)
            vals = with_ones(own_ref[shape.heads + h, :width, :])
            acc_ref[h, rows, :] = jnp.dot(p, vals, preferred_element_type=jnp.float32)


def mixed_tiles(shape, slots, h, mask_ref, q_ref, peak_ref, piece_refs):
    parts = []
    for at in range(0, len(slots), PIECES_AT_ONCE):
        some_slots = slots[at:at + PIECES_AT_ONCE]
        some_refs = piece_refs[at:at + PIECES_AT_ONCE]
        vals = jnp.concatenate([ref[shape.heads + h] for ref in some_refs], axis=0)
        seen_vals = []
        for b in range(shape.blocks_here):
            masks = jnp.concatenate(
                [
                    jnp.broadcast_to(
                        mask_ref[h, b, pl.ds(slot * shape.blocks_here + j, 1), :],
                        (BLOCK, shape.head_dim),
                    )
                    for slot in some_slots for j in range(shape.blocks_here)
                ],
                axis=0,
            ).astype(jnp.bfloat16)
            seen_vals.append(jnp.concatenate([vals * masks, masks], axis=1))
        parts.append((jnp.concatenate([ref[h] for ref in some_refs], axis=0), seen_vals))
    for b, start in tiles_of(shape):
        rows = pl.ds(b * shape.rows_unit + start, ROW_TILE)
        q = q_ref[h, rows, :]
        m = peak_ref[h, rows, :]
        mixed = None
        for keys, seen_vals in parts:
            s = scores(q, keys) * shape.factor
            p = jnp.exp2(s - jnp.concatenate([m] * (s.shape[1] // m.shape[1]), axis=1))
            part = jnp.dot(
                p.astype(jnp.bfloat16), seen_vals[b], preferred_element_type=jnp.float32
            )
            mixed = part if mixed is None else mixed + part
        yield rows, mixed


def middle_kernel(shape, slots, mask_ref, q_ref, peak_ref, acc_in, *refs):
    del acc_in
    piece_refs, acc_ref = refs[:-1], refs[-1]
    nearest = min(shape.away(slot) for slot in slots)

    @pl.when(lax.axis_index("seq") // INNER >= nearest)
    def _():
        for h in range(shape.heads):
            for rows, mixed in mixed_tiles(
                shape, slots, h, mask_ref, q_ref, peak_ref, piece_refs
            ):
                acc_ref[h, rows, :] += mixed


def last_kernel(shape, slots, n_lists, mask_ref, q_ref, peak_in, acc_in, *refs):
    del peak_in, acc_in
    heads, head_dim = shape.heads, shape.head_dim
    n, n_all = len(slots), shape.n_slots
    piece_refs, all_refs, list_refs = refs[:n], refs[n:n + n_all], refs[n + n_all:][:n_lists]
    out_ref, peak_ref, acc_ref, *scratch = refs[n + n_all + n_lists:]
    out_rows, worst, kv, allowed_ref, *lists, sems = scratch
    seq_pos = lax.axis_index("seq")
    first_block = seq_pos * shape.blocks_here
    line = seq_pos // INNER

    def finish(h, rows, sums):
        total = sums[:, head_dim:]
        out_rows[pl.ds(rows.start * heads + h, ROW_TILE, stride=heads), :] = (
            sums[:, :head_dim] / total
        )
        bad = jnp.where(total < SAFE_TOTAL, 0.0, 1.0)
        worst[...] = jnp.maximum(
            worst[...], jnp.max(bad.reshape(ROW_TILE // 8, 8, head_dim), axis=0)
        )

    def finish_all():
        for h in range(heads):
            for b, start in tiles_of(shape):
                rows = pl.ds(b * shape.rows_unit + start, ROW_TILE)
                finish(h, rows, acc_ref[h, rows, :])

    worst[...] = jnp.zeros_like(worst)
    steps = sorted({shape.away(slot) for slot in slots}) + [shape.outer]
    for least, below in zip([0] + steps, steps):
        here = [i for i, slot in enumerate(slots) if shape.away(slot) <= least]

        @pl.when((line >= least) & (line < below))
        def _(here=here):
            if not here:
                finish_all()
                return
            for h in range(heads):
                for rows, mixed in mixed_tiles(
                    shape, [slots[i] for i in here], h, mask_ref, q_ref, peak_ref,
                    [piece_refs[i] for i in here],
                ):
                    finish(h, rows, acc_ref[h, rows, :] + mixed)

    out_ref[...] = out_rows[...].astype(out_ref.dtype)

    @pl.when(jnp.max(worst[...]) > 0.0)
    def _():
        copies = read_lists(list_refs, lists, sems) + [
            pltpu.make_async_copy(all_refs[i], kv.at[i], sems.at[n_lists + i])
            for i in range(n_all)
        ]
        for copy in copies:
            copy.start()
        for copy in copies:
            copy.wait()
        mark_allowed(shape, *lists, allowed_ref)

        def every_tile(step):
            def slot_step(i, carry):
                owner = owner_of(shape, seq_pos, i)

                @pl.when((owner >= 0) & (owner <= seq_pos))
                def _():
                    for h in range(heads):
                        for b, start in tiles_of(shape):
                            rows = pl.ds(b * shape.rows_unit + start, ROW_TILE)
                            s = scores(q_ref[h, rows, :], kv[i, h]) * shape.factor
                            columns = []
                            for j in range(shape.blocks_here):
                                block = owner * shape.blocks_here + j
                                part = s[:, j * BLOCK:(j + 1) * BLOCK]
                                row = start + lax.broadcasted_iota(jnp.int32, part.shape, 0)
                                column = lax.broadcasted_iota(jnp.int32, part.shape, 1)
                                ahead = (first_block + b - block) * BLOCK
                                part = jnp.where(
                                    (column - ahead) * shape.group <= row, part, HIDDEN
                                )
                                seen = allowed_ref[h, b, block] > 0
                                columns.append(part + jnp.where(seen, 0.0, HIDDEN))
                            step(h, rows, jnp.concatenate(columns, axis=1), i)

                return carry

            lax.fori_loop(0, n_all, slot_step, 0)

        def widen(h, rows, s, i):
            m = jnp.max(s, axis=1, keepdims=True)
            peak_ref[h, rows, :] = jnp.maximum(peak_ref[h, rows, :], m)

        def collect(h, rows, s, i):
            m = peak_ref[h, rows, :]
            p = jnp.exp2(s - jnp.concatenate([m] * shape.blocks_here, axis=1))
            acc_ref[h, rows, :] += jnp.dot(
                p.astype(jnp.bfloat16), with_ones(kv[i, heads + h]),
                preferred_element_type=jnp.float32,
            )

        every_tile(widen)
        acc_ref[...] = jnp.zeros_like(acc_ref)
        every_tile(collect)
        finish_all()
        out_ref[...] = out_rows[...].astype(out_ref.dtype)


def per_device(
    n_seq, queries, keys, values, retrieval_ids, vertical_blocks, slash_offsets, sink_blocks,
    window_blocks,
):
    tokens_here, heads, width = queries.shape
    head_dim = keys.shape[2]
    group = width // head_dim
    blocks_here = tokens_here // BLOCK
    shape = Shape(heads, blocks_here, n_seq * blocks_here, group, head_dim, n_seq)
    outer = shape.outer

    vmem = pl.BlockSpec(memory_space=pltpu.VMEM)
    hbm = pl.BlockSpec(memory_space=pltpu.HBM)
    anywhere = pl.BlockSpec(memory_space=pl.ANY)
    mask_shape = jax.ShapeDtypeStruct(
        (heads, blocks_here, shape.block_total, head_dim), jnp.float32
    )
    q_shape = jax.ShapeDtypeStruct((heads, shape.rows, head_dim), jnp.bfloat16)
    peak_shape = jax.ShapeDtypeStruct((heads, shape.rows, head_dim), jnp.float32)
    acc_shape = jax.ShapeDtypeStruct((heads, shape.rows, 2 * head_dim), jnp.float32)
    allowed_scratch = pltpu.SMEM((heads, blocks_here, shape.block_total), jnp.int32)
    params = pltpu.CompilerParams(vmem_limit_bytes=16 << 20)
    cost = pl.CostEstimate(flops=1 << 20, transcendentals=0, bytes_accessed=1 << 10)

    own = jnp.concatenate(
        [jnp.transpose(keys, (1, 0, 2)), jnp.transpose(values, (1, 0, 2))], axis=0
    )
    q_raw = queries.reshape(tokens_here, heads, group, head_dim)
    q_raw = jnp.transpose(q_raw, (0, 2, 1, 3)).reshape(heads * shape.rows, head_dim)
    q_raw = pltpu.with_memory_space_constraint(q_raw, pltpu.HBM)
    lists = tuple(
        pltpu.with_memory_space_constraint(x, pltpu.HBM)
        for x in (retrieval_ids, vertical_blocks, slash_offsets, sink_blocks, window_blocks)
    )
    n_lists = len(lists)
    list_scratch = [pltpu.SMEM(x.shape, jnp.int32) for x in lists]

    def prepare():
        return pl.pallas_call(
            functools.partial(prepare_kernel, shape, n_lists),
            out_shape=(mask_shape, q_shape),
            in_specs=[hbm] * (n_lists + 1),
            out_specs=(vmem, vmem),
            scratch_shapes=[
                pltpu.VMEM((heads * shape.rows, head_dim), jnp.bfloat16),
                pltpu.VMEM((heads * shape.rows, head_dim), jnp.float32),
                allowed_scratch,
                *list_scratch,
                pltpu.SemaphoreType.DMA((n_lists + 1,)),
            ],
            compiler_params=params,
            cost_estimate=cost,
        )(*lists, q_raw)

    def start_sums():
        return pl.pallas_call(
            functools.partial(own_kernel, shape),
            out_shape=(peak_shape, acc_shape),
            in_specs=[vmem] * 3,
            out_specs=(vmem, vmem),
            compiler_params=params,
            cost_estimate=cost,
        )(mask, q, own)

    def add(acc, slots):
        return pl.pallas_call(
            functools.partial(middle_kernel, shape, slots),
            out_shape=acc_shape,
            in_specs=[vmem] * (4 + len(slots)),
            out_specs=vmem,
            input_output_aliases={3: 0},
            compiler_params=params,
            cost_estimate=cost,
        )(mask, q, peak, acc, *[piece[slot] for slot in slots])

    def send(x, pairs):
        return lax.ppermute(x, "seq", pairs)

    def along(x, least, step=1, most=outer):
        return send(x, [
            (s, s + step * INNER) for s in range(n_seq)
            if least <= s // INNER < min(most, outer - step)
        ])

    def across(x, least):
        return send(x, [
            (s, s ^ 1) for s in range(n_seq)
            if s // INNER >= least and (least > 0 or s % INNER == 0)
        ])

    piece = {0: own}
    if outer == 4:
        piece[1] = along(own, 0)
        piece[4] = send(own, [(s, s ^ 1) for s in range(n_seq) if s % INNER == 0 or s == 1])
        mask, q = prepare()
        piece[1], q = lax.optimization_barrier((piece[1], q))
        piece[2] = along(piece[1], 1)
        piece[5] = across(piece[1], 1)
        piece[7] = along(piece[4], 0, step=3, most=1)
        q, piece[4] = lax.optimization_barrier((q, piece[4]))
        peak, acc = start_sums()
        piece[2], acc = lax.optimization_barrier((piece[2], acc))
        piece[3] = along(piece[2], 2)
        piece[6] = across(piece[2], 2)
        acc = add(acc, [1, 4, 5, 2])
        last_slots = [6, 3, 7]
    else:
        mask, q = prepare()
        peak, acc = start_sums()
        for step in range(outer):
            if step + 1 < outer:
                piece[step + 1] = along(piece[step], step)
            piece[outer + step] = across(piece[step], step)
            if step > 0:
                acc = add(acc, [step, outer + step - 1])
            if step + 1 < outer:
                piece[step + 1], acc = lax.optimization_barrier((piece[step + 1], acc))
        last_slots = [n_seq - 1]

    out, _, _ = pl.pallas_call(
        functools.partial(last_kernel, shape, last_slots, n_lists),
        out_shape=(
            jax.ShapeDtypeStruct((heads * shape.rows, head_dim), jnp.bfloat16),
            peak_shape,
            acc_shape,
        ),
        in_specs=[vmem] * (4 + len(last_slots)) + [anywhere] * n_seq + [hbm] * n_lists,
        out_specs=(vmem, vmem, vmem),
        input_output_aliases={2: 1, 3: 2},
        scratch_shapes=[
            pltpu.VMEM((heads * shape.rows, head_dim), jnp.float32),
            pltpu.VMEM((8, head_dim), jnp.float32),
            pltpu.VMEM((n_seq,) + own.shape, jnp.bfloat16),
            allowed_scratch,
            *list_scratch,
            pltpu.SemaphoreType.DMA((n_lists + n_seq,)),
        ],
        compiler_params=pltpu.CompilerParams(
            vmem_limit_bytes=(16 << 20) + 2 * n_seq * own.size
        ),
        cost_estimate=cost,
    )(
        mask, q, peak, acc, *[piece[slot] for slot in last_slots],
        *[piece[slot] for slot in range(n_seq)], *lists,
    )
    out = out.reshape(tokens_here, group, heads, head_dim)
    return jnp.transpose(out, (0, 2, 1, 3)).reshape(tokens_here, heads, width)


def solution(mesh):
    in_specs = (
        P("seq", "head", None),
        P("seq", "head", None),
        P("seq", "head", None),
        P(),
        P("seq", None, None),
        P("seq", None, None),
        P(),
        P(),
    )
    out_specs = P("seq", "head", None)
    return jax.shard_map(
        functools.partial(per_device, mesh.shape["seq"]),
        mesh=mesh, in_specs=in_specs, out_specs=out_specs, check_vma=False,
    )
```

```python
import functools
import math

import jax
import jax.numpy as jnp
from jax import lax
from jax.experimental import pallas as pl
from jax.experimental.pallas import tpu as pltpu
from jax.sharding import PartitionSpec as P

KV_HEADS = 8
BLOCK = 128
INNER = 2
ROW_TILE = 256
PIECES_AT_ONCE = 2
HIDDEN = -1e30
SAFE_TOTAL = 1e30


class Shape:
    def __init__(self, heads, blocks_here, block_total, group, head_dim, n_slots):
        self.heads = heads
        self.blocks_here = blocks_here
        self.block_total = block_total
        self.group = group
        self.head_dim = head_dim
        self.n_slots = n_slots
        self.outer = n_slots // INNER
        self.rows_unit = BLOCK * group
        self.rows = blocks_here * self.rows_unit
        self.factor = head_dim ** -0.5 * math.log2(math.e)

    def away(self, slot):
        return slot % self.outer


def owner_of(shape, seq_pos, slot):
    crossed = slot >= shape.outer
    line = seq_pos // INNER - jnp.where(crossed, slot - shape.outer, slot)
    place = seq_pos % INNER
    return line * INNER + jnp.where(crossed, 1 - place, place)


def scores(q, keys):
    return lax.dot_general(q, keys, (((1,), (1,)), ((), ())), preferred_element_type=jnp.float32)


def with_ones(vals):
    return jnp.concatenate([vals, jnp.ones_like(vals)], axis=1)


def tiles_of(shape):
    return [(b, r * ROW_TILE) for b in range(shape.blocks_here)
            for r in range(shape.rows_unit // ROW_TILE)]


def mark_allowed(shape, retr_ref, vert_ref, slash_ref, sink_ref, window_ref, allowed_ref):
    first_block = lax.axis_index("seq") * shape.blocks_here
    first_head = lax.axis_index("head") * shape.heads
    n_retr = retr_ref.shape[0]
    for h in range(shape.heads):
        head_id = first_head + h
        is_retr = functools.reduce(
            jnp.logical_or, [retr_ref[i] == head_id for i in range(n_retr)]
        )
        for b in range(shape.blocks_here):
            query_block = first_block + b
            sinks = jnp.where(is_retr, 0, sink_ref[head_id])
            lowest = query_block - jnp.where(is_retr, 1, window_ref[head_id])

            def clear(c, carry):
                read = ((c < sinks) | (c > lowest)) & (c <= query_block)
                allowed_ref[h, b, c] = read.astype(jnp.int32)
                return carry

            lax.fori_loop(0, shape.block_total, clear, 0)
            for j in range(vert_ref.shape[2]):
                c = vert_ref[b, head_id, j]
                allowed_ref[h, b, jnp.where(is_retr, c, query_block)] = 1
            for j in range(slash_ref.shape[2]):
                c = query_block - slash_ref[b, head_id, j]
                allowed_ref[h, b, jnp.where(is_retr, c, query_block)] = 1


def read_lists(list_refs, lists, sems):
    return [pltpu.make_async_copy(list_refs[i], lists[i], sems.at[i]) for i in range(len(lists))]


def prepare_kernel(shape, n_lists, *refs):
    list_refs, q_raw_ref, mask_ref, q_ref = refs[:n_lists], *refs[n_lists:n_lists + 3]
    q_raw, wide, allowed_ref, *lists, sems = refs[n_lists + 3:]
    seq_pos = lax.axis_index("seq")
    copies = read_lists(list_refs, lists, sems)
    for copy in copies:
        copy.start()
    q_copy = pltpu.make_async_copy(q_raw_ref, q_raw, sems.at[n_lists])
    q_copy.start()
    for copy in copies:
        copy.wait()
    mark_allowed(shape, *lists, allowed_ref)

    def fill_masks(slot, carry):
        owner = owner_of(shape, seq_pos, slot)
        there = (owner >= 0) & (owner <= seq_pos)
        base = jnp.where(there, owner, 0) * shape.blocks_here
        for h in range(shape.heads):
            for b in range(shape.blocks_here):
                for j in range(shape.blocks_here):
                    seen = there & (allowed_ref[h, b, base + j] > 0)
                    mask_ref[h, b, pl.ds(slot * shape.blocks_here + j, 1), :] = jnp.full(
                        (1, shape.head_dim), jnp.where(seen, 1.0, 0.0), jnp.float32
                    )
        return carry

    lax.fori_loop(0, shape.n_slots, fill_masks, 0)
    q_copy.wait()
    wide[...] = q_raw[...].astype(jnp.float32)
    for h in range(shape.heads):
        q_ref[h] = wide[pl.ds(h, shape.rows, stride=shape.heads), :].astype(q_ref.dtype)


def own_kernel(shape, mask_ref, q_ref, own_ref, peak_ref, acc_ref):
    for h in range(shape.heads):
        for b, start in tiles_of(shape):
            rows = pl.ds(b * shape.rows_unit + start, ROW_TILE)
            width = (b + 1) * BLOCK
            s = scores(q_ref[h, rows, :], own_ref[h, :width, :]) * shape.factor
            columns = []
            for j in range(b):
                seen = mask_ref[h, b, pl.ds(j, 1), :]
                columns.append(jnp.where(seen > 0.0, s[:, j * BLOCK:(j + 1) * BLOCK], HIDDEN))
            diagonal = s[:, b * BLOCK:]
            row = start + lax.broadcasted_iota(jnp.int32, diagonal.shape, 0)
            column = lax.broadcasted_iota(jnp.int32, diagonal.shape, 1)
            columns.append(jnp.where(column * shape.group <= row, diagonal, HIDDEN))
            s = jnp.concatenate(columns, axis=1)
            m = jnp.max(s, axis=1, keepdims=True)
            peak_ref[h, rows, :] = jnp.broadcast_to(m, (ROW_TILE, BLOCK))
            p = jnp.exp2(s - m).astype(jnp.bfloat16)
            vals = with_ones(own_ref[shape.heads + h, :width, :])
            acc_ref[h, rows, :] = jnp.dot(p, vals, preferred_element_type=jnp.float32)


def mixed_tiles(shape, slots, h, mask_ref, q_ref, peak_ref, piece_refs):
    parts = []
    for at in range(0, len(slots), PIECES_AT_ONCE):
        some_slots = slots[at:at + PIECES_AT_ONCE]
        some_refs = piece_refs[at:at + PIECES_AT_ONCE]
        vals = jnp.concatenate([ref[shape.heads + h] for ref in some_refs], axis=0)
        seen_vals = []
        for b in range(shape.blocks_here):
            masks = jnp.concatenate(
                [
                    jnp.broadcast_to(
                        mask_ref[h, b, pl.ds(slot * shape.blocks_here + j, 1), :],
                        (BLOCK, shape.head_dim),
                    )
                    for slot in some_slots for j in range(shape.blocks_here)
                ],
                axis=0,
            ).astype(jnp.bfloat16)
            seen_vals.append(jnp.concatenate([vals * masks, masks], axis=1))
        parts.append((jnp.concatenate([ref[h] for ref in some_refs], axis=0), seen_vals))
    for b, start in tiles_of(shape):
        rows = pl.ds(b * shape.rows_unit + start, ROW_TILE)
        q = q_ref[h, rows, :]
        m = peak_ref[h, rows, :]
        mixed = None
        for keys, seen_vals in parts:
            s = scores(q, keys) * shape.factor
            p = jnp.exp2(s - jnp.concatenate([m] * (s.shape[1] // m.shape[1]), axis=1))
            part = jnp.dot(
                p.astype(jnp.bfloat16), seen_vals[b], preferred_element_type=jnp.float32
            )
            mixed = part if mixed is None else mixed + part
        yield rows, mixed


def middle_kernel(shape, slots, mask_ref, q_ref, peak_ref, acc_in, *refs):
    del acc_in
    piece_refs, acc_ref = refs[:-1], refs[-1]
    nearest = min(shape.away(slot) for slot in slots)

    @pl.when(lax.axis_index("seq") // INNER >= nearest)
    def _():
        for h in range(shape.heads):
            for rows, mixed in mixed_tiles(
                shape, slots, h, mask_ref, q_ref, peak_ref, piece_refs
            ):
                acc_ref[h, rows, :] += mixed


def last_kernel(shape, slots, n_lists, mask_ref, q_ref, peak_in, acc_in, *refs):
    del peak_in, acc_in
    heads, head_dim = shape.heads, shape.head_dim
    n, n_all = len(slots), shape.n_slots
    piece_refs, all_refs, list_refs = refs[:n], refs[n:n + n_all], refs[n + n_all:][:n_lists]
    out_ref, peak_ref, acc_ref, *scratch = refs[n + n_all + n_lists:]
    out_rows, worst, kv, allowed_ref, *lists, sems = scratch
    seq_pos = lax.axis_index("seq")
    first_block = seq_pos * shape.blocks_here
    line = seq_pos // INNER

    def finish(h, rows, sums):
        total = sums[:, head_dim:]
        out_rows[pl.ds(rows.start * heads + h, ROW_TILE, stride=heads), :] = (
            sums[:, :head_dim] / total
        )
        bad = jnp.where(total < SAFE_TOTAL, 0.0, 1.0)
        worst[...] = jnp.maximum(
            worst[...], jnp.max(bad.reshape(ROW_TILE // 8, 8, head_dim), axis=0)
        )

    def finish_all():
        for h in range(heads):
            for b, start in tiles_of(shape):
                rows = pl.ds(b * shape.rows_unit + start, ROW_TILE)
                finish(h, rows, acc_ref[h, rows, :])

    worst[...] = jnp.zeros_like(worst)
    steps = sorted({shape.away(slot) for slot in slots}) + [shape.outer]
    for least, below in zip([0] + steps, steps):
        here = [i for i, slot in enumerate(slots) if shape.away(slot) <= least]

        @pl.when((line >= least) & (line < below))
        def _(here=here):
            if not here:
                finish_all()
                return
            for h in range(heads):
                for rows, mixed in mixed_tiles(
                    shape, [slots[i] for i in here], h, mask_ref, q_ref, peak_ref,
                    [piece_refs[i] for i in here],
                ):
                    finish(h, rows, acc_ref[h, rows, :] + mixed)

    out_ref[...] = out_rows[...].astype(out_ref.dtype)

    @pl.when(jnp.max(worst[...]) > 0.0)
    def _():
        copies = read_lists(list_refs, lists, sems) + [
            pltpu.make_async_copy(all_refs[i], kv.at[i], sems.at[n_lists + i])
            for i in range(n_all)
        ]
        for copy in copies:
            copy.start()
        for copy in copies:
            copy.wait()
        mark_allowed(shape, *lists, allowed_ref)

        def every_tile(step):
            def slot_step(i, carry):
                owner = owner_of(shape, seq_pos, i)

                @pl.when((owner >= 0) & (owner <= seq_pos))
                def _():
                    for h in range(heads):
                        for b, start in tiles_of(shape):
                            rows = pl.ds(b * shape.rows_unit + start, ROW_TILE)
                            s = scores(q_ref[h, rows, :], kv[i, h]) * shape.factor
                            columns = []
                            for j in range(shape.blocks_here):
                                block = owner * shape.blocks_here + j
                                part = s[:, j * BLOCK:(j + 1) * BLOCK]
                                row = start + lax.broadcasted_iota(jnp.int32, part.shape, 0)
                                column = lax.broadcasted_iota(jnp.int32, part.shape, 1)
                                ahead = (first_block + b - block) * BLOCK
                                part = jnp.where(
                                    (column - ahead) * shape.group <= row, part, HIDDEN
                                )
                                seen = allowed_ref[h, b, block] > 0
                                columns.append(part + jnp.where(seen, 0.0, HIDDEN))
                            step(h, rows, jnp.concatenate(columns, axis=1), i)

                return carry

            lax.fori_loop(0, n_all, slot_step, 0)

        def widen(h, rows, s, i):
            m = jnp.max(s, axis=1, keepdims=True)
            peak_ref[h, rows, :] = jnp.maximum(peak_ref[h, rows, :], m)

        def collect(h, rows, s, i):
            m = peak_ref[h, rows, :]
            p = jnp.exp2(s - jnp.concatenate([m] * shape.blocks_here, axis=1))
            acc_ref[h, rows, :] += jnp.dot(
                p.astype(jnp.bfloat16), with_ones(kv[i, heads + h]),
                preferred_element_type=jnp.float32,
            )

        every_tile(widen)
        acc_ref[...] = jnp.zeros_like(acc_ref)
        every_tile(collect)
        finish_all()
        out_ref[...] = out_rows[...].astype(out_ref.dtype)


def per_device(
    n_seq, queries, keys, values, retrieval_ids, vertical_blocks, slash_offsets, sink_blocks,
    window_blocks,
):
    tokens_here, heads, width = queries.shape
    head_dim = keys.shape[2]
    group = width // head_dim
    blocks_here = tokens_here // BLOCK
    shape = Shape(heads, blocks_here, n_seq * blocks_here, group, head_dim, n_seq)
    outer = shape.outer

    vmem = pl.BlockSpec(memory_space=pltpu.VMEM)
    hbm = pl.BlockSpec(memory_space=pltpu.HBM)
    anywhere = pl.BlockSpec(memory_space=pl.ANY)
    mask_shape = jax.ShapeDtypeStruct(
        (heads, blocks_here, shape.block_total, head_dim), jnp.float32
    )
    q_shape = jax.ShapeDtypeStruct((heads, shape.rows, head_dim), jnp.bfloat16)
    peak_shape = jax.ShapeDtypeStruct((heads, shape.rows, head_dim), jnp.float32)
    acc_shape = jax.ShapeDtypeStruct((heads, shape.rows, 2 * head_dim), jnp.float32)
    allowed_scratch = pltpu.SMEM((heads, blocks_here, shape.block_total), jnp.int32)
    params = pltpu.CompilerParams(vmem_limit_bytes=16 << 20)
    cost = pl.CostEstimate(flops=1 << 20, transcendentals=0, bytes_accessed=1 << 10)

    own = jnp.concatenate(
        [jnp.transpose(keys, (1, 0, 2)), jnp.transpose(values, (1, 0, 2))], axis=0
    )
    q_raw = queries.reshape(tokens_here, heads, group, head_dim)
    q_raw = jnp.transpose(q_raw, (0, 2, 1, 3)).reshape(heads * shape.rows, head_dim)
    q_raw = pltpu.with_memory_space_constraint(q_raw, pltpu.HBM)
    lists = tuple(
        pltpu.with_memory_space_constraint(x, pltpu.HBM)
        for x in (retrieval_ids, vertical_blocks, slash_offsets, sink_blocks, window_blocks)
    )
    n_lists = len(lists)
    list_scratch = [pltpu.SMEM(x.shape, jnp.int32) for x in lists]

    def prepare():
        return pl.pallas_call(
            functools.partial(prepare_kernel, shape, n_lists),
            out_shape=(mask_shape, q_shape),
            in_specs=[hbm] * (n_lists + 1),
            out_specs=(vmem, vmem),
            scratch_shapes=[
                pltpu.VMEM((heads * shape.rows, head_dim), jnp.bfloat16),
                pltpu.VMEM((heads * shape.rows, head_dim), jnp.float32),
                allowed_scratch,
                *list_scratch,
                pltpu.SemaphoreType.DMA((n_lists + 1,)),
            ],
            compiler_params=params,
            cost_estimate=cost,
        )(*lists, q_raw)

    def start_sums():
        return pl.pallas_call(
            functools.partial(own_kernel, shape),
            out_shape=(peak_shape, acc_shape),
            in_specs=[vmem] * 3,
            out_specs=(vmem, vmem),
            compiler_params=params,
            cost_estimate=cost,
        )(mask, q, own)

    def add(acc, slots):
        return pl.pallas_call(
            functools.partial(middle_kernel, shape, slots),
            out_shape=acc_shape,
            in_specs=[vmem] * (4 + len(slots)),
            out_specs=vmem,
            input_output_aliases={3: 0},
            compiler_params=params,
            cost_estimate=cost,
        )(mask, q, peak, acc, *[piece[slot] for slot in slots])

    def send(x, pairs):
        return lax.ppermute(x, "seq", pairs)

    def along(x, least, step=1, most=outer):
        return send(x, [
            (s, s + step * INNER) for s in range(n_seq)
            if least <= s // INNER < min(most, outer - step)
        ])

    def across(x, least):
        return send(x, [
            (s, s ^ 1) for s in range(n_seq)
            if s // INNER >= least and (least > 0 or s % INNER == 0)
        ])

    piece = {0: own}
    if outer == 4:
        piece[1] = along(own, 0)
        piece[4] = send(own, [(s, s ^ 1) for s in range(n_seq) if s % INNER == 0 or s == 1])
        mask, q = prepare()
        piece[1], q = lax.optimization_barrier((piece[1], q))
        piece[2] = along(piece[1], 1)
        peak, acc = start_sums()
        piece[7] = along(piece[4], 0, step=3, most=1)
        near, acc, piece[4] = lax.optimization_barrier((piece[1], acc, piece[4]))
        piece[5] = across(near, 1)
        piece[2], acc = lax.optimization_barrier((piece[2], acc))
        piece[3] = along(piece[2], 2)
        piece[6] = across(piece[2], 2)
        acc = add(acc, [1, 4, 2, 7])
        last_slots = [5, 6, 3]
    else:
        mask, q = prepare()
        peak, acc = start_sums()
        for step in range(outer):
            if step + 1 < outer:
                piece[step + 1] = along(piece[step], step)
            piece[outer + step] = across(piece[step], step)
            if step > 0:
                acc = add(acc, [step, outer + step - 1])
            if step + 1 < outer:
                piece[step + 1], acc = lax.optimization_barrier((piece[step + 1], acc))
        last_slots = [n_seq - 1]

    out, _, _ = pl.pallas_call(
        functools.partial(last_kernel, shape, last_slots, n_lists),
        out_shape=(
            jax.ShapeDtypeStruct((heads * shape.rows, head_dim), jnp.bfloat16),
            peak_shape,
            acc_shape,
        ),
        in_specs=[vmem] * (4 + len(last_slots)) + [anywhere] * n_seq + [hbm] * n_lists,
        out_specs=(vmem, vmem, vmem),
        input_output_aliases={2: 1, 3: 2},
        scratch_shapes=[
            pltpu.VMEM((heads * shape.rows, head_dim), jnp.float32),
            pltpu.VMEM((8, head_dim), jnp.float32),
            pltpu.VMEM((n_seq,) + own.shape, jnp.bfloat16),
            allowed_scratch,
            *list_scratch,
            pltpu.SemaphoreType.DMA((n_lists + n_seq,)),
        ],
        compiler_params=pltpu.CompilerParams(
            vmem_limit_bytes=(16 << 20) + 2 * n_seq * own.size
        ),
        cost_estimate=cost,
    )(
        mask, q, peak, acc, *[piece[slot] for slot in last_slots],
        *[piece[slot] for slot in range(n_seq)], *lists,
    )
    out = out.reshape(tokens_here, group, heads, head_dim)
    return jnp.transpose(out, (0, 2, 1, 3)).reshape(tokens_here, heads, width)


def solution(mesh):
    in_specs = (
        P("seq", "head", None),
        P("seq", "head", None),
        P("seq", "head", None),
        P(),
        P("seq", None, None),
        P("seq", None, None),
        P(),
        P(),
    )
    out_specs = P("seq", "head", None)
    return jax.shard_map(
        functools.partial(per_device, mesh.shape["seq"]),
        mesh=mesh, in_specs=in_specs, out_specs=out_specs, check_vma=False,
    )
```

```python
import functools
import math

import jax
import jax.numpy as jnp
from jax import lax
from jax.experimental import pallas as pl
from jax.experimental.pallas import tpu as pltpu
from jax.sharding import PartitionSpec as P

KV_HEADS = 8
BLOCK = 128
INNER = 2
ROW_TILE = 256
PIECES_AT_ONCE = 2
HIDDEN = -1e30
SAFE_TOTAL = 1e30


class Shape:
    def __init__(self, heads, blocks_here, block_total, group, head_dim, n_slots):
        self.heads = heads
        self.blocks_here = blocks_here
        self.block_total = block_total
        self.group = group
        self.head_dim = head_dim
        self.n_slots = n_slots
        self.outer = n_slots // INNER
        self.rows_unit = BLOCK * group
        self.rows = blocks_here * self.rows_unit
        self.factor = head_dim ** -0.5 * math.log2(math.e)

    def away(self, slot):
        return slot % self.outer


def owner_of(shape, seq_pos, slot):
    crossed = slot >= shape.outer
    line = seq_pos // INNER - jnp.where(crossed, slot - shape.outer, slot)
    place = seq_pos % INNER
    return line * INNER + jnp.where(crossed, 1 - place, place)


def scores(q, keys):
    return lax.dot_general(q, keys, (((1,), (1,)), ((), ())), preferred_element_type=jnp.float32)


def with_ones(vals):
    return jnp.concatenate([vals, jnp.ones_like(vals)], axis=1)


def tiles_of(shape):
    return [(b, r * ROW_TILE) for b in range(shape.blocks_here)
            for r in range(shape.rows_unit // ROW_TILE)]


def mark_allowed(shape, retr_ref, vert_ref, slash_ref, sink_ref, window_ref, allowed_ref):
    first_block = lax.axis_index("seq") * shape.blocks_here
    first_head = lax.axis_index("head") * shape.heads
    n_retr = retr_ref.shape[0]
    for h in range(shape.heads):
        head_id = first_head + h
        is_retr = functools.reduce(
            jnp.logical_or, [retr_ref[i] == head_id for i in range(n_retr)]
        )
        for b in range(shape.blocks_here):
            query_block = first_block + b
            sinks = jnp.where(is_retr, 0, sink_ref[head_id])
            lowest = query_block - jnp.where(is_retr, 1, window_ref[head_id])

            def clear(c, carry):
                read = ((c < sinks) | (c > lowest)) & (c <= query_block)
                allowed_ref[h, b, c] = read.astype(jnp.int32)
                return carry

            lax.fori_loop(0, shape.block_total, clear, 0)
            for j in range(vert_ref.shape[2]):
                c = vert_ref[b, head_id, j]
                allowed_ref[h, b, jnp.where(is_retr, c, query_block)] = 1
            for j in range(slash_ref.shape[2]):
                c = query_block - slash_ref[b, head_id, j]
                allowed_ref[h, b, jnp.where(is_retr, c, query_block)] = 1


def read_lists(list_refs, lists, sems):
    return [pltpu.make_async_copy(list_refs[i], lists[i], sems.at[i]) for i in range(len(lists))]


def prepare_kernel(shape, n_lists, *refs):
    list_refs, q_raw_ref, mask_ref, q_ref = refs[:n_lists], *refs[n_lists:n_lists + 3]
    q_raw, wide, allowed_ref, *lists, sems = refs[n_lists + 3:]
    seq_pos = lax.axis_index("seq")
    copies = read_lists(list_refs, lists, sems)
    for copy in copies:
        copy.start()
    q_copy = pltpu.make_async_copy(q_raw_ref, q_raw, sems.at[n_lists])
    q_copy.start()
    for copy in copies:
        copy.wait()
    mark_allowed(shape, *lists, allowed_ref)

    def fill_masks(slot, carry):
        owner = owner_of(shape, seq_pos, slot)
        there = (owner >= 0) & (owner <= seq_pos)
        base = jnp.where(there, owner, 0) * shape.blocks_here
        for h in range(shape.heads):
            for b in range(shape.blocks_here):
                for j in range(shape.blocks_here):
                    seen = there & (allowed_ref[h, b, base + j] > 0)
                    mask_ref[h, b, pl.ds(slot * shape.blocks_here + j, 1), :] = jnp.full(
                        (1, shape.head_dim), jnp.where(seen, 1.0, 0.0), jnp.float32
                    )
        return carry

    lax.fori_loop(0, shape.n_slots, fill_masks, 0)
    q_copy.wait()
    wide[...] = q_raw[...].astype(jnp.float32)
    for h in range(shape.heads):
        q_ref[h] = wide[pl.ds(h, shape.rows, stride=shape.heads), :].astype(q_ref.dtype)


def own_kernel(shape, mask_ref, q_ref, own_ref, peak_ref, acc_ref):
    for h in range(shape.heads):
        for b, start in tiles_of(shape):
            rows = pl.ds(b * shape.rows_unit + start, ROW_TILE)
            width = (b + 1) * BLOCK
            s = scores(q_ref[h, rows, :], own_ref[h, :width, :]) * shape.factor
            columns = []
            for j in range(b):
                seen = mask_ref[h, b, pl.ds(j, 1), :]
                columns.append(jnp.where(seen > 0.0, s[:, j * BLOCK:(j + 1) * BLOCK], HIDDEN))
            diagonal = s[:, b * BLOCK:]
            row = start + lax.broadcasted_iota(jnp.int32, diagonal.shape, 0)
            column = lax.broadcasted_iota(jnp.int32, diagonal.shape, 1)
            columns.append(jnp.where(column * shape.group <= row, diagonal, HIDDEN))
            s = jnp.concatenate(columns, axis=1)
            m = jnp.max(s, axis=1, keepdims=True)
            peak_ref[h, rows, :] = jnp.broadcast_to(m, (ROW_TILE, BLOCK))
            p = jnp.exp2(s - m).astype(jnp.bfloat16)
            vals = with_ones(own_ref[shape.heads + h, :width, :])
            acc_ref[h, rows, :] = jnp.dot(p, vals, preferred_element_type=jnp.float32)


def mixed_tiles(shape, slots, h, mask_ref, q_ref, peak_ref, piece_refs):
    parts = []
    for at in range(0, len(slots), PIECES_AT_ONCE):
        some_slots = slots[at:at + PIECES_AT_ONCE]
        some_refs = piece_refs[at:at + PIECES_AT_ONCE]
        vals = jnp.concatenate([ref[shape.heads + h] for ref in some_refs], axis=0)
        seen_vals = []
        for b in range(shape.blocks_here):
            masks = jnp.concatenate(
                [
                    jnp.broadcast_to(
                        mask_ref[h, b, pl.ds(slot * shape.blocks_here + j, 1), :],
                        (BLOCK, shape.head_dim),
                    )
                    for slot in some_slots for j in range(shape.blocks_here)
                ],
                axis=0,
            ).astype(jnp.bfloat16)
            seen_vals.append(jnp.concatenate([vals * masks, masks], axis=1))
        parts.append((jnp.concatenate([ref[h] for ref in some_refs], axis=0), seen_vals))
    for b, start in tiles_of(shape):
        rows = pl.ds(b * shape.rows_unit + start, ROW_TILE)
        q = q_ref[h, rows, :]
        m = peak_ref[h, rows, :]
        mixed = None
        for keys, seen_vals in parts:
            s = scores(q, keys) * shape.factor
            p = jnp.exp2(s - jnp.concatenate([m] * (s.shape[1] // m.shape[1]), axis=1))
            part = jnp.dot(
                p.astype(jnp.bfloat16), seen_vals[b], preferred_element_type=jnp.float32
            )
            mixed = part if mixed is None else mixed + part
        yield rows, mixed


def middle_kernel(shape, slots, mask_ref, q_ref, peak_ref, acc_in, *refs):
    del acc_in
    piece_refs, acc_ref = refs[:-1], refs[-1]
    nearest = min(shape.away(slot) for slot in slots)

    @pl.when(lax.axis_index("seq") // INNER >= nearest)
    def _():
        for h in range(shape.heads):
            for rows, mixed in mixed_tiles(
                shape, slots, h, mask_ref, q_ref, peak_ref, piece_refs
            ):
                acc_ref[h, rows, :] += mixed


def last_kernel(shape, slots, n_lists, mask_ref, q_ref, peak_in, acc_in, *refs):
    del peak_in, acc_in
    heads, head_dim = shape.heads, shape.head_dim
    n, n_all = len(slots), shape.n_slots
    piece_refs, all_refs, list_refs = refs[:n], refs[n:n + n_all], refs[n + n_all:][:n_lists]
    out_ref, peak_ref, acc_ref, *scratch = refs[n + n_all + n_lists:]
    out_rows, worst, kv, allowed_ref, *lists, sems = scratch
    seq_pos = lax.axis_index("seq")
    first_block = seq_pos * shape.blocks_here
    line = seq_pos // INNER

    def finish(h, rows, sums):
        total = sums[:, head_dim:]
        out_rows[pl.ds(rows.start * heads + h, ROW_TILE, stride=heads), :] = (
            sums[:, :head_dim] / total
        )
        bad = jnp.where(total < SAFE_TOTAL, 0.0, 1.0)
        worst[...] = jnp.maximum(
            worst[...], jnp.max(bad.reshape(ROW_TILE // 8, 8, head_dim), axis=0)
        )

    def finish_all():
        for h in range(heads):
            for b, start in tiles_of(shape):
                rows = pl.ds(b * shape.rows_unit + start, ROW_TILE)
                finish(h, rows, acc_ref[h, rows, :])

    worst[...] = jnp.zeros_like(worst)
    steps = sorted({shape.away(slot) for slot in slots}) + [shape.outer]
    for least, below in zip([0] + steps, steps):
        here = [i for i, slot in enumerate(slots) if shape.away(slot) <= least]

        @pl.when((line >= least) & (line < below))
        def _(here=here):
            if not here:
                finish_all()
                return
            for h in range(heads):
                for rows, mixed in mixed_tiles(
                    shape, [slots[i] for i in here], h, mask_ref, q_ref, peak_ref,
                    [piece_refs[i] for i in here],
                ):
                    finish(h, rows, acc_ref[h, rows, :] + mixed)

    out_ref[...] = out_rows[...].astype(out_ref.dtype)

    @pl.when(jnp.max(worst[...]) > 0.0)
    def _():
        copies = read_lists(list_refs, lists, sems) + [
            pltpu.make_async_copy(all_refs[i], kv.at[i], sems.at[n_lists + i])
            for i in range(n_all)
        ]
        for copy in copies:
            copy.start()
        for copy in copies:
            copy.wait()
        mark_allowed(shape, *lists, allowed_ref)

        def every_tile(step):
            def slot_step(i, carry):
                owner = owner_of(shape, seq_pos, i)

                @pl.when((owner >= 0) & (owner <= seq_pos))
                def _():
                    for h in range(heads):
                        for b, start in tiles_of(shape):
                            rows = pl.ds(b * shape.rows_unit + start, ROW_TILE)
                            s = scores(q_ref[h, rows, :], kv[i, h]) * shape.factor
                            columns = []
                            for j in range(shape.blocks_here):
                                block = owner * shape.blocks_here + j
                                part = s[:, j * BLOCK:(j + 1) * BLOCK]
                                row = start + lax.broadcasted_iota(jnp.int32, part.shape, 0)
                                column = lax.broadcasted_iota(jnp.int32, part.shape, 1)
                                ahead = (first_block + b - block) * BLOCK
                                part = jnp.where(
                                    (column - ahead) * shape.group <= row, part, HIDDEN
                                )
                                seen = allowed_ref[h, b, block] > 0
                                columns.append(part + jnp.where(seen, 0.0, HIDDEN))
                            step(h, rows, jnp.concatenate(columns, axis=1), i)

                return carry

            lax.fori_loop(0, n_all, slot_step, 0)

        def widen(h, rows, s, i):
            m = jnp.max(s, axis=1, keepdims=True)
            peak_ref[h, rows, :] = jnp.maximum(peak_ref[h, rows, :], m)

        def collect(h, rows, s, i):
            m = peak_ref[h, rows, :]
            p = jnp.exp2(s - jnp.concatenate([m] * shape.blocks_here, axis=1))
            acc_ref[h, rows, :] += jnp.dot(
                p.astype(jnp.bfloat16), with_ones(kv[i, heads + h]),
                preferred_element_type=jnp.float32,
            )

        every_tile(widen)
        acc_ref[...] = jnp.zeros_like(acc_ref)
        every_tile(collect)
        finish_all()
        out_ref[...] = out_rows[...].astype(out_ref.dtype)


def per_device(
    n_seq, queries, keys, values, retrieval_ids, vertical_blocks, slash_offsets, sink_blocks,
    window_blocks,
):
    tokens_here, heads, width = queries.shape
    head_dim = keys.shape[2]
    group = width // head_dim
    blocks_here = tokens_here // BLOCK
    shape = Shape(heads, blocks_here, n_seq * blocks_here, group, head_dim, n_seq)
    outer = shape.outer

    vmem = pl.BlockSpec(memory_space=pltpu.VMEM)
    hbm = pl.BlockSpec(memory_space=pltpu.HBM)
    anywhere = pl.BlockSpec(memory_space=pl.ANY)
    mask_shape = jax.ShapeDtypeStruct(
        (heads, blocks_here, shape.block_total, head_dim), jnp.float32
    )
    q_shape = jax.ShapeDtypeStruct((heads, shape.rows, head_dim), jnp.bfloat16)
    peak_shape = jax.ShapeDtypeStruct((heads, shape.rows, head_dim), jnp.float32)
    acc_shape = jax.ShapeDtypeStruct((heads, shape.rows, 2 * head_dim), jnp.float32)
    allowed_scratch = pltpu.SMEM((heads, blocks_here, shape.block_total), jnp.int32)
    params = pltpu.CompilerParams(vmem_limit_bytes=16 << 20)
    cost = pl.CostEstimate(flops=1 << 20, transcendentals=0, bytes_accessed=1 << 10)

    own = jnp.concatenate(
        [jnp.transpose(keys, (1, 0, 2)), jnp.transpose(values, (1, 0, 2))], axis=0
    )
    q_raw = queries.reshape(tokens_here, heads, group, head_dim)
    q_raw = jnp.transpose(q_raw, (0, 2, 1, 3)).reshape(heads * shape.rows, head_dim)
    q_raw = pltpu.with_memory_space_constraint(q_raw, pltpu.HBM)
    lists = tuple(
        pltpu.with_memory_space_constraint(x, pltpu.HBM)
        for x in (retrieval_ids, vertical_blocks, slash_offsets, sink_blocks, window_blocks)
    )
    n_lists = len(lists)
    list_scratch = [pltpu.SMEM(x.shape, jnp.int32) for x in lists]

    def prepare(q_raw):
        return pl.pallas_call(
            functools.partial(prepare_kernel, shape, n_lists),
            out_shape=(mask_shape, q_shape),
            in_specs=[hbm] * (n_lists + 1),
            out_specs=(vmem, vmem),
            scratch_shapes=[
                pltpu.VMEM((heads * shape.rows, head_dim), jnp.bfloat16),
                pltpu.VMEM((heads * shape.rows, head_dim), jnp.float32),
                allowed_scratch,
                *list_scratch,
                pltpu.SemaphoreType.DMA((n_lists + 1,)),
            ],
            compiler_params=params,
            cost_estimate=cost,
        )(*lists, q_raw)

    def start_sums():
        return pl.pallas_call(
            functools.partial(own_kernel, shape),
            out_shape=(peak_shape, acc_shape),
            in_specs=[vmem] * 3,
            out_specs=(vmem, vmem),
            compiler_params=params,
            cost_estimate=cost,
        )(mask, q, own)

    def add(acc, slots):
        return pl.pallas_call(
            functools.partial(middle_kernel, shape, slots),
            out_shape=acc_shape,
            in_specs=[vmem] * (4 + len(slots)),
            out_specs=vmem,
            input_output_aliases={3: 0},
            compiler_params=params,
            cost_estimate=cost,
        )(mask, q, peak, acc, *[piece[slot] for slot in slots])

    def send(x, pairs):
        return lax.ppermute(x, "seq", pairs)

    def along(x, least, step=1, most=outer):
        return send(x, [
            (s, s + step * INNER) for s in range(n_seq)
            if least <= s // INNER < min(most, outer - step)
        ])

    def across(x, least):
        return send(x, [
            (s, s ^ 1) for s in range(n_seq)
            if s // INNER >= least and (least > 0 or s % INNER == 0)
        ])

    piece = {0: own}
    if outer == 4:
        first = [along(own, k, most=k + 1) for k in range(3)]
        second = [None, along(first[0], 1, most=2), None]
        q_raw, first[0] = lax.optimization_barrier((q_raw, first[0]))
        mask, q = prepare(q_raw)
        first[1], q = lax.optimization_barrier((first[1], q))
        second[2] = along(first[1], 2)
        peak, acc = start_sums()
        late, acc = lax.optimization_barrier((own, acc))
        second[1], first[2], acc = lax.optimization_barrier((second[1], first[2], acc))
        piece[4] = send(late, [(s, s ^ 1) for s in range(n_seq) if s % INNER == 0 or s == 1])
        piece[3] = along(second[1], 2)
        piece[1] = first[0] + first[1] + first[2]
        piece[5] = across(piece[1], 1)
        piece[7] = along(piece[4], 0, step=3, most=1)
        piece[2] = second[1] + second[2]
        piece[6] = across(piece[2], 2)
        acc = add(acc, [1, 4])
        acc = add(acc, [3, 2])
        acc = add(acc, [5])
        last_slots = [6, 7]
    else:
        mask, q = prepare(q_raw)
        peak, acc = start_sums()
        for step in range(outer):
            if step + 1 < outer:
                piece[step + 1] = along(piece[step], step)
            piece[outer + step] = across(piece[step], step)
            if step > 0:
                acc = add(acc, [step, outer + step - 1])
            if step + 1 < outer:
                piece[step + 1], acc = lax.optimization_barrier((piece[step + 1], acc))
        last_slots = [n_seq - 1]

    out, _, _ = pl.pallas_call(
        functools.partial(last_kernel, shape, last_slots, n_lists),
        out_shape=(
            jax.ShapeDtypeStruct((heads * shape.rows, head_dim), jnp.bfloat16),
            peak_shape,
            acc_shape,
        ),
        in_specs=[vmem] * (4 + len(last_slots)) + [anywhere] * n_seq + [hbm] * n_lists,
        out_specs=(vmem, vmem, vmem),
        input_output_aliases={2: 1, 3: 2},
        scratch_shapes=[
            pltpu.VMEM((heads * shape.rows, head_dim), jnp.float32),
            pltpu.VMEM((8, head_dim), jnp.float32),
            pltpu.VMEM((n_seq,) + own.shape, jnp.bfloat16),
            allowed_scratch,
            *list_scratch,
            pltpu.SemaphoreType.DMA((n_lists + n_seq,)),
        ],
        compiler_params=pltpu.CompilerParams(
            vmem_limit_bytes=(16 << 20) + 2 * n_seq * own.size
        ),
        cost_estimate=cost,
    )(
        mask, q, peak, acc, *[piece[slot] for slot in last_slots],
        *[piece[slot] for slot in range(n_seq)], *lists,
    )
    out = out.reshape(tokens_here, group, heads, head_dim)
    return jnp.transpose(out, (0, 2, 1, 3)).reshape(tokens_here, heads, width)


def solution(mesh):
    in_specs = (
        P("seq", "head", None),
        P("seq", "head", None),
        P("seq", "head", None),
        P(),
        P("seq", None, None),
        P("seq", None, None),
        P(),
        P(),
    )
    out_specs = P("seq", "head", None)
    return jax.shard_map(
        functools.partial(per_device, mesh.shape["seq"]),
        mesh=mesh, in_specs=in_specs, out_specs=out_specs, check_vma=False,
    )
```

```python
import functools
import math

import jax
import jax.numpy as jnp
from jax import lax
from jax.experimental import pallas as pl
from jax.experimental.pallas import tpu as pltpu
from jax.sharding import PartitionSpec as P

KV_HEADS = 8
BLOCK = 128
INNER = 2
ROW_TILE = 256
PIECES_AT_ONCE = 2
HIDDEN = -1e30
SAFE_TOTAL = 1e30


class Shape:
    def __init__(self, heads, blocks_here, block_total, group, head_dim, n_slots):
        self.heads = heads
        self.blocks_here = blocks_here
        self.block_total = block_total
        self.group = group
        self.head_dim = head_dim
        self.n_slots = n_slots
        self.outer = n_slots // INNER
        self.rows_unit = BLOCK * group
        self.rows = blocks_here * self.rows_unit
        self.factor = head_dim ** -0.5 * math.log2(math.e)

    def away(self, slot):
        return slot % self.outer


def owner_of(shape, seq_pos, slot):
    crossed = slot >= shape.outer
    line = seq_pos // INNER - jnp.where(crossed, slot - shape.outer, slot)
    place = seq_pos % INNER
    return line * INNER + jnp.where(crossed, 1 - place, place)


def scores(q, keys):
    return lax.dot_general(q, keys, (((1,), (1,)), ((), ())), preferred_element_type=jnp.float32)


def with_ones(vals):
    return jnp.concatenate([vals, jnp.ones_like(vals)], axis=1)


def tiles_of(shape):
    return [(b, r * ROW_TILE) for b in range(shape.blocks_here)
            for r in range(shape.rows_unit // ROW_TILE)]


def mark_allowed(shape, retr_ref, vert_ref, slash_ref, sink_ref, window_ref, allowed_ref):
    first_block = lax.axis_index("seq") * shape.blocks_here
    first_head = lax.axis_index("head") * shape.heads
    n_retr = retr_ref.shape[0]
    for h in range(shape.heads):
        head_id = first_head + h
        is_retr = functools.reduce(
            jnp.logical_or, [retr_ref[i] == head_id for i in range(n_retr)]
        )
        for b in range(shape.blocks_here):
            query_block = first_block + b
            sinks = jnp.where(is_retr, 0, sink_ref[head_id])
            lowest = query_block - jnp.where(is_retr, 1, window_ref[head_id])

            def clear(c, carry):
                read = ((c < sinks) | (c > lowest)) & (c <= query_block)
                allowed_ref[h, b, c] = read.astype(jnp.int32)
                return carry

            lax.fori_loop(0, shape.block_total, clear, 0)
            for j in range(vert_ref.shape[2]):
                c = vert_ref[b, head_id, j]
                allowed_ref[h, b, jnp.where(is_retr, c, query_block)] = 1
            for j in range(slash_ref.shape[2]):
                c = query_block - slash_ref[b, head_id, j]
                allowed_ref[h, b, jnp.where(is_retr, c, query_block)] = 1


def read_lists(list_refs, lists, sems):
    return [pltpu.make_async_copy(list_refs[i], lists[i], sems.at[i]) for i in range(len(lists))]


def prepare_kernel(shape, n_lists, *refs):
    list_refs, q_raw_ref, mask_ref, q_ref = refs[:n_lists], *refs[n_lists:n_lists + 3]
    q_raw, wide, allowed_ref, *lists, sems = refs[n_lists + 3:]
    seq_pos = lax.axis_index("seq")
    copies = read_lists(list_refs, lists, sems)
    for copy in copies:
        copy.start()
    q_copy = pltpu.make_async_copy(q_raw_ref, q_raw, sems.at[n_lists])
    q_copy.start()
    for copy in copies:
        copy.wait()
    mark_allowed(shape, *lists, allowed_ref)

    def fill_masks(slot, carry):
        owner = owner_of(shape, seq_pos, slot)
        there = (owner >= 0) & (owner <= seq_pos)
        base = jnp.where(there, owner, 0) * shape.blocks_here
        for h in range(shape.heads):
            for b in range(shape.blocks_here):
                for j in range(shape.blocks_here):
                    seen = there & (allowed_ref[h, b, base + j] > 0)
                    mask_ref[h, b, pl.ds(slot * shape.blocks_here + j, 1), :] = jnp.full(
                        (1, shape.head_dim), jnp.where(seen, 1.0, 0.0), jnp.float32
                    )
        return carry

    lax.fori_loop(0, shape.n_slots, fill_masks, 0)
    q_copy.wait()
    wide[...] = q_raw[...].astype(jnp.float32)
    for h in range(shape.heads):
        q_ref[h] = wide[pl.ds(h, shape.rows, stride=shape.heads), :].astype(q_ref.dtype)


def own_kernel(shape, mask_ref, q_ref, own_ref, peak_ref, acc_ref):
    for h in range(shape.heads):
        for b, start in tiles_of(shape):
            rows = pl.ds(b * shape.rows_unit + start, ROW_TILE)
            width = (b + 1) * BLOCK
            s = scores(q_ref[h, rows, :], own_ref[h, :width, :]) * shape.factor
            columns = []
            for j in range(b):
                seen = mask_ref[h, b, pl.ds(j, 1), :]
                columns.append(jnp.where(seen > 0.0, s[:, j * BLOCK:(j + 1) * BLOCK], HIDDEN))
            diagonal = s[:, b * BLOCK:]
            row = start + lax.broadcasted_iota(jnp.int32, diagonal.shape, 0)
            column = lax.broadcasted_iota(jnp.int32, diagonal.shape, 1)
            columns.append(jnp.where(column * shape.group <= row, diagonal, HIDDEN))
            s = jnp.concatenate(columns, axis=1)
            m = jnp.max(s, axis=1, keepdims=True)
            peak_ref[h, rows, :] = jnp.broadcast_to(m, (ROW_TILE, BLOCK))
            p = jnp.exp2(s - m).astype(jnp.bfloat16)
            vals = with_ones(own_ref[shape.heads + h, :width, :])
            acc_ref[h, rows, :] = jnp.dot(p, vals, preferred_element_type=jnp.float32)


def mixed_tiles(shape, slots, h, mask_ref, q_ref, peak_ref, piece_refs):
    parts = []
    for at in range(0, len(slots), PIECES_AT_ONCE):
        some_slots = slots[at:at + PIECES_AT_ONCE]
        some_refs = piece_refs[at:at + PIECES_AT_ONCE]
        vals = jnp.concatenate([ref[shape.heads + h] for ref in some_refs], axis=0)
        seen_vals = []
        for b in range(shape.blocks_here):
            masks = jnp.concatenate(
                [
                    jnp.broadcast_to(
                        mask_ref[h, b, pl.ds(slot * shape.blocks_here + j, 1), :],
                        (BLOCK, shape.head_dim),
                    )
                    for slot in some_slots for j in range(shape.blocks_here)
                ],
                axis=0,
            ).astype(jnp.bfloat16)
            seen_vals.append(jnp.concatenate([vals * masks, masks], axis=1))
        parts.append((jnp.concatenate([ref[h] for ref in some_refs], axis=0), seen_vals))
    for b, start in tiles_of(shape):
        rows = pl.ds(b * shape.rows_unit + start, ROW_TILE)
        q = q_ref[h, rows, :]
        m = peak_ref[h, rows, :]
        mixed = None
        for keys, seen_vals in parts:
            s = scores(q, keys) * shape.factor
            p = jnp.exp2(s - jnp.concatenate([m] * (s.shape[1] // m.shape[1]), axis=1))
            part = jnp.dot(
                p.astype(jnp.bfloat16), seen_vals[b], preferred_element_type=jnp.float32
            )
            mixed = part if mixed is None else mixed + part
        yield rows, mixed


def middle_kernel(shape, slots, mask_ref, q_ref, peak_ref, acc_in, *refs):
    del acc_in
    piece_refs, acc_ref = refs[:-1], refs[-1]
    nearest = min(shape.away(slot) for slot in slots)

    @pl.when(lax.axis_index("seq") // INNER >= nearest)
    def _():
        for h in range(shape.heads):
            for rows, mixed in mixed_tiles(
                shape, slots, h, mask_ref, q_ref, peak_ref, piece_refs
            ):
                acc_ref[h, rows, :] += mixed


def last_kernel(shape, slots, n_lists, mask_ref, q_ref, peak_in, acc_in, *refs):
    del peak_in, acc_in
    heads, head_dim = shape.heads, shape.head_dim
    n, n_all = len(slots), shape.n_slots
    piece_refs, all_refs, list_refs = refs[:n], refs[n:n + n_all], refs[n + n_all:][:n_lists]
    out_ref, peak_ref, acc_ref, *scratch = refs[n + n_all + n_lists:]
    out_rows, worst, kv, allowed_ref, *lists, sems = scratch
    seq_pos = lax.axis_index("seq")
    first_block = seq_pos * shape.blocks_here
    line = seq_pos // INNER

    def finish(h, rows, sums):
        total = sums[:, head_dim:]
        out_rows[pl.ds(rows.start * heads + h, ROW_TILE, stride=heads), :] = (
            sums[:, :head_dim] / total
        )
        bad = jnp.where(total < SAFE_TOTAL, 0.0, 1.0)
        worst[...] = jnp.maximum(
            worst[...], jnp.max(bad.reshape(ROW_TILE // 8, 8, head_dim), axis=0)
        )

    def finish_all():
        for h in range(heads):
            for b, start in tiles_of(shape):
                rows = pl.ds(b * shape.rows_unit + start, ROW_TILE)
                finish(h, rows, acc_ref[h, rows, :])

    worst[...] = jnp.zeros_like(worst)
    steps = sorted({shape.away(slot) for slot in slots}) + [shape.outer]
    for least, below in zip([0] + steps, steps):
        here = [i for i, slot in enumerate(slots) if shape.away(slot) <= least]

        @pl.when((line >= least) & (line < below))
        def _(here=here):
            if not here:
                finish_all()
                return
            for h in range(heads):
                for rows, mixed in mixed_tiles(
                    shape, [slots[i] for i in here], h, mask_ref, q_ref, peak_ref,
                    [piece_refs[i] for i in here],
                ):
                    finish(h, rows, acc_ref[h, rows, :] + mixed)

    out_ref[...] = out_rows[...].astype(out_ref.dtype)

    @pl.when(jnp.max(worst[...]) > 0.0)
    def _():
        copies = read_lists(list_refs, lists, sems) + [
            pltpu.make_async_copy(all_refs[i], kv.at[i], sems.at[n_lists + i])
            for i in range(n_all)
        ]
        for copy in copies:
            copy.start()
        for copy in copies:
            copy.wait()
        mark_allowed(shape, *lists, allowed_ref)

        def every_tile(step):
            def slot_step(i, carry):
                owner = owner_of(shape, seq_pos, i)

                @pl.when((owner >= 0) & (owner <= seq_pos))
                def _():
                    for h in range(heads):
                        for b, start in tiles_of(shape):
                            rows = pl.ds(b * shape.rows_unit + start, ROW_TILE)
                            s = scores(q_ref[h, rows, :], kv[i, h]) * shape.factor
                            columns = []
                            for j in range(shape.blocks_here):
                                block = owner * shape.blocks_here + j
                                part = s[:, j * BLOCK:(j + 1) * BLOCK]
                                row = start + lax.broadcasted_iota(jnp.int32, part.shape, 0)
                                column = lax.broadcasted_iota(jnp.int32, part.shape, 1)
                                ahead = (first_block + b - block) * BLOCK
                                part = jnp.where(
                                    (column - ahead) * shape.group <= row, part, HIDDEN
                                )
                                seen = allowed_ref[h, b, block] > 0
                                columns.append(part + jnp.where(seen, 0.0, HIDDEN))
                            step(h, rows, jnp.concatenate(columns, axis=1), i)

                return carry

            lax.fori_loop(0, n_all, slot_step, 0)

        def widen(h, rows, s, i):
            m = jnp.max(s, axis=1, keepdims=True)
            peak_ref[h, rows, :] = jnp.maximum(peak_ref[h, rows, :], m)

        def collect(h, rows, s, i):
            m = peak_ref[h, rows, :]
            p = jnp.exp2(s - jnp.concatenate([m] * shape.blocks_here, axis=1))
            acc_ref[h, rows, :] += jnp.dot(
                p.astype(jnp.bfloat16), with_ones(kv[i, heads + h]),
                preferred_element_type=jnp.float32,
            )

        every_tile(widen)
        acc_ref[...] = jnp.zeros_like(acc_ref)
        every_tile(collect)
        finish_all()
        out_ref[...] = out_rows[...].astype(out_ref.dtype)


def per_device(
    n_seq, queries, keys, values, retrieval_ids, vertical_blocks, slash_offsets, sink_blocks,
    window_blocks,
):
    tokens_here, heads, width = queries.shape
    head_dim = keys.shape[2]
    group = width // head_dim
    blocks_here = tokens_here // BLOCK
    shape = Shape(heads, blocks_here, n_seq * blocks_here, group, head_dim, n_seq)
    outer = shape.outer

    vmem = pl.BlockSpec(memory_space=pltpu.VMEM)
    hbm = pl.BlockSpec(memory_space=pltpu.HBM)
    anywhere = pl.BlockSpec(memory_space=pl.ANY)
    mask_shape = jax.ShapeDtypeStruct(
        (heads, blocks_here, shape.block_total, head_dim), jnp.float32
    )
    q_shape = jax.ShapeDtypeStruct((heads, shape.rows, head_dim), jnp.bfloat16)
    peak_shape = jax.ShapeDtypeStruct((heads, shape.rows, head_dim), jnp.float32)
    acc_shape = jax.ShapeDtypeStruct((heads, shape.rows, 2 * head_dim), jnp.float32)
    allowed_scratch = pltpu.SMEM((heads, blocks_here, shape.block_total), jnp.int32)
    params = pltpu.CompilerParams(vmem_limit_bytes=16 << 20)
    cost = pl.CostEstimate(flops=1 << 20, transcendentals=0, bytes_accessed=1 << 10)

    own = jnp.concatenate(
        [jnp.transpose(keys, (1, 0, 2)), jnp.transpose(values, (1, 0, 2))], axis=0
    )
    q_raw = queries.reshape(tokens_here, heads, group, head_dim)
    q_raw = jnp.transpose(q_raw, (0, 2, 1, 3)).reshape(heads * shape.rows, head_dim)
    q_raw = pltpu.with_memory_space_constraint(q_raw, pltpu.HBM)
    lists = tuple(
        pltpu.with_memory_space_constraint(x, pltpu.HBM)
        for x in (retrieval_ids, vertical_blocks, slash_offsets, sink_blocks, window_blocks)
    )
    n_lists = len(lists)
    list_scratch = [pltpu.SMEM(x.shape, jnp.int32) for x in lists]

    def prepare(q_raw):
        return pl.pallas_call(
            functools.partial(prepare_kernel, shape, n_lists),
            out_shape=(mask_shape, q_shape),
            in_specs=[hbm] * (n_lists + 1),
            out_specs=(vmem, vmem),
            scratch_shapes=[
                pltpu.VMEM((heads * shape.rows, head_dim), jnp.bfloat16),
                pltpu.VMEM((heads * shape.rows, head_dim), jnp.float32),
                allowed_scratch,
                *list_scratch,
                pltpu.SemaphoreType.DMA((n_lists + 1,)),
            ],
            compiler_params=params,
            cost_estimate=cost,
        )(*lists, q_raw)

    def start_sums():
        return pl.pallas_call(
            functools.partial(own_kernel, shape),
            out_shape=(peak_shape, acc_shape),
            in_specs=[vmem] * 3,
            out_specs=(vmem, vmem),
            compiler_params=params,
            cost_estimate=cost,
        )(mask, q, own)

    def add(acc, slots):
        return pl.pallas_call(
            functools.partial(middle_kernel, shape, slots),
            out_shape=acc_shape,
            in_specs=[vmem] * (4 + len(slots)),
            out_specs=vmem,
            input_output_aliases={3: 0},
            compiler_params=params,
            cost_estimate=cost,
        )(mask, q, peak, acc, *[piece[slot] for slot in slots])

    def send(x, pairs):
        return lax.ppermute(x, "seq", pairs)

    def along(x, least, step=1, most=outer):
        return send(x, [
            (s, s + step * INNER) for s in range(n_seq)
            if least <= s // INNER < min(most, outer - step)
        ])

    def across(x, least):
        return send(x, [
            (s, s ^ 1) for s in range(n_seq)
            if s // INNER >= least and (least > 0 or s % INNER == 0)
        ])

    piece = {0: own}
    if outer == 4:
        first = [along(own, k, most=k + 1) for k in range(3)]
        piece[4] = send(own, [(s, s ^ 1) for s in range(n_seq) if s % INNER == 0 or s == 1])
        second = [None, along(first[0], 1, most=2), None]
        q_raw, first[0] = lax.optimization_barrier((q_raw, first[0]))
        mask, q = prepare(q_raw)
        first[1], q = lax.optimization_barrier((first[1], q))
        second[2] = along(first[1], 2)
        piece[1] = first[0] + first[1] + first[2]
        piece[5] = across(piece[1], 1)
        peak, acc = start_sums()
        second[1], acc = lax.optimization_barrier((second[1], acc))
        piece[3] = along(second[1], 2)
        piece[4], acc = lax.optimization_barrier((piece[4], acc))
        piece[7] = along(piece[4], 0, step=3, most=1)
        piece[2] = second[1] + second[2]
        piece[6] = across(piece[2], 2)
        acc = add(acc, [1, 4])
        acc = add(acc, [2, 5])
        acc = add(acc, [3])
        last_slots = [6, 7]
    else:
        mask, q = prepare(q_raw)
        peak, acc = start_sums()
        for step in range(outer):
            if step + 1 < outer:
                piece[step + 1] = along(piece[step], step)
            piece[outer + step] = across(piece[step], step)
            if step > 0:
                acc = add(acc, [step, outer + step - 1])
            if step + 1 < outer:
                piece[step + 1], acc = lax.optimization_barrier((piece[step + 1], acc))
        last_slots = [n_seq - 1]

    out, _, _ = pl.pallas_call(
        functools.partial(last_kernel, shape, last_slots, n_lists),
        out_shape=(
            jax.ShapeDtypeStruct((heads * shape.rows, head_dim), jnp.bfloat16),
            peak_shape,
            acc_shape,
        ),
        in_specs=[vmem] * (4 + len(last_slots)) + [anywhere] * n_seq + [hbm] * n_lists,
        out_specs=(vmem, vmem, vmem),
        input_output_aliases={2: 1, 3: 2},
        scratch_shapes=[
            pltpu.VMEM((heads * shape.rows, head_dim), jnp.float32),
            pltpu.VMEM((8, head_dim), jnp.float32),
            pltpu.VMEM((n_seq,) + own.shape, jnp.bfloat16),
            allowed_scratch,
            *list_scratch,
            pltpu.SemaphoreType.DMA((n_lists + n_seq,)),
        ],
        compiler_params=pltpu.CompilerParams(
            vmem_limit_bytes=(16 << 20) + 2 * n_seq * own.size
        ),
        cost_estimate=cost,
    )(
        mask, q, peak, acc, *[piece[slot] for slot in last_slots],
        *[piece[slot] for slot in range(n_seq)], *lists,
    )
    out = out.reshape(tokens_here, group, heads, head_dim)
    return jnp.transpose(out, (0, 2, 1, 3)).reshape(tokens_here, heads, width)


def solution(mesh):
    in_specs = (
        P("seq", "head", None),
        P("seq", "head", None),
        P("seq", "head", None),
        P(),
        P("seq", None, None),
        P("seq", None, None),
        P(),
        P(),
    )
    out_specs = P("seq", "head", None)
    return jax.shard_map(
        functools.partial(per_device, mesh.shape["seq"]),
        mesh=mesh, in_specs=in_specs, out_specs=out_specs, check_vma=False,
    )
```

```python
import functools
import math

import jax
import jax.numpy as jnp
from jax import lax
from jax.experimental import pallas as pl
from jax.experimental.pallas import tpu as pltpu
from jax.sharding import PartitionSpec as P

KV_HEADS = 8
BLOCK = 128
INNER = 2
ROW_TILE = 256
PIECES_AT_ONCE = 2
HIDDEN = -1e30
SAFE_TOTAL = 1e30


class Shape:
    def __init__(self, heads, blocks_here, block_total, group, head_dim, n_slots):
        self.heads = heads
        self.blocks_here = blocks_here
        self.block_total = block_total
        self.group = group
        self.head_dim = head_dim
        self.n_slots = n_slots
        self.outer = n_slots // INNER
        self.rows_unit = BLOCK * group
        self.rows = blocks_here * self.rows_unit
        self.factor = head_dim ** -0.5 * math.log2(math.e)

    def away(self, slot):
        return slot % self.outer


def owner_of(shape, seq_pos, slot):
    crossed = slot >= shape.outer
    line = seq_pos // INNER - jnp.where(crossed, slot - shape.outer, slot)
    place = seq_pos % INNER
    return line * INNER + jnp.where(crossed, 1 - place, place)


def scores(q, keys):
    return lax.dot_general(q, keys, (((1,), (1,)), ((), ())), preferred_element_type=jnp.float32)


def with_ones(vals):
    return jnp.concatenate([vals, jnp.ones_like(vals)], axis=1)


def tiles_of(shape):
    return [(b, r * ROW_TILE) for b in range(shape.blocks_here)
            for r in range(shape.rows_unit // ROW_TILE)]


def mark_allowed(shape, retr_ref, vert_ref, slash_ref, sink_ref, window_ref, allowed_ref):
    first_block = lax.axis_index("seq") * shape.blocks_here
    first_head = lax.axis_index("head") * shape.heads
    n_retr = retr_ref.shape[0]
    for h in range(shape.heads):
        head_id = first_head + h
        is_retr = functools.reduce(
            jnp.logical_or, [retr_ref[i] == head_id for i in range(n_retr)]
        )
        for b in range(shape.blocks_here):
            query_block = first_block + b
            sinks = jnp.where(is_retr, 0, sink_ref[head_id])
            lowest = query_block - jnp.where(is_retr, 1, window_ref[head_id])

            def clear(c, carry):
                read = ((c < sinks) | (c > lowest)) & (c <= query_block)
                allowed_ref[h, b, c] = read.astype(jnp.int32)
                return carry

            lax.fori_loop(0, shape.block_total, clear, 0)
            for j in range(vert_ref.shape[2]):
                c = vert_ref[b, head_id, j]
                allowed_ref[h, b, jnp.where(is_retr, c, query_block)] = 1
            for j in range(slash_ref.shape[2]):
                c = query_block - slash_ref[b, head_id, j]
                allowed_ref[h, b, jnp.where(is_retr, c, query_block)] = 1


def read_lists(list_refs, lists, sems):
    return [pltpu.make_async_copy(list_refs[i], lists[i], sems.at[i]) for i in range(len(lists))]


def prepare_kernel(shape, n_lists, *refs):
    list_refs, q_raw_ref, mask_ref, q_ref = refs[:n_lists], *refs[n_lists:n_lists + 3]
    q_raw, wide, allowed_ref, *lists, sems = refs[n_lists + 3:]
    seq_pos = lax.axis_index("seq")
    copies = read_lists(list_refs, lists, sems)
    for copy in copies:
        copy.start()
    q_copy = pltpu.make_async_copy(q_raw_ref, q_raw, sems.at[n_lists])
    q_copy.start()
    for copy in copies:
        copy.wait()
    mark_allowed(shape, *lists, allowed_ref)

    def fill_masks(slot, carry):
        owner = owner_of(shape, seq_pos, slot)
        there = (owner >= 0) & (owner <= seq_pos)
        base = jnp.where(there, owner, 0) * shape.blocks_here
        for h in range(shape.heads):
            for b in range(shape.blocks_here):
                for j in range(shape.blocks_here):
                    seen = there & (allowed_ref[h, b, base + j] > 0)
                    mask_ref[h, b, pl.ds(slot * shape.blocks_here + j, 1), :] = jnp.full(
                        (1, shape.head_dim), jnp.where(seen, 1.0, 0.0), jnp.float32
                    )
        return carry

    lax.fori_loop(0, shape.n_slots, fill_masks, 0)
    q_copy.wait()
    wide[...] = q_raw[...].astype(jnp.float32)
    for h in range(shape.heads):
        q_ref[h] = wide[pl.ds(h, shape.rows, stride=shape.heads), :].astype(q_ref.dtype)


def own_kernel(shape, mask_ref, q_ref, own_ref, peak_ref, acc_ref):
    for h in range(shape.heads):
        for b, start in tiles_of(shape):
            rows = pl.ds(b * shape.rows_unit + start, ROW_TILE)
            width = (b + 1) * BLOCK
            s = scores(q_ref[h, rows, :], own_ref[h, :width, :]) * shape.factor
            columns = []
            for j in range(b):
                seen = mask_ref[h, b, pl.ds(j, 1), :]
                columns.append(jnp.where(seen > 0.0, s[:, j * BLOCK:(j + 1) * BLOCK], HIDDEN))
            diagonal = s[:, b * BLOCK:]
            row = start + lax.broadcasted_iota(jnp.int32, diagonal.shape, 0)
            column = lax.broadcasted_iota(jnp.int32, diagonal.shape, 1)
            columns.append(jnp.where(column * shape.group <= row, diagonal, HIDDEN))
            s = jnp.concatenate(columns, axis=1)
            m = jnp.max(s, axis=1, keepdims=True)
            peak_ref[h, rows, :] = jnp.broadcast_to(m, (ROW_TILE, BLOCK))
            p = jnp.exp2(s - m).astype(jnp.bfloat16)
            vals = with_ones(own_ref[shape.heads + h, :width, :])
            acc_ref[h, rows, :] = jnp.dot(p, vals, preferred_element_type=jnp.float32)


def mixed_tiles(shape, slots, h, mask_ref, q_ref, peak_ref, piece_refs):
    parts = []
    for at in range(0, len(slots), PIECES_AT_ONCE):
        some_slots = slots[at:at + PIECES_AT_ONCE]
        some_refs = piece_refs[at:at + PIECES_AT_ONCE]
        vals = jnp.concatenate([ref[shape.heads + h] for ref in some_refs], axis=0)
        seen_vals = []
        for b in range(shape.blocks_here):
            masks = jnp.concatenate(
                [
                    jnp.broadcast_to(
                        mask_ref[h, b, pl.ds(slot * shape.blocks_here + j, 1), :],
                        (BLOCK, shape.head_dim),
                    )
                    for slot in some_slots for j in range(shape.blocks_here)
                ],
                axis=0,
            ).astype(jnp.bfloat16)
            seen_vals.append(jnp.concatenate([vals * masks, masks], axis=1))
        parts.append((jnp.concatenate([ref[h] for ref in some_refs], axis=0), seen_vals))
    for b, start in tiles_of(shape):
        rows = pl.ds(b * shape.rows_unit + start, ROW_TILE)
        q = q_ref[h, rows, :]
        m = peak_ref[h, rows, :]
        mixed = None
        for keys, seen_vals in parts:
            s = scores(q, keys) * shape.factor
            p = jnp.exp2(s - jnp.concatenate([m] * (s.shape[1] // m.shape[1]), axis=1))
            part = jnp.dot(
                p.astype(jnp.bfloat16), seen_vals[b], preferred_element_type=jnp.float32
            )
            mixed = part if mixed is None else mixed + part
        yield rows, mixed


def middle_kernel(shape, slots, mask_ref, q_ref, peak_ref, acc_in, *refs):
    del acc_in
    piece_refs, acc_ref = refs[:-1], refs[-1]
    nearest = min(shape.away(slot) for slot in slots)

    @pl.when(lax.axis_index("seq") // INNER >= nearest)
    def _():
        for h in range(shape.heads):
            for rows, mixed in mixed_tiles(
                shape, slots, h, mask_ref, q_ref, peak_ref, piece_refs
            ):
                acc_ref[h, rows, :] += mixed


def last_kernel(shape, slots, n_lists, mask_ref, q_ref, peak_in, acc_in, *refs):
    del peak_in, acc_in
    heads, head_dim = shape.heads, shape.head_dim
    n, n_all = len(slots), shape.n_slots
    piece_refs, all_refs, list_refs = refs[:n], refs[n:n + n_all], refs[n + n_all:][:n_lists]
    out_ref, peak_ref, acc_ref, *scratch = refs[n + n_all + n_lists:]
    out_rows, worst, kv, allowed_ref, *lists, sems = scratch
    seq_pos = lax.axis_index("seq")
    first_block = seq_pos * shape.blocks_here
    line = seq_pos // INNER

    def finish(h, rows, sums):
        total = sums[:, head_dim:]
        out_rows[pl.ds(rows.start * heads + h, ROW_TILE, stride=heads), :] = (
            sums[:, :head_dim] / total
        )
        bad = jnp.where(total < SAFE_TOTAL, 0.0, 1.0)
        worst[...] = jnp.maximum(
            worst[...], jnp.max(bad.reshape(ROW_TILE // 8, 8, head_dim), axis=0)
        )

    def finish_all():
        for h in range(heads):
            for b, start in tiles_of(shape):
                rows = pl.ds(b * shape.rows_unit + start, ROW_TILE)
                finish(h, rows, acc_ref[h, rows, :])

    worst[...] = jnp.zeros_like(worst)
    steps = sorted({shape.away(slot) for slot in slots}) + [shape.outer]
    for least, below in zip([0] + steps, steps):
        here = [i for i, slot in enumerate(slots) if shape.away(slot) <= least]

        @pl.when((line >= least) & (line < below))
        def _(here=here):
            if not here:
                finish_all()
                return
            for h in range(heads):
                for rows, mixed in mixed_tiles(
                    shape, [slots[i] for i in here], h, mask_ref, q_ref, peak_ref,
                    [piece_refs[i] for i in here],
                ):
                    finish(h, rows, acc_ref[h, rows, :] + mixed)

    out_ref[...] = out_rows[...].astype(out_ref.dtype)

    @pl.when(jnp.max(worst[...]) > 0.0)
    def _():
        copies = read_lists(list_refs, lists, sems) + [
            pltpu.make_async_copy(all_refs[i], kv.at[i], sems.at[n_lists + i])
            for i in range(n_all)
        ]
        for copy in copies:
            copy.start()
        for copy in copies:
            copy.wait()
        mark_allowed(shape, *lists, allowed_ref)

        def every_tile(step):
            def slot_step(i, carry):
                owner = owner_of(shape, seq_pos, i)

                @pl.when((owner >= 0) & (owner <= seq_pos))
                def _():
                    for h in range(heads):
                        for b, start in tiles_of(shape):
                            rows = pl.ds(b * shape.rows_unit + start, ROW_TILE)
                            s = scores(q_ref[h, rows, :], kv[i, h]) * shape.factor
                            columns = []
                            for j in range(shape.blocks_here):
                                block = owner * shape.blocks_here + j
                                part = s[:, j * BLOCK:(j + 1) * BLOCK]
                                row = start + lax.broadcasted_iota(jnp.int32, part.shape, 0)
                                column = lax.broadcasted_iota(jnp.int32, part.shape, 1)
                                ahead = (first_block + b - block) * BLOCK
                                part = jnp.where(
                                    (column - ahead) * shape.group <= row, part, HIDDEN
                                )
                                seen = allowed_ref[h, b, block] > 0
                                columns.append(part + jnp.where(seen, 0.0, HIDDEN))
                            step(h, rows, jnp.concatenate(columns, axis=1), i)

                return carry

            lax.fori_loop(0, n_all, slot_step, 0)

        def widen(h, rows, s, i):
            m = jnp.max(s, axis=1, keepdims=True)
            peak_ref[h, rows, :] = jnp.maximum(peak_ref[h, rows, :], m)

        def collect(h, rows, s, i):
            m = peak_ref[h, rows, :]
            p = jnp.exp2(s - jnp.concatenate([m] * shape.blocks_here, axis=1))
            acc_ref[h, rows, :] += jnp.dot(
                p.astype(jnp.bfloat16), with_ones(kv[i, heads + h]),
                preferred_element_type=jnp.float32,
            )

        every_tile(widen)
        acc_ref[...] = jnp.zeros_like(acc_ref)
        every_tile(collect)
        finish_all()
        out_ref[...] = out_rows[...].astype(out_ref.dtype)


def per_device(
    n_seq, queries, keys, values, retrieval_ids, vertical_blocks, slash_offsets, sink_blocks,
    window_blocks,
):
    tokens_here, heads, width = queries.shape
    head_dim = keys.shape[2]
    group = width // head_dim
    blocks_here = tokens_here // BLOCK
    shape = Shape(heads, blocks_here, n_seq * blocks_here, group, head_dim, n_seq)
    outer = shape.outer

    vmem = pl.BlockSpec(memory_space=pltpu.VMEM)
    hbm = pl.BlockSpec(memory_space=pltpu.HBM)
    anywhere = pl.BlockSpec(memory_space=pl.ANY)
    mask_shape = jax.ShapeDtypeStruct(
        (heads, blocks_here, shape.block_total, head_dim), jnp.float32
    )
    q_shape = jax.ShapeDtypeStruct((heads, shape.rows, head_dim), jnp.bfloat16)
    peak_shape = jax.ShapeDtypeStruct((heads, shape.rows, head_dim), jnp.float32)
    acc_shape = jax.ShapeDtypeStruct((heads, shape.rows, 2 * head_dim), jnp.float32)
    allowed_scratch = pltpu.SMEM((heads, blocks_here, shape.block_total), jnp.int32)
    params = pltpu.CompilerParams(vmem_limit_bytes=16 << 20)
    cost = pl.CostEstimate(flops=1 << 20, transcendentals=0, bytes_accessed=1 << 10)

    own = jnp.concatenate(
        [jnp.transpose(keys, (1, 0, 2)), jnp.transpose(values, (1, 0, 2))], axis=0
    )
    q_raw = queries.reshape(tokens_here, heads, group, head_dim)
    q_raw = jnp.transpose(q_raw, (0, 2, 1, 3)).reshape(heads * shape.rows, head_dim)
    q_raw = pltpu.with_memory_space_constraint(q_raw, pltpu.HBM)
    lists = tuple(
        pltpu.with_memory_space_constraint(x, pltpu.HBM)
        for x in (retrieval_ids, vertical_blocks, slash_offsets, sink_blocks, window_blocks)
    )
    n_lists = len(lists)
    list_scratch = [pltpu.SMEM(x.shape, jnp.int32) for x in lists]

    def prepare(q_raw):
        return pl.pallas_call(
            functools.partial(prepare_kernel, shape, n_lists),
            out_shape=(mask_shape, q_shape),
            in_specs=[hbm] * (n_lists + 1),
            out_specs=(vmem, vmem),
            scratch_shapes=[
                pltpu.VMEM((heads * shape.rows, head_dim), jnp.bfloat16),
                pltpu.VMEM((heads * shape.rows, head_dim), jnp.float32),
                allowed_scratch,
                *list_scratch,
                pltpu.SemaphoreType.DMA((n_lists + 1,)),
            ],
            compiler_params=params,
            cost_estimate=cost,
        )(*lists, q_raw)

    def start_sums():
        return pl.pallas_call(
            functools.partial(own_kernel, shape),
            out_shape=(peak_shape, acc_shape),
            in_specs=[vmem] * 3,
            out_specs=(vmem, vmem),
            compiler_params=params,
            cost_estimate=cost,
        )(mask, q, own)

    def add(acc, slots):
        return pl.pallas_call(
            functools.partial(middle_kernel, shape, slots),
            out_shape=acc_shape,
            in_specs=[vmem] * (4 + len(slots)),
            out_specs=vmem,
            input_output_aliases={3: 0},
            compiler_params=params,
            cost_estimate=cost,
        )(mask, q, peak, acc, *[piece[slot] for slot in slots])

    def send(x, pairs):
        return lax.ppermute(x, "seq", pairs)

    def along(x, least, step=1, most=outer):
        return send(x, [
            (s, s + step * INNER) for s in range(n_seq)
            if least <= s // INNER < min(most, outer - step)
        ])

    def across(x, least):
        return send(x, [
            (s, s ^ 1) for s in range(n_seq)
            if s // INNER >= least and (least > 0 or s % INNER == 0)
        ])

    piece = {0: own}
    if outer == 4:
        first = [along(own, k, most=k + 1) for k in range(3)]
        piece[4] = send(own, [(s, s ^ 1) for s in range(n_seq) if s % INNER == 0 or s == 1])
        second = [None, along(first[0], 1, most=2), None]
        second[2] = along(first[1], 2)
        q_raw, first[0] = lax.optimization_barrier((q_raw, first[0]))
        mask, q = prepare(q_raw)
        piece[1] = first[0] + first[1] + first[2]
        piece[1], q = lax.optimization_barrier((piece[1], q))
        piece[5] = across(piece[1], 1)
        piece[3] = along(second[1], 2)
        piece[7] = along(piece[4], 0, step=3, most=1)
        q, second[1], piece[4] = lax.optimization_barrier((q, second[1], piece[4]))
        peak, acc = start_sums()
        piece[2] = second[1] + second[2]
        piece[2], acc = lax.optimization_barrier((piece[2], acc))
        piece[6] = across(piece[2], 2)
        acc = add(acc, [1, 4])
        acc = add(acc, [2, 5])
        acc = add(acc, [7])
        last_slots = [3, 6]
    else:
        mask, q = prepare(q_raw)
        peak, acc = start_sums()
        for step in range(outer):
            if step + 1 < outer:
                piece[step + 1] = along(piece[step], step)
            piece[outer + step] = across(piece[step], step)
            if step > 0:
                acc = add(acc, [step, outer + step - 1])
            if step + 1 < outer:
                piece[step + 1], acc = lax.optimization_barrier((piece[step + 1], acc))
        last_slots = [n_seq - 1]

    out, _, _ = pl.pallas_call(
        functools.partial(last_kernel, shape, last_slots, n_lists),
        out_shape=(
            jax.ShapeDtypeStruct((heads * shape.rows, head_dim), jnp.bfloat16),
            peak_shape,
            acc_shape,
        ),
        in_specs=[vmem] * (4 + len(last_slots)) + [anywhere] * n_seq + [hbm] * n_lists,
        out_specs=(vmem, vmem, vmem),
        input_output_aliases={2: 1, 3: 2},
        scratch_shapes=[
            pltpu.VMEM((heads * shape.rows, head_dim), jnp.float32),
            pltpu.VMEM((8, head_dim), jnp.float32),
            pltpu.VMEM((n_seq,) + own.shape, jnp.bfloat16),
            allowed_scratch,
            *list_scratch,
            pltpu.SemaphoreType.DMA((n_lists + n_seq,)),
        ],
        compiler_params=pltpu.CompilerParams(
            vmem_limit_bytes=(16 << 20) + 2 * n_seq * own.size
        ),
        cost_estimate=cost,
    )(
        mask, q, peak, acc, *[piece[slot] for slot in last_slots],
        *[piece[slot] for slot in range(n_seq)], *lists,
    )
    out = out.reshape(tokens_here, group, heads, head_dim)
    return jnp.transpose(out, (0, 2, 1, 3)).reshape(tokens_here, heads, width)


def solution(mesh):
    in_specs = (
        P("seq", "head", None),
        P("seq", "head", None),
        P("seq", "head", None),
        P(),
        P("seq", None, None),
        P("seq", None, None),
        P(),
        P(),
    )
    out_specs = P("seq", "head", None)
    return jax.shard_map(
        functools.partial(per_device, mesh.shape["seq"]),
        mesh=mesh, in_specs=in_specs, out_specs=out_specs, check_vma=False,
    )
```

```python
import functools
import math

import jax
import jax.numpy as jnp
from jax import lax
from jax.experimental import pallas as pl
from jax.experimental.pallas import tpu as pltpu
from jax.sharding import PartitionSpec as P

KV_HEADS = 8
BLOCK = 128
INNER = 2
ROW_TILE = 256
PIECES_AT_ONCE = 2
HIDDEN = -1e30
SAFE_TOTAL = 1e30


class Shape:
    def __init__(self, heads, blocks_here, block_total, group, head_dim, n_slots):
        self.heads = heads
        self.blocks_here = blocks_here
        self.block_total = block_total
        self.group = group
        self.head_dim = head_dim
        self.n_slots = n_slots
        self.outer = n_slots // INNER
        self.rows_unit = BLOCK * group
        self.rows = blocks_here * self.rows_unit
        self.factor = head_dim ** -0.5 * math.log2(math.e)

    def away(self, slot):
        return slot % self.outer


def owner_of(shape, seq_pos, slot):
    crossed = slot >= shape.outer
    line = seq_pos // INNER - jnp.where(crossed, slot - shape.outer, slot)
    place = seq_pos % INNER
    return line * INNER + jnp.where(crossed, 1 - place, place)


def scores(q, keys):
    return lax.dot_general(q, keys, (((1,), (1,)), ((), ())), preferred_element_type=jnp.float32)


def with_ones(vals):
    return jnp.concatenate([vals, jnp.ones_like(vals)], axis=1)


def tiles_of(shape):
    return [(b, r * ROW_TILE) for b in range(shape.blocks_here)
            for r in range(shape.rows_unit // ROW_TILE)]


def mark_allowed(shape, retr_ref, vert_ref, slash_ref, sink_ref, window_ref, allowed_ref):
    first_block = lax.axis_index("seq") * shape.blocks_here
    first_head = lax.axis_index("head") * shape.heads
    n_retr = retr_ref.shape[0]
    for h in range(shape.heads):
        head_id = first_head + h
        is_retr = functools.reduce(
            jnp.logical_or, [retr_ref[i] == head_id for i in range(n_retr)]
        )
        for b in range(shape.blocks_here):
            query_block = first_block + b
            sinks = jnp.where(is_retr, 0, sink_ref[head_id])
            lowest = query_block - jnp.where(is_retr, 1, window_ref[head_id])

            def clear(c, carry):
                read = ((c < sinks) | (c > lowest)) & (c <= query_block)
                allowed_ref[h, b, c] = read.astype(jnp.int32)
                return carry

            lax.fori_loop(0, shape.block_total, clear, 0)
            for j in range(vert_ref.shape[2]):
                c = vert_ref[b, head_id, j]
                allowed_ref[h, b, jnp.where(is_retr, c, query_block)] = 1
            for j in range(slash_ref.shape[2]):
                c = query_block - slash_ref[b, head_id, j]
                allowed_ref[h, b, jnp.where(is_retr, c, query_block)] = 1


def read_lists(list_refs, lists, sems):
    return [pltpu.make_async_copy(list_refs[i], lists[i], sems.at[i]) for i in range(len(lists))]


def prepare_kernel(shape, n_lists, *refs):
    list_refs, q_raw_ref, mask_ref, q_ref = refs[:n_lists], *refs[n_lists:n_lists + 3]
    q_raw, wide, allowed_ref, *lists, sems = refs[n_lists + 3:]
    seq_pos = lax.axis_index("seq")
    copies = read_lists(list_refs, lists, sems)
    for copy in copies:
        copy.start()
    q_copy = pltpu.make_async_copy(q_raw_ref, q_raw, sems.at[n_lists])
    q_copy.start()
    for copy in copies:
        copy.wait()
    mark_allowed(shape, *lists, allowed_ref)

    def fill_masks(slot, carry):
        owner = owner_of(shape, seq_pos, slot)
        there = (owner >= 0) & (owner <= seq_pos)
        base = jnp.where(there, owner, 0) * shape.blocks_here
        for h in range(shape.heads):
            for b in range(shape.blocks_here):
                for j in range(shape.blocks_here):
                    seen = there & (allowed_ref[h, b, base + j] > 0)
                    mask_ref[h, b, pl.ds(slot * shape.blocks_here + j, 1), :] = jnp.full(
                        (1, shape.head_dim), jnp.where(seen, 1.0, 0.0), jnp.float32
                    )
        return carry

    lax.fori_loop(0, shape.n_slots, fill_masks, 0)
    q_copy.wait()
    wide[...] = q_raw[...].astype(jnp.float32)
    for h in range(shape.heads):
        q_ref[h] = wide[pl.ds(h, shape.rows, stride=shape.heads), :].astype(q_ref.dtype)


def own_kernel(shape, mask_ref, q_ref, own_ref, peak_ref, acc_ref):
    for h in range(shape.heads):
        for b, start in tiles_of(shape):
            rows = pl.ds(b * shape.rows_unit + start, ROW_TILE)
            width = (b + 1) * BLOCK
            s = scores(q_ref[h, rows, :], own_ref[h, :width, :]) * shape.factor
            columns = []
            for j in range(b):
                seen = mask_ref[h, b, pl.ds(j, 1), :]
                columns.append(jnp.where(seen > 0.0, s[:, j * BLOCK:(j + 1) * BLOCK], HIDDEN))
            diagonal = s[:, b * BLOCK:]
            row = start + lax.broadcasted_iota(jnp.int32, diagonal.shape, 0)
            column = lax.broadcasted_iota(jnp.int32, diagonal.shape, 1)
            columns.append(jnp.where(column * shape.group <= row, diagonal, HIDDEN))
            s = jnp.concatenate(columns, axis=1)
            m = jnp.max(s, axis=1, keepdims=True)
            peak_ref[h, rows, :] = jnp.broadcast_to(m, (ROW_TILE, BLOCK))
            p = jnp.exp2(s - m).astype(jnp.bfloat16)
            vals = with_ones(own_ref[shape.heads + h, :width, :])
            acc_ref[h, rows, :] = jnp.dot(p, vals, preferred_element_type=jnp.float32)


def parts_of(shape, slots, h, mask_ref, piece_refs):
    parts = []
    for at in range(0, len(slots), PIECES_AT_ONCE):
        some_slots = slots[at:at + PIECES_AT_ONCE]
        some_refs = piece_refs[at:at + PIECES_AT_ONCE]
        vals = jnp.concatenate([ref[shape.heads + h] for ref in some_refs], axis=0)
        seen_vals = []
        for b in range(shape.blocks_here):
            masks = jnp.concatenate(
                [
                    jnp.broadcast_to(
                        mask_ref[h, b, pl.ds(slot * shape.blocks_here + j, 1), :],
                        (BLOCK, shape.head_dim),
                    )
                    for slot in some_slots for j in range(shape.blocks_here)
                ],
                axis=0,
            ).astype(jnp.bfloat16)
            seen_vals.append(jnp.concatenate([vals * masks, masks], axis=1))
        parts.append((jnp.concatenate([ref[h] for ref in some_refs], axis=0), seen_vals))
    return parts


def mixed_tile(shape, parts, h, b, rows, q_ref, peak_ref):
    q = q_ref[h, rows, :]
    m = peak_ref[h, rows, :]
    mixed = None
    for keys, seen_vals in parts:
        s = scores(q, keys) * shape.factor
        p = jnp.exp2(s - jnp.concatenate([m] * (s.shape[1] // m.shape[1]), axis=1))
        part = jnp.dot(p.astype(jnp.bfloat16), seen_vals[b], preferred_element_type=jnp.float32)
        mixed = part if mixed is None else mixed + part
    return mixed


def for_each_form(shape, slots, work):
    line = lax.axis_index("seq") // INNER
    steps = sorted({0} | {shape.away(slot) for slot in slots}) + [shape.outer]
    for least, below in zip(steps, steps[1:]):
        here = [i for i, slot in enumerate(slots) if shape.away(slot) <= least]
        pl.when((line >= least) & (line < below))(functools.partial(work, here))


def middle_kernel(shape, slots, mask_ref, q_ref, peak_ref, acc_in, *refs):
    del acc_in
    piece_refs, acc_ref = refs[:-1], refs[-1]

    def work(here):
        for h in range(shape.heads if here else 0):
            parts = parts_of(
                shape, [slots[i] for i in here], h, mask_ref, [piece_refs[i] for i in here]
            )
            for b, start in tiles_of(shape):
                rows = pl.ds(b * shape.rows_unit + start, ROW_TILE)
                acc_ref[h, rows, :] += mixed_tile(shape, parts, h, b, rows, q_ref, peak_ref)

    for_each_form(shape, slots, work)


def last_kernel(shape, slots, n_lists, mask_ref, q_ref, peak_in, acc_in, *refs):
    del peak_in, acc_in
    heads, head_dim = shape.heads, shape.head_dim
    n, n_all = len(slots), shape.n_slots
    piece_refs, all_refs, list_refs = refs[:n], refs[n:n + n_all], refs[n + n_all:][:n_lists]
    out_ref, peak_ref, acc_ref, *scratch = refs[n + n_all + n_lists:]
    out_rows, out_tiles, worst, kv, allowed_ref, *lists, sems, out_sems = scratch
    seq_pos = lax.axis_index("seq")
    first_block = seq_pos * shape.blocks_here

    def finish(h, at, sums):
        total = sums[:, head_dim:]
        inverse = pl.reciprocal(total, approx=True)
        inverse = inverse * (2.0 - total * inverse)
        out_rows[at % 2, pl.ds(h, ROW_TILE, stride=heads), :] = sums[:, :head_dim] * inverse
        bad = jnp.where(total < SAFE_TOTAL, 0.0, 1.0)
        worst[...] = jnp.maximum(
            worst[...], jnp.max(bad.reshape(ROW_TILE // 8, 8, head_dim), axis=0)
        )

    def finish_all(parts):
        copies = []
        for at, (b, start) in enumerate(tiles_of(shape)):
            rows = pl.ds(b * shape.rows_unit + start, ROW_TILE)
            for h in range(heads):
                sums = acc_ref[h, rows, :]
                if parts:
                    sums = sums + mixed_tile(shape, parts[h], h, b, rows, q_ref, peak_ref)
                finish(h, at, sums)
            out_tiles[at] = out_rows[at % 2].astype(out_tiles.dtype)
            copies.append(
                pltpu.make_async_copy(
                    out_tiles.at[at],
                    out_ref.at[pl.ds(rows.start * heads, ROW_TILE * heads), :],
                    out_sems.at[at],
                )
            )
            copies[-1].start()
        for copy in copies:
            copy.wait()

    worst[...] = jnp.zeros_like(worst)
    for_each_form(
        shape, slots,
        lambda here: finish_all([
            parts_of(shape, [slots[i] for i in here], h, mask_ref, [piece_refs[i] for i in here])
            for h in range(heads)
        ] if here else []),
    )

    @pl.when(jnp.max(worst[...]) > 0.0)
    def _():
        copies = read_lists(list_refs, lists, sems) + [
            pltpu.make_async_copy(all_refs[i], kv.at[i], sems.at[n_lists + i])
            for i in range(n_all)
        ]
        for copy in copies:
            copy.start()
        for copy in copies:
            copy.wait()
        mark_allowed(shape, *lists, allowed_ref)

        def every_tile(step):
            def slot_step(i, carry):
                owner = owner_of(shape, seq_pos, i)

                @pl.when((owner >= 0) & (owner <= seq_pos))
                def _():
                    for h in range(heads):
                        for b, start in tiles_of(shape):
                            rows = pl.ds(b * shape.rows_unit + start, ROW_TILE)
                            s = scores(q_ref[h, rows, :], kv[i, h]) * shape.factor
                            columns = []
                            for j in range(shape.blocks_here):
                                block = owner * shape.blocks_here + j
                                part = s[:, j * BLOCK:(j + 1) * BLOCK]
                                row = start + lax.broadcasted_iota(jnp.int32, part.shape, 0)
                                column = lax.broadcasted_iota(jnp.int32, part.shape, 1)
                                ahead = (first_block + b - block) * BLOCK
                                part = jnp.where(
                                    (column - ahead) * shape.group <= row, part, HIDDEN
                                )
                                seen = allowed_ref[h, b, block] > 0
                                columns.append(part + jnp.where(seen, 0.0, HIDDEN))
                            step(h, rows, jnp.concatenate(columns, axis=1), i)

                return carry

            lax.fori_loop(0, n_all, slot_step, 0)

        def widen(h, rows, s, i):
            m = jnp.max(s, axis=1, keepdims=True)
            peak_ref[h, rows, :] = jnp.maximum(peak_ref[h, rows, :], m)

        def collect(h, rows, s, i):
            m = peak_ref[h, rows, :]
            p = jnp.exp2(s - jnp.concatenate([m] * shape.blocks_here, axis=1))
            acc_ref[h, rows, :] += jnp.dot(
                p.astype(jnp.bfloat16), with_ones(kv[i, heads + h]),
                preferred_element_type=jnp.float32,
            )

        every_tile(widen)
        acc_ref[...] = jnp.zeros_like(acc_ref)
        every_tile(collect)
        finish_all([])


def per_device(
    n_seq, queries, keys, values, retrieval_ids, vertical_blocks, slash_offsets, sink_blocks,
    window_blocks,
):
    tokens_here, heads, width = queries.shape
    head_dim = keys.shape[2]
    group = width // head_dim
    blocks_here = tokens_here // BLOCK
    shape = Shape(heads, blocks_here, n_seq * blocks_here, group, head_dim, n_seq)
    outer = shape.outer

    vmem = pl.BlockSpec(memory_space=pltpu.VMEM)
    hbm = pl.BlockSpec(memory_space=pltpu.HBM)
    anywhere = pl.BlockSpec(memory_space=pl.ANY)
    mask_shape = jax.ShapeDtypeStruct(
        (heads, blocks_here, shape.block_total, head_dim), jnp.float32
    )
    q_shape = jax.ShapeDtypeStruct((heads, shape.rows, head_dim), jnp.bfloat16)
    peak_shape = jax.ShapeDtypeStruct((heads, shape.rows, head_dim), jnp.float32)
    acc_shape = jax.ShapeDtypeStruct((heads, shape.rows, 2 * head_dim), jnp.float32)
    allowed_scratch = pltpu.SMEM((heads, blocks_here, shape.block_total), jnp.int32)
    params = pltpu.CompilerParams(vmem_limit_bytes=16 << 20)
    cost = pl.CostEstimate(flops=1 << 20, transcendentals=0, bytes_accessed=1 << 10)

    own = jnp.concatenate(
        [jnp.transpose(keys, (1, 0, 2)), jnp.transpose(values, (1, 0, 2))], axis=0
    )
    q_raw = queries.reshape(tokens_here, heads, group, head_dim)
    q_raw = jnp.transpose(q_raw, (0, 2, 1, 3)).reshape(heads * shape.rows, head_dim)
    q_raw = pltpu.with_memory_space_constraint(q_raw, pltpu.HBM)
    lists = tuple(
        pltpu.with_memory_space_constraint(x, pltpu.HBM)
        for x in (retrieval_ids, vertical_blocks, slash_offsets, sink_blocks, window_blocks)
    )
    n_lists = len(lists)
    list_scratch = [pltpu.SMEM(x.shape, jnp.int32) for x in lists]

    def prepare(q_raw):
        return pl.pallas_call(
            functools.partial(prepare_kernel, shape, n_lists),
            out_shape=(mask_shape, q_shape),
            in_specs=[hbm] * (n_lists + 1),
            out_specs=(vmem, vmem),
            scratch_shapes=[
                pltpu.VMEM((heads * shape.rows, head_dim), jnp.bfloat16),
                pltpu.VMEM((heads * shape.rows, head_dim), jnp.float32),
                allowed_scratch,
                *list_scratch,
                pltpu.SemaphoreType.DMA((n_lists + 1,)),
            ],
            compiler_params=params,
            cost_estimate=cost,
        )(*lists, q_raw)

    def start_sums():
        return pl.pallas_call(
            functools.partial(own_kernel, shape),
            out_shape=(peak_shape, acc_shape),
            in_specs=[vmem] * 3,
            out_specs=(vmem, vmem),
            compiler_params=params,
            cost_estimate=cost,
        )(mask, q, own)

    def add(acc, slots):
        return pl.pallas_call(
            functools.partial(middle_kernel, shape, slots),
            out_shape=acc_shape,
            in_specs=[vmem] * (4 + len(slots)),
            out_specs=vmem,
            input_output_aliases={3: 0},
            compiler_params=params,
            cost_estimate=cost,
        )(mask, q, peak, acc, *[piece[slot] for slot in slots])

    def send(x, pairs):
        return lax.ppermute(x, "seq", pairs)

    def along(x, least, step=1, most=outer):
        return send(x, [
            (s, s + step * INNER) for s in range(n_seq)
            if least <= s // INNER < min(most, outer - step)
        ])

    def across(x, least):
        return send(x, [
            (s, s ^ 1) for s in range(n_seq)
            if s // INNER >= least and (least > 0 or s % INNER == 0)
        ])

    piece = {0: own}
    if outer == 4:
        first = [along(own, k, most=k + 1) for k in range(3)]
        piece[4] = send(own, [(s, s ^ 1) for s in range(n_seq) if s % INNER == 0 or s == 1])
        second = [None, along(first[0], 1, most=2), along(first[1], 2)]
        q_raw, first[0] = lax.optimization_barrier((q_raw, first[0]))
        mask, q = prepare(q_raw)
        piece[1] = first[0] + first[1] + first[2]
        piece[1], q = lax.optimization_barrier((piece[1], q))
        piece[4], q = lax.optimization_barrier((piece[4], q))
        piece[7] = along(piece[4], 0, step=3, most=1)
        peak, acc = start_sums()
        piece[1], _, acc = lax.optimization_barrier((piece[1], second[1], acc))
        piece[5] = across(piece[1], 1)
        piece[3] = along(second[1], 2)
        piece[2] = second[1] + second[2]
        piece[2], acc = lax.optimization_barrier((piece[2], acc))
        piece[6] = across(piece[2], 2)
        acc = add(acc, [1, 4])
        acc = add(acc, [2, 7])
        acc = add(acc, [5])
        last_slots = [3, 6]
    else:
        mask, q = prepare(q_raw)
        peak, acc = start_sums()
        for step in range(outer):
            if step + 1 < outer:
                piece[step + 1] = along(piece[step], step)
            piece[outer + step] = across(piece[step], step)
            if step > 0:
                acc = add(acc, [step, outer + step - 1])
            if step + 1 < outer:
                piece[step + 1], acc = lax.optimization_barrier((piece[step + 1], acc))
        last_slots = [n_seq - 1]

    out, _, _ = pl.pallas_call(
        functools.partial(last_kernel, shape, last_slots, n_lists),
        out_shape=(
            jax.ShapeDtypeStruct((heads * shape.rows, head_dim), jnp.bfloat16),
            peak_shape,
            acc_shape,
        ),
        in_specs=[vmem] * (4 + len(last_slots)) + [anywhere] * n_seq + [hbm] * n_lists,
        out_specs=(hbm, vmem, vmem),
        input_output_aliases={2: 1, 3: 2},
        scratch_shapes=[
            pltpu.VMEM((2, heads * ROW_TILE, head_dim), jnp.float32),
            pltpu.VMEM((shape.rows // ROW_TILE, heads * ROW_TILE, head_dim), jnp.bfloat16),
            pltpu.VMEM((8, head_dim), jnp.float32),
            pltpu.VMEM((n_seq,) + own.shape, jnp.bfloat16),
            allowed_scratch,
            *list_scratch,
            pltpu.SemaphoreType.DMA((n_lists + n_seq,)),
            pltpu.SemaphoreType.DMA((shape.rows // ROW_TILE,)),
        ],
        compiler_params=pltpu.CompilerParams(
            vmem_limit_bytes=(16 << 20) + 2 * n_seq * own.size
        ),
        cost_estimate=cost,
    )(
        mask, q, peak, acc, *[piece[slot] for slot in last_slots],
        *[piece[slot] for slot in range(n_seq)], *lists,
    )
    out = out.reshape(tokens_here, group, heads, head_dim)
    return jnp.transpose(out, (0, 2, 1, 3)).reshape(tokens_here, heads, width)


def solution(mesh):
    in_specs = (
        P("seq", "head", None),
        P("seq", "head", None),
        P("seq", "head", None),
        P(),
        P("seq", None, None),
        P("seq", None, None),
        P(),
        P(),
    )
    out_specs = P("seq", "head", None)
    return jax.shard_map(
        functools.partial(per_device, mesh.shape["seq"]),
        mesh=mesh, in_specs=in_specs, out_specs=out_specs, check_vma=False,
    )
```

```python
import functools
import math

import jax
import jax.numpy as jnp
from jax import lax
from jax.experimental import pallas as pl
from jax.experimental.pallas import tpu as pltpu
from jax.sharding import PartitionSpec as P

KV_HEADS = 8
BLOCK = 128
INNER = 2
ROW_TILE = 256
PIECES_AT_ONCE = 2
HIDDEN = -1e30
SAFE_TOTAL = 1e30


class Shape:
    def __init__(self, heads, blocks_here, block_total, group, head_dim, n_slots):
        self.heads = heads
        self.blocks_here = blocks_here
        self.block_total = block_total
        self.group = group
        self.head_dim = head_dim
        self.n_slots = n_slots
        self.outer = n_slots // INNER
        self.rows_unit = BLOCK * group
        self.rows = blocks_here * self.rows_unit
        self.factor = head_dim ** -0.5 * math.log2(math.e)

    def away(self, slot):
        return slot % self.outer


def owner_of(shape, seq_pos, slot):
    crossed = slot >= shape.outer
    line = seq_pos // INNER - jnp.where(crossed, slot - shape.outer, slot)
    place = seq_pos % INNER
    return line * INNER + jnp.where(crossed, 1 - place, place)


def scores(q, keys):
    return lax.dot_general(q, keys, (((1,), (1,)), ((), ())), preferred_element_type=jnp.float32)


def with_ones(vals):
    return jnp.concatenate([vals, jnp.ones_like(vals)], axis=1)


def tiles_of(shape):
    return [(b, r * ROW_TILE) for b in range(shape.blocks_here)
            for r in range(shape.rows_unit // ROW_TILE)]


def mark_allowed(shape, retr_ref, vert_ref, slash_ref, sink_ref, window_ref, allowed_ref):
    first_block = lax.axis_index("seq") * shape.blocks_here
    first_head = lax.axis_index("head") * shape.heads
    n_retr = retr_ref.shape[0]
    for h in range(shape.heads):
        head_id = first_head + h
        is_retr = functools.reduce(
            jnp.logical_or, [retr_ref[i] == head_id for i in range(n_retr)]
        )
        for b in range(shape.blocks_here):
            query_block = first_block + b
            sinks = jnp.where(is_retr, 0, sink_ref[head_id])
            lowest = query_block - jnp.where(is_retr, 1, window_ref[head_id])

            def clear(c, carry):
                read = ((c < sinks) | (c > lowest)) & (c <= query_block)
                allowed_ref[h, b, c] = read.astype(jnp.int32)
                return carry

            lax.fori_loop(0, shape.block_total, clear, 0)
            for j in range(vert_ref.shape[2]):
                c = vert_ref[b, head_id, j]
                allowed_ref[h, b, jnp.where(is_retr, c, query_block)] = 1
            for j in range(slash_ref.shape[2]):
                c = query_block - slash_ref[b, head_id, j]
                allowed_ref[h, b, jnp.where(is_retr, c, query_block)] = 1


def read_lists(list_refs, lists, sems):
    return [pltpu.make_async_copy(list_refs[i], lists[i], sems.at[i]) for i in range(len(lists))]


def prepare_kernel(shape, n_lists, *refs):
    list_refs, q_raw_ref, mask_ref, q_ref = refs[:n_lists], *refs[n_lists:n_lists + 3]
    q_raw, wide, allowed_ref, *lists, sems = refs[n_lists + 3:]
    seq_pos = lax.axis_index("seq")
    copies = read_lists(list_refs, lists, sems)
    for copy in copies:
        copy.start()
    q_copy = pltpu.make_async_copy(q_raw_ref, q_raw, sems.at[n_lists])
    q_copy.start()
    for copy in copies:
        copy.wait()
    mark_allowed(shape, *lists, allowed_ref)

    def fill_masks(slot, carry):
        owner = owner_of(shape, seq_pos, slot)
        there = (owner >= 0) & (owner <= seq_pos)
        base = jnp.where(there, owner, 0) * shape.blocks_here
        for h in range(shape.heads):
            for b in range(shape.blocks_here):
                for j in range(shape.blocks_here):
                    seen = there & (allowed_ref[h, b, base + j] > 0)
                    mask_ref[h, b, pl.ds(slot * shape.blocks_here + j, 1), :] = jnp.full(
                        (1, shape.head_dim), jnp.where(seen, 1.0, 0.0), jnp.float32
                    )
        return carry

    lax.fori_loop(0, shape.n_slots, fill_masks, 0)
    q_copy.wait()
    wide[...] = q_raw[...].astype(jnp.float32)
    for h in range(shape.heads):
        q_ref[h] = wide[pl.ds(h, shape.rows, stride=shape.heads), :].astype(q_ref.dtype)


def own_kernel(shape, mask_ref, q_ref, own_ref, peak_ref, acc_ref):
    for h in range(shape.heads):
        for b, start in tiles_of(shape):
            rows = pl.ds(b * shape.rows_unit + start, ROW_TILE)
            width = (b + 1) * BLOCK
            s = scores(q_ref[h, rows, :], own_ref[h, :width, :]) * shape.factor
            columns = []
            for j in range(b):
                seen = mask_ref[h, b, pl.ds(j, 1), :]
                columns.append(jnp.where(seen > 0.0, s[:, j * BLOCK:(j + 1) * BLOCK], HIDDEN))
            diagonal = s[:, b * BLOCK:]
            row = start + lax.broadcasted_iota(jnp.int32, diagonal.shape, 0)
            column = lax.broadcasted_iota(jnp.int32, diagonal.shape, 1)
            columns.append(jnp.where(column * shape.group <= row, diagonal, HIDDEN))
            s = jnp.concatenate(columns, axis=1)
            m = jnp.max(s, axis=1, keepdims=True)
            peak_ref[h, rows, :] = jnp.broadcast_to(m, (ROW_TILE, BLOCK))
            p = jnp.exp2(s - m).astype(jnp.bfloat16)
            vals = with_ones(own_ref[shape.heads + h, :width, :])
            acc_ref[h, rows, :] = jnp.dot(p, vals, preferred_element_type=jnp.float32)


def parts_of(shape, slots, h, mask_ref, piece_refs):
    parts = []
    for at in range(0, len(slots), PIECES_AT_ONCE):
        some_slots = slots[at:at + PIECES_AT_ONCE]
        some_refs = piece_refs[at:at + PIECES_AT_ONCE]
        vals = jnp.concatenate([ref[shape.heads + h] for ref in some_refs], axis=0)
        seen_vals = []
        for b in range(shape.blocks_here):
            masks = jnp.concatenate(
                [
                    jnp.broadcast_to(
                        mask_ref[h, b, pl.ds(slot * shape.blocks_here + j, 1), :],
                        (BLOCK, shape.head_dim),
                    )
                    for slot in some_slots for j in range(shape.blocks_here)
                ],
                axis=0,
            ).astype(jnp.bfloat16)
            seen_vals.append(jnp.concatenate([vals * masks, masks], axis=1))
        parts.append((jnp.concatenate([ref[h] for ref in some_refs], axis=0), seen_vals))
    return parts


def mixed_tile(shape, parts, h, b, rows, q_ref, peak_ref):
    q = q_ref[h, rows, :]
    m = peak_ref[h, rows, :]
    mixed = None
    for keys, seen_vals in parts:
        s = scores(q, keys) * shape.factor
        p = jnp.exp2(s - jnp.concatenate([m] * (s.shape[1] // m.shape[1]), axis=1))
        part = jnp.dot(p.astype(jnp.bfloat16), seen_vals[b], preferred_element_type=jnp.float32)
        mixed = part if mixed is None else mixed + part
    return mixed


def for_each_form(shape, slots, work):
    line = lax.axis_index("seq") // INNER
    steps = sorted({0} | {shape.away(slot) for slot in slots}) + [shape.outer]
    for least, below in zip(steps, steps[1:]):
        here = [i for i, slot in enumerate(slots) if shape.away(slot) <= least]
        pl.when((line >= least) & (line < below))(functools.partial(work, here))


def middle_kernel(shape, slots, mask_ref, q_ref, peak_ref, acc_in, *refs):
    del acc_in
    piece_refs, acc_ref = refs[:-1], refs[-1]

    def work(here):
        for h in range(shape.heads if here else 0):
            parts = parts_of(
                shape, [slots[i] for i in here], h, mask_ref, [piece_refs[i] for i in here]
            )
            for b, start in tiles_of(shape):
                rows = pl.ds(b * shape.rows_unit + start, ROW_TILE)
                acc_ref[h, rows, :] += mixed_tile(shape, parts, h, b, rows, q_ref, peak_ref)

    for_each_form(shape, slots, work)


def last_kernel(shape, slots, n_lists, mask_ref, q_ref, peak_in, acc_in, *refs):
    del peak_in, acc_in
    heads, head_dim = shape.heads, shape.head_dim
    n, n_all = len(slots), shape.n_slots
    piece_refs, all_refs, list_refs = refs[:n], refs[n:n + n_all], refs[n + n_all:][:n_lists]
    out_ref, peak_ref, acc_ref, *scratch = refs[n + n_all + n_lists:]
    out_tiles, worst, kv, allowed_ref, *lists, sems, out_sems = scratch
    seq_pos = lax.axis_index("seq")
    first_block = seq_pos * shape.blocks_here

    n_group = BLOCK * heads
    source = lax.broadcasted_iota(jnp.int32, (n_group, n_group), 1)
    target = (source % BLOCK) * heads + source // BLOCK
    order = (lax.broadcasted_iota(jnp.int32, (n_group, n_group), 0) == target).astype(jnp.float32)
    order = order.astype(jnp.bfloat16)

    def finish(sums):
        total = sums[:, head_dim:]
        inverse = pl.reciprocal(total, approx=True)
        inverse = inverse * (2.0 - total * inverse)
        bad = jnp.where(total < SAFE_TOTAL, 0.0, 1.0)
        worst[...] = jnp.maximum(
            worst[...], jnp.max(bad.reshape(ROW_TILE // 8, 8, head_dim), axis=0)
        )
        return (sums[:, :head_dim] * inverse).astype(jnp.bfloat16)

    def finish_all(parts):
        copies = []
        for at, (b, start) in enumerate(tiles_of(shape)):
            rows = pl.ds(b * shape.rows_unit + start, ROW_TILE)
            done = []
            for h in range(heads):
                sums = acc_ref[h, rows, :]
                if parts:
                    sums = sums + mixed_tile(shape, parts[h], h, b, rows, q_ref, peak_ref)
                done.append(finish(sums))
            for r in range(0, ROW_TILE, BLOCK):
                group = jnp.concatenate([x[r:r + BLOCK] for x in done], axis=0)
                out_tiles[at, pl.ds(r * heads, n_group), :] = jnp.dot(
                    order, group, preferred_element_type=jnp.float32
                ).astype(out_tiles.dtype)
            copies.append(
                pltpu.make_async_copy(
                    out_tiles.at[at],
                    out_ref.at[pl.ds(rows.start * heads, ROW_TILE * heads), :],
                    out_sems.at[at],
                )
            )
            copies[-1].start()
        for copy in copies:
            copy.wait()

    worst[...] = jnp.zeros_like(worst)
    for_each_form(
        shape, slots,
        lambda here: finish_all([
            parts_of(shape, [slots[i] for i in here], h, mask_ref, [piece_refs[i] for i in here])
            for h in range(heads)
        ] if here else []),
    )

    @pl.when(jnp.max(worst[...]) > 0.0)
    def _():
        copies = read_lists(list_refs, lists, sems) + [
            pltpu.make_async_copy(all_refs[i], kv.at[i], sems.at[n_lists + i])
            for i in range(n_all)
        ]
        for copy in copies:
            copy.start()
        for copy in copies:
            copy.wait()
        mark_allowed(shape, *lists, allowed_ref)

        def every_tile(step):
            def slot_step(i, carry):
                owner = owner_of(shape, seq_pos, i)

                @pl.when((owner >= 0) & (owner <= seq_pos))
                def _():
                    for h in range(heads):
                        for b, start in tiles_of(shape):
                            rows = pl.ds(b * shape.rows_unit + start, ROW_TILE)
                            s = scores(q_ref[h, rows, :], kv[i, h]) * shape.factor
                            columns = []
                            for j in range(shape.blocks_here):
                                block = owner * shape.blocks_here + j
                                part = s[:, j * BLOCK:(j + 1) * BLOCK]
                                row = start + lax.broadcasted_iota(jnp.int32, part.shape, 0)
                                column = lax.broadcasted_iota(jnp.int32, part.shape, 1)
                                ahead = (first_block + b - block) * BLOCK
                                part = jnp.where(
                                    (column - ahead) * shape.group <= row, part, HIDDEN
                                )
                                seen = allowed_ref[h, b, block] > 0
                                columns.append(part + jnp.where(seen, 0.0, HIDDEN))
                            step(h, rows, jnp.concatenate(columns, axis=1), i)

                return carry

            lax.fori_loop(0, n_all, slot_step, 0)

        def widen(h, rows, s, i):
            m = jnp.max(s, axis=1, keepdims=True)
            peak_ref[h, rows, :] = jnp.maximum(peak_ref[h, rows, :], m)

        def collect(h, rows, s, i):
            m = peak_ref[h, rows, :]
            p = jnp.exp2(s - jnp.concatenate([m] * shape.blocks_here, axis=1))
            acc_ref[h, rows, :] += jnp.dot(
                p.astype(jnp.bfloat16), with_ones(kv[i, heads + h]),
                preferred_element_type=jnp.float32,
            )

        every_tile(widen)
        acc_ref[...] = jnp.zeros_like(acc_ref)
        every_tile(collect)
        finish_all([])


def per_device(
    n_seq, queries, keys, values, retrieval_ids, vertical_blocks, slash_offsets, sink_blocks,
    window_blocks,
):
    tokens_here, heads, width = queries.shape
    head_dim = keys.shape[2]
    group = width // head_dim
    blocks_here = tokens_here // BLOCK
    shape = Shape(heads, blocks_here, n_seq * blocks_here, group, head_dim, n_seq)
    outer = shape.outer

    vmem = pl.BlockSpec(memory_space=pltpu.VMEM)
    hbm = pl.BlockSpec(memory_space=pltpu.HBM)
    anywhere = pl.BlockSpec(memory_space=pl.ANY)
    mask_shape = jax.ShapeDtypeStruct(
        (heads, blocks_here, shape.block_total, head_dim), jnp.float32
    )
    q_shape = jax.ShapeDtypeStruct((heads, shape.rows, head_dim), jnp.bfloat16)
    peak_shape = jax.ShapeDtypeStruct((heads, shape.rows, head_dim), jnp.float32)
    acc_shape = jax.ShapeDtypeStruct((heads, shape.rows, 2 * head_dim), jnp.float32)
    allowed_scratch = pltpu.SMEM((heads, blocks_here, shape.block_total), jnp.int32)
    params = pltpu.CompilerParams(vmem_limit_bytes=16 << 20)
    cost = pl.CostEstimate(flops=1 << 20, transcendentals=0, bytes_accessed=1 << 10)

    own = jnp.concatenate(
        [jnp.transpose(keys, (1, 0, 2)), jnp.transpose(values, (1, 0, 2))], axis=0
    )
    q_raw = queries.reshape(tokens_here, heads, group, head_dim)
    q_raw = jnp.transpose(q_raw, (0, 2, 1, 3)).reshape(heads * shape.rows, head_dim)
    q_raw = pltpu.with_memory_space_constraint(q_raw, pltpu.HBM)
    lists = tuple(
        pltpu.with_memory_space_constraint(x, pltpu.HBM)
        for x in (retrieval_ids, vertical_blocks, slash_offsets, sink_blocks, window_blocks)
    )
    n_lists = len(lists)
    list_scratch = [pltpu.SMEM(x.shape, jnp.int32) for x in lists]

    def prepare(q_raw):
        return pl.pallas_call(
            functools.partial(prepare_kernel, shape, n_lists),
            out_shape=(mask_shape, q_shape),
            in_specs=[hbm] * (n_lists + 1),
            out_specs=(vmem, vmem),
            scratch_shapes=[
                pltpu.VMEM((heads * shape.rows, head_dim), jnp.bfloat16),
                pltpu.VMEM((heads * shape.rows, head_dim), jnp.float32),
                allowed_scratch,
                *list_scratch,
                pltpu.SemaphoreType.DMA((n_lists + 1,)),
            ],
            compiler_params=params,
            cost_estimate=cost,
        )(*lists, q_raw)

    def start_sums():
        return pl.pallas_call(
            functools.partial(own_kernel, shape),
            out_shape=(peak_shape, acc_shape),
            in_specs=[vmem] * 3,
            out_specs=(vmem, vmem),
            compiler_params=params,
            cost_estimate=cost,
        )(mask, q, own)

    def add(acc, slots):
        return pl.pallas_call(
            functools.partial(middle_kernel, shape, slots),
            out_shape=acc_shape,
            in_specs=[vmem] * (4 + len(slots)),
            out_specs=vmem,
            input_output_aliases={3: 0},
            compiler_params=params,
            cost_estimate=cost,
        )(mask, q, peak, acc, *[piece[slot] for slot in slots])

    def send(x, pairs):
        return lax.ppermute(x, "seq", pairs)

    def along(x, least, step=1, most=outer):
        return send(x, [
            (s, s + step * INNER) for s in range(n_seq)
            if least <= s // INNER < min(most, outer - step)
        ])

    def across(x, least):
        return send(x, [
            (s, s ^ 1) for s in range(n_seq)
            if s // INNER >= least and (least > 0 or s % INNER == 0)
        ])

    piece = {0: own}
    if outer == 4:
        first = [along(own, k, most=k + 1) for k in range(3)]
        piece[4] = send(own, [(s, s ^ 1) for s in range(n_seq) if s % INNER == 0 or s == 1])
        second = [None, along(first[0], 1, most=2), along(first[1], 2)]
        q_raw, first[0] = lax.optimization_barrier((q_raw, first[0]))
        mask, q = prepare(q_raw)
        piece[1] = first[0] + first[1] + first[2]
        piece[1], q = lax.optimization_barrier((piece[1], q))
        piece[5] = across(piece[1], 1)
        piece[7] = along(piece[4], 0, step=3, most=1)
        q, second[1], piece[4] = lax.optimization_barrier((q, second[1], piece[4]))
        piece[3] = along(second[1], 2)
        peak, acc = start_sums()
        second[2], acc = lax.optimization_barrier((second[2], acc))
        piece[2] = second[1] + second[2]
        piece[6] = across(piece[2], 2)
        acc = add(acc, [1, 4])
        acc = add(acc, [2, 5])
        acc = add(acc, [7])
        last_slots = [3, 6]
    else:
        mask, q = prepare(q_raw)
        peak, acc = start_sums()
        for step in range(outer):
            if step + 1 < outer:
                piece[step + 1] = along(piece[step], step)
            piece[outer + step] = across(piece[step], step)
            if step > 0:
                acc = add(acc, [step, outer + step - 1])
            if step + 1 < outer:
                piece[step + 1], acc = lax.optimization_barrier((piece[step + 1], acc))
        last_slots = [n_seq - 1]

    out, _, _ = pl.pallas_call(
        functools.partial(last_kernel, shape, last_slots, n_lists),
        out_shape=(
            jax.ShapeDtypeStruct((heads * shape.rows, head_dim), jnp.bfloat16),
            peak_shape,
            acc_shape,
        ),
        in_specs=[vmem] * (4 + len(last_slots)) + [anywhere] * n_seq + [hbm] * n_lists,
        out_specs=(hbm, vmem, vmem),
        input_output_aliases={2: 1, 3: 2},
        scratch_shapes=[
            pltpu.VMEM((shape.rows // ROW_TILE, heads * ROW_TILE, head_dim), jnp.bfloat16),
            pltpu.VMEM((8, head_dim), jnp.float32),
            pltpu.VMEM((n_seq,) + own.shape, jnp.bfloat16),
            allowed_scratch,
            *list_scratch,
            pltpu.SemaphoreType.DMA((n_lists + n_seq,)),
            pltpu.SemaphoreType.DMA((shape.rows // ROW_TILE,)),
        ],
        compiler_params=pltpu.CompilerParams(
            vmem_limit_bytes=(16 << 20) + 2 * n_seq * own.size
        ),
        cost_estimate=cost,
    )(
        mask, q, peak, acc, *[piece[slot] for slot in last_slots],
        *[piece[slot] for slot in range(n_seq)], *lists,
    )
    out = out.reshape(tokens_here, group, heads, head_dim)
    return jnp.transpose(out, (0, 2, 1, 3)).reshape(tokens_here, heads, width)


def solution(mesh):
    in_specs = (
        P("seq", "head", None),
        P("seq", "head", None),
        P("seq", "head", None),
        P(),
        P("seq", None, None),
        P("seq", None, None),
        P(),
        P(),
    )
    out_specs = P("seq", "head", None)
    return jax.shard_map(
        functools.partial(per_device, mesh.shape["seq"]),
        mesh=mesh, in_specs=in_specs, out_specs=out_specs, check_vma=False,
    )
```

```python
import functools
import math

import jax
import jax.numpy as jnp
from jax import lax
from jax.experimental import pallas as pl
from jax.experimental.pallas import tpu as pltpu
from jax.sharding import PartitionSpec as P

KV_HEADS = 8
BLOCK = 128
INNER = 2
ROW_TILE = 256
PIECES_AT_ONCE = 2
HIDDEN = -1e30
SAFE_TOTAL = 1e30


class Shape:
    def __init__(self, heads, blocks_here, block_total, group, head_dim, n_slots):
        self.heads = heads
        self.blocks_here = blocks_here
        self.block_total = block_total
        self.group = group
        self.head_dim = head_dim
        self.n_slots = n_slots
        self.outer = n_slots // INNER
        self.rows_unit = BLOCK * group
        self.rows = blocks_here * self.rows_unit
        self.factor = head_dim ** -0.5 * math.log2(math.e)

    def away(self, slot):
        return slot % self.outer


def owner_of(shape, seq_pos, slot):
    crossed = slot >= shape.outer
    line = seq_pos // INNER - jnp.where(crossed, slot - shape.outer, slot)
    place = seq_pos % INNER
    return line * INNER + jnp.where(crossed, 1 - place, place)


def scores(q, keys):
    return lax.dot_general(q, keys, (((1,), (1,)), ((), ())), preferred_element_type=jnp.float32)


def with_ones(vals):
    return jnp.concatenate([vals, jnp.ones_like(vals)], axis=1)


def tiles_of(shape):
    return [(b, r * ROW_TILE) for b in range(shape.blocks_here)
            for r in range(shape.rows_unit // ROW_TILE)]


def mark_allowed(shape, retr_ref, vert_ref, slash_ref, sink_ref, window_ref, allowed_ref):
    first_block = lax.axis_index("seq") * shape.blocks_here
    first_head = lax.axis_index("head") * shape.heads
    n_retr = retr_ref.shape[0]
    for h in range(shape.heads):
        head_id = first_head + h
        is_retr = functools.reduce(
            jnp.logical_or, [retr_ref[i] == head_id for i in range(n_retr)]
        )
        for b in range(shape.blocks_here):
            query_block = first_block + b
            sinks = jnp.where(is_retr, 0, sink_ref[head_id])
            lowest = query_block - jnp.where(is_retr, 1, window_ref[head_id])

            def clear(c, carry):
                read = ((c < sinks) | (c > lowest)) & (c <= query_block)
                allowed_ref[h, b, c] = read.astype(jnp.int32)
                return carry

            lax.fori_loop(0, shape.block_total, clear, 0)
            for j in range(vert_ref.shape[2]):
                c = vert_ref[b, head_id, j]
                allowed_ref[h, b, jnp.where(is_retr, c, query_block)] = 1
            for j in range(slash_ref.shape[2]):
                c = query_block - slash_ref[b, head_id, j]
                allowed_ref[h, b, jnp.where(is_retr, c, query_block)] = 1


def read_lists(list_refs, lists, sems):
    return [pltpu.make_async_copy(list_refs[i], lists[i], sems.at[i]) for i in range(len(lists))]


def prepare_kernel(shape, n_lists, *refs):
    list_refs, q_raw_ref, mask_ref, q_ref = refs[:n_lists], *refs[n_lists:n_lists + 3]
    q_raw, wide, allowed_ref, *lists, sems = refs[n_lists + 3:]
    seq_pos = lax.axis_index("seq")
    copies = read_lists(list_refs, lists, sems)
    for copy in copies:
        copy.start()
    q_copy = pltpu.make_async_copy(q_raw_ref, q_raw, sems.at[n_lists])
    q_copy.start()
    for copy in copies:
        copy.wait()
    mark_allowed(shape, *lists, allowed_ref)

    def fill_masks(slot, carry):
        owner = owner_of(shape, seq_pos, slot)
        there = (owner >= 0) & (owner <= seq_pos)
        base = jnp.where(there, owner, 0) * shape.blocks_here
        for h in range(shape.heads):
            for b in range(shape.blocks_here):
                for j in range(shape.blocks_here):
                    seen = there & (allowed_ref[h, b, base + j] > 0)
                    mask_ref[h, b, pl.ds(slot * shape.blocks_here + j, 1), :] = jnp.full(
                        (1, shape.head_dim), jnp.where(seen, 1.0, 0.0), jnp.float32
                    )
        return carry

    lax.fori_loop(0, shape.n_slots, fill_masks, 0)
    q_copy.wait()
    wide[...] = q_raw[...].astype(jnp.float32)
    for h in range(shape.heads):
        q_ref[h] = wide[pl.ds(h, shape.rows, stride=shape.heads), :].astype(q_ref.dtype)


def own_kernel(shape, mask_ref, q_ref, own_ref, peak_ref, acc_ref):
    for h in range(shape.heads):
        for b, start in tiles_of(shape):
            rows = pl.ds(b * shape.rows_unit + start, ROW_TILE)
            width = (b + 1) * BLOCK
            s = scores(q_ref[h, rows, :], own_ref[h, :width, :]) * shape.factor
            columns = []
            for j in range(b):
                seen = mask_ref[h, b, pl.ds(j, 1), :]
                columns.append(jnp.where(seen > 0.0, s[:, j * BLOCK:(j + 1) * BLOCK], HIDDEN))
            diagonal = s[:, b * BLOCK:]
            row = start + lax.broadcasted_iota(jnp.int32, diagonal.shape, 0)
            column = lax.broadcasted_iota(jnp.int32, diagonal.shape, 1)
            columns.append(jnp.where(column * shape.group <= row, diagonal, HIDDEN))
            s = jnp.concatenate(columns, axis=1)
            m = jnp.max(s, axis=1, keepdims=True)
            peak_ref[h, rows, :] = jnp.broadcast_to(m, (ROW_TILE, BLOCK))
            p = jnp.exp2(s - m).astype(jnp.bfloat16)
            vals = with_ones(own_ref[shape.heads + h, :width, :])
            acc_ref[h, rows, :] = jnp.dot(p, vals, preferred_element_type=jnp.float32)


def parts_of(shape, slots, h, mask_ref, piece_refs):
    parts = []
    for at in range(0, len(slots), PIECES_AT_ONCE):
        some_slots = slots[at:at + PIECES_AT_ONCE]
        some_refs = piece_refs[at:at + PIECES_AT_ONCE]
        vals = jnp.concatenate([ref[shape.heads + h] for ref in some_refs], axis=0)
        seen_vals = []
        for b in range(shape.blocks_here):
            masks = jnp.concatenate(
                [
                    jnp.broadcast_to(
                        mask_ref[h, b, pl.ds(slot * shape.blocks_here + j, 1), :],
                        (BLOCK, shape.head_dim),
                    )
                    for slot in some_slots for j in range(shape.blocks_here)
                ],
                axis=0,
            ).astype(jnp.bfloat16)
            seen_vals.append(jnp.concatenate([vals * masks, masks], axis=1))
        parts.append((jnp.concatenate([ref[h] for ref in some_refs], axis=0), seen_vals))
    return parts


def mixed_tile(shape, parts, h, b, rows, q_ref, peak_ref):
    q = q_ref[h, rows, :]
    m = peak_ref[h, rows, :]
    mixed = None
    for keys, seen_vals in parts:
        s = scores(q, keys) * shape.factor
        p = jnp.exp2(s - jnp.concatenate([m] * (s.shape[1] // m.shape[1]), axis=1))
        part = jnp.dot(p.astype(jnp.bfloat16), seen_vals[b], preferred_element_type=jnp.float32)
        mixed = part if mixed is None else mixed + part
    return mixed


def for_each_form(shape, slots, work):
    line = lax.axis_index("seq") // INNER
    steps = sorted({0} | {shape.away(slot) for slot in slots}) + [shape.outer]
    for least, below in zip(steps, steps[1:]):
        here = [i for i, slot in enumerate(slots) if shape.away(slot) <= least]
        pl.when((line >= least) & (line < below))(functools.partial(work, here))


def middle_kernel(shape, slots, mask_ref, q_ref, peak_ref, acc_in, *refs):
    del acc_in
    piece_refs, acc_ref = refs[:-1], refs[-1]

    def work(here):
        for h in range(shape.heads if here else 0):
            parts = parts_of(
                shape, [slots[i] for i in here], h, mask_ref, [piece_refs[i] for i in here]
            )
            for b, start in tiles_of(shape):
                rows = pl.ds(b * shape.rows_unit + start, ROW_TILE)
                acc_ref[h, rows, :] += mixed_tile(shape, parts, h, b, rows, q_ref, peak_ref)

    for_each_form(shape, slots, work)


def last_kernel(shape, slots, n_lists, mask_ref, q_ref, peak_in, acc_in, *refs):
    del peak_in, acc_in
    heads, head_dim = shape.heads, shape.head_dim
    n, n_all = len(slots), shape.n_slots
    piece_refs, all_refs, list_refs = refs[:n], refs[n:n + n_all], refs[n + n_all:][:n_lists]
    out_ref, peak_ref, acc_ref, *scratch = refs[n + n_all + n_lists:]
    out_rows, out_tiles, worst, kv, allowed_ref, *lists, sems, out_sems = scratch
    seq_pos = lax.axis_index("seq")
    first_block = seq_pos * shape.blocks_here

    def finish(h, at, sums):
        total = sums[:, head_dim:]
        inverse = pl.reciprocal(total, approx=True)
        inverse = inverse * (2.0 - total * inverse)
        out_rows[at, pl.ds(h, ROW_TILE, stride=heads), :] = sums[:, :head_dim] * inverse
        bad = jnp.where(total < SAFE_TOTAL, 0.0, 1.0)
        worst[...] = jnp.maximum(
            worst[...], jnp.max(bad.reshape(ROW_TILE // 8, 8, head_dim), axis=0)
        )

    def finish_all(parts):
        copies = []
        for h in range(heads):
            for at, (b, start) in enumerate(tiles_of(shape)):
                rows = pl.ds(b * shape.rows_unit + start, ROW_TILE)
                sums = acc_ref[h, rows, :]
                if parts:
                    sums = sums + mixed_tile(shape, parts[h], h, b, rows, q_ref, peak_ref)
                finish(h, at, sums)
                if h + 1 < heads:
                    continue
                out_tiles[at] = out_rows[at].astype(out_tiles.dtype)
                copies.append(
                    pltpu.make_async_copy(
                        out_tiles.at[at],
                        out_ref.at[pl.ds(rows.start * heads, ROW_TILE * heads), :],
                        out_sems.at[at],
                    )
                )
                copies[-1].start()
        for copy in copies:
            copy.wait()

    worst[...] = jnp.zeros_like(worst)
    for_each_form(
        shape, slots,
        lambda here: finish_all([
            parts_of(shape, [slots[i] for i in here], h, mask_ref, [piece_refs[i] for i in here])
            for h in range(heads)
        ] if here else []),
    )

    @pl.when(jnp.max(worst[...]) > 0.0)
    def _():
        copies = read_lists(list_refs, lists, sems) + [
            pltpu.make_async_copy(all_refs[i], kv.at[i], sems.at[n_lists + i])
            for i in range(n_all)
        ]
        for copy in copies:
            copy.start()
        for copy in copies:
            copy.wait()
        mark_allowed(shape, *lists, allowed_ref)

        def every_tile(step):
            def slot_step(i, carry):
                owner = owner_of(shape, seq_pos, i)

                @pl.when((owner >= 0) & (owner <= seq_pos))
                def _():
                    for h in range(heads):
                        for b, start in tiles_of(shape):
                            rows = pl.ds(b * shape.rows_unit + start, ROW_TILE)
                            s = scores(q_ref[h, rows, :], kv[i, h]) * shape.factor
                            columns = []
                            for j in range(shape.blocks_here):
                                block = owner * shape.blocks_here + j
                                part = s[:, j * BLOCK:(j + 1) * BLOCK]
                                row = start + lax.broadcasted_iota(jnp.int32, part.shape, 0)
                                column = lax.broadcasted_iota(jnp.int32, part.shape, 1)
                                ahead = (first_block + b - block) * BLOCK
                                part = jnp.where(
                                    (column - ahead) * shape.group <= row, part, HIDDEN
                                )
                                seen = allowed_ref[h, b, block] > 0
                                columns.append(part + jnp.where(seen, 0.0, HIDDEN))
                            step(h, rows, jnp.concatenate(columns, axis=1), i)

                return carry

            lax.fori_loop(0, n_all, slot_step, 0)

        def widen(h, rows, s, i):
            m = jnp.max(s, axis=1, keepdims=True)
            peak_ref[h, rows, :] = jnp.maximum(peak_ref[h, rows, :], m)

        def collect(h, rows, s, i):
            m = peak_ref[h, rows, :]
            p = jnp.exp2(s - jnp.concatenate([m] * shape.blocks_here, axis=1))
            acc_ref[h, rows, :] += jnp.dot(
                p.astype(jnp.bfloat16), with_ones(kv[i, heads + h]),
                preferred_element_type=jnp.float32,
            )

        every_tile(widen)
        acc_ref[...] = jnp.zeros_like(acc_ref)
        every_tile(collect)
        finish_all([])


def per_device(
    n_seq, queries, keys, values, retrieval_ids, vertical_blocks, slash_offsets, sink_blocks,
    window_blocks,
):
    tokens_here, heads, width = queries.shape
    head_dim = keys.shape[2]
    group = width // head_dim
    blocks_here = tokens_here // BLOCK
    shape = Shape(heads, blocks_here, n_seq * blocks_here, group, head_dim, n_seq)
    outer = shape.outer

    vmem = pl.BlockSpec(memory_space=pltpu.VMEM)
    hbm = pl.BlockSpec(memory_space=pltpu.HBM)
    anywhere = pl.BlockSpec(memory_space=pl.ANY)
    mask_shape = jax.ShapeDtypeStruct(
        (heads, blocks_here, shape.block_total, head_dim), jnp.float32
    )
    q_shape = jax.ShapeDtypeStruct((heads, shape.rows, head_dim), jnp.bfloat16)
    peak_shape = jax.ShapeDtypeStruct((heads, shape.rows, head_dim), jnp.float32)
    acc_shape = jax.ShapeDtypeStruct((heads, shape.rows, 2 * head_dim), jnp.float32)
    allowed_scratch = pltpu.SMEM((heads, blocks_here, shape.block_total), jnp.int32)
    params = pltpu.CompilerParams(vmem_limit_bytes=16 << 20)
    cost = pl.CostEstimate(flops=1 << 20, transcendentals=0, bytes_accessed=1 << 10)

    own = jnp.concatenate(
        [jnp.transpose(keys, (1, 0, 2)), jnp.transpose(values, (1, 0, 2))], axis=0
    )
    q_raw = queries.reshape(tokens_here, heads, group, head_dim)
    q_raw = jnp.transpose(q_raw, (0, 2, 1, 3)).reshape(heads * shape.rows, head_dim)
    q_raw = pltpu.with_memory_space_constraint(q_raw, pltpu.HBM)
    lists = tuple(
        pltpu.with_memory_space_constraint(x, pltpu.HBM)
        for x in (retrieval_ids, vertical_blocks, slash_offsets, sink_blocks, window_blocks)
    )
    n_lists = len(lists)
    list_scratch = [pltpu.SMEM(x.shape, jnp.int32) for x in lists]

    def prepare(q_raw):
        return pl.pallas_call(
            functools.partial(prepare_kernel, shape, n_lists),
            out_shape=(mask_shape, q_shape),
            in_specs=[hbm] * (n_lists + 1),
            out_specs=(vmem, vmem),
            scratch_shapes=[
                pltpu.VMEM((heads * shape.rows, head_dim), jnp.bfloat16),
                pltpu.VMEM((heads * shape.rows, head_dim), jnp.float32),
                allowed_scratch,
                *list_scratch,
                pltpu.SemaphoreType.DMA((n_lists + 1,)),
            ],
            compiler_params=params,
            cost_estimate=cost,
        )(*lists, q_raw)

    def start_sums():
        return pl.pallas_call(
            functools.partial(own_kernel, shape),
            out_shape=(peak_shape, acc_shape),
            in_specs=[vmem] * 3,
            out_specs=(vmem, vmem),
            compiler_params=params,
            cost_estimate=cost,
        )(mask, q, own)

    def add(acc, slots, cost=cost):
        return pl.pallas_call(
            functools.partial(middle_kernel, shape, slots),
            out_shape=acc_shape,
            in_specs=[vmem] * (4 + len(slots)),
            out_specs=vmem,
            input_output_aliases={3: 0},
            compiler_params=params,
            cost_estimate=cost,
        )(mask, q, peak, acc, *[piece[slot] for slot in slots])

    def send(x, pairs):
        return lax.ppermute(x, "seq", pairs)

    def along(x, least, step=1, most=outer):
        return send(x, [
            (s, s + step * INNER) for s in range(n_seq)
            if least <= s // INNER < min(most, outer - step)
        ])

    def across(x, least):
        return send(x, [
            (s, s ^ 1) for s in range(n_seq)
            if s // INNER >= least and (least > 0 or s % INNER == 0)
        ])

    piece = {0: own}
    if outer == 4:
        first = [along(own, k, most=k + 1) for k in range(3)]
        piece[4] = send(own, [(s, s ^ 1) for s in range(n_seq) if s % INNER == 0 or s == 1])
        second = [None, along(first[0], 1, most=2), along(first[1], 2)]
        q_raw, first[0] = lax.optimization_barrier((q_raw, first[0]))
        mask, q = prepare(q_raw)
        piece[1] = first[0] + first[1] + first[2]
        piece[1], q = lax.optimization_barrier((piece[1], q))
        piece[5] = across(piece[1], 1)
        piece[7] = along(piece[4], 0, step=3, most=1)
        q, second[1], piece[4] = lax.optimization_barrier((q, second[1], piece[4]))
        piece[3] = along(second[1], 2)
        peak, acc = start_sums()
        second[2], acc = lax.optimization_barrier((second[2], acc))
        piece[2] = second[1] + second[2]
        piece[6] = across(piece[2], 2)
        heavy = pl.CostEstimate(flops=1 << 36, transcendentals=0, bytes_accessed=1 << 10)
        acc = add(acc, [1, 4], heavy)
        acc = add(acc, [2, 5])
        acc = add(acc, [7])
        acc = add(acc, [6])
        last_slots = [3]
    else:
        mask, q = prepare(q_raw)
        peak, acc = start_sums()
        for step in range(outer):
            if step + 1 < outer:
                piece[step + 1] = along(piece[step], step)
            piece[outer + step] = across(piece[step], step)
            if step > 0:
                acc = add(acc, [step, outer + step - 1])
            if step + 1 < outer:
                piece[step + 1], acc = lax.optimization_barrier((piece[step + 1], acc))
        last_slots = [n_seq - 1]

    out, _, _ = pl.pallas_call(
        functools.partial(last_kernel, shape, last_slots, n_lists),
        out_shape=(
            jax.ShapeDtypeStruct((heads * shape.rows, head_dim), jnp.bfloat16),
            peak_shape,
            acc_shape,
        ),
        in_specs=[vmem] * (4 + len(last_slots)) + [anywhere] * n_seq + [hbm] * n_lists,
        out_specs=(hbm, vmem, vmem),
        input_output_aliases={2: 1, 3: 2},
        scratch_shapes=[
            pltpu.VMEM((shape.rows // ROW_TILE, heads * ROW_TILE, head_dim), jnp.float32),
            pltpu.VMEM((shape.rows // ROW_TILE, heads * ROW_TILE, head_dim), jnp.bfloat16),
            pltpu.VMEM((8, head_dim), jnp.float32),
            pltpu.VMEM((n_seq,) + own.shape, jnp.bfloat16),
            allowed_scratch,
            *list_scratch,
            pltpu.SemaphoreType.DMA((n_lists + n_seq,)),
            pltpu.SemaphoreType.DMA((shape.rows // ROW_TILE,)),
        ],
        compiler_params=pltpu.CompilerParams(
            vmem_limit_bytes=(16 << 20) + 2 * n_seq * own.size
        ),
        cost_estimate=cost,
    )(
        mask, q, peak, acc, *[piece[slot] for slot in last_slots],
        *[piece[slot] for slot in range(n_seq)], *lists,
    )
    out = out.reshape(tokens_here, group, heads, head_dim)
    return jnp.transpose(out, (0, 2, 1, 3)).reshape(tokens_here, heads, width)


def solution(mesh):
    in_specs = (
        P("seq", "head", None),
        P("seq", "head", None),
        P("seq", "head", None),
        P(),
        P("seq", None, None),
        P("seq", None, None),
        P(),
        P(),
    )
    out_specs = P("seq", "head", None)
    return jax.shard_map(
        functools.partial(per_device, mesh.shape["seq"]),
        mesh=mesh, in_specs=in_specs, out_specs=out_specs, check_vma=False,
    )
```

```python
import functools
import math

import jax
import jax.numpy as jnp
from jax import lax
from jax.experimental import pallas as pl
from jax.experimental.pallas import tpu as pltpu
from jax.sharding import PartitionSpec as P

KV_HEADS = 8
BLOCK = 128
INNER = 2
ROW_TILE = 256
PIECES_AT_ONCE = 2
HIDDEN = -1e30
SAFE_TOTAL = 1e30


class Shape:
    def __init__(self, heads, blocks_here, block_total, group, head_dim, n_slots):
        self.heads = heads
        self.blocks_here = blocks_here
        self.block_total = block_total
        self.group = group
        self.head_dim = head_dim
        self.n_slots = n_slots
        self.outer = n_slots // INNER
        self.rows_unit = BLOCK * group
        self.rows = blocks_here * self.rows_unit
        self.factor = head_dim ** -0.5 * math.log2(math.e)

    def away(self, slot):
        return slot % self.outer


def owner_of(shape, seq_pos, slot):
    crossed = slot >= shape.outer
    line = seq_pos // INNER - jnp.where(crossed, slot - shape.outer, slot)
    place = seq_pos % INNER
    return line * INNER + jnp.where(crossed, 1 - place, place)


def scores(q, keys):
    return lax.dot_general(q, keys, (((1,), (1,)), ((), ())), preferred_element_type=jnp.float32)


def with_ones(vals):
    return jnp.concatenate([vals, jnp.ones_like(vals)], axis=1)


def tiles_of(shape):
    return [(b, r * ROW_TILE) for b in range(shape.blocks_here)
            for r in range(shape.rows_unit // ROW_TILE)]


def mark_allowed(shape, retr_ref, vert_ref, slash_ref, sink_ref, window_ref, allowed_ref):
    first_block = lax.axis_index("seq") * shape.blocks_here
    first_head = lax.axis_index("head") * shape.heads
    n_retr = retr_ref.shape[0]
    for h in range(shape.heads):
        head_id = first_head + h
        is_retr = functools.reduce(
            jnp.logical_or, [retr_ref[i] == head_id for i in range(n_retr)]
        )
        for b in range(shape.blocks_here):
            query_block = first_block + b
            sinks = jnp.where(is_retr, 0, sink_ref[head_id])
            lowest = query_block - jnp.where(is_retr, 1, window_ref[head_id])

            def clear(c, carry):
                read = ((c < sinks) | (c > lowest)) & (c <= query_block)
                allowed_ref[h, b, c] = read.astype(jnp.int32)
                return carry

            lax.fori_loop(0, shape.block_total, clear, 0, unroll=shape.block_total <= 16)
            for j in range(vert_ref.shape[2]):
                c = vert_ref[b, head_id, j]
                allowed_ref[h, b, jnp.where(is_retr, c, query_block)] = 1
            for j in range(slash_ref.shape[2]):
                c = query_block - slash_ref[b, head_id, j]
                allowed_ref[h, b, jnp.where(is_retr, c, query_block)] = 1


def read_lists(list_refs, lists, sems):
    return [pltpu.make_async_copy(list_refs[i], lists[i], sems.at[i]) for i in range(len(lists))]


def prepare_kernel(shape, n_lists, *refs):
    list_refs, q_raw_ref, mask_ref, q_ref = refs[:n_lists], *refs[n_lists:n_lists + 3]
    q_raw, wide, allowed_ref, *lists, sems = refs[n_lists + 3:]
    seq_pos = lax.axis_index("seq")
    copies = read_lists(list_refs, lists, sems)
    for copy in copies:
        copy.start()
    q_copy = pltpu.make_async_copy(q_raw_ref, q_raw, sems.at[n_lists])
    q_copy.start()
    for copy in copies + [q_copy]:
        copy.wait()
    mark_allowed(shape, *lists, allowed_ref)
    wide[...] = q_raw[...].astype(jnp.float32)
    for h in range(shape.heads):
        q_ref[h] = wide[pl.ds(h, shape.rows, stride=shape.heads), :].astype(q_ref.dtype)

    def fill_masks(slot, carry):
        owner = owner_of(shape, seq_pos, slot)
        there = (owner >= 0) & (owner <= seq_pos)
        base = jnp.where(there, owner, 0) * shape.blocks_here
        for h in range(shape.heads):
            for b in range(shape.blocks_here):
                for j in range(shape.blocks_here):
                    seen = there & (allowed_ref[h, b, base + j] > 0)
                    mask_ref[h, b, pl.ds(slot * shape.blocks_here + j, 1), :] = jnp.full(
                        (1, shape.head_dim), jnp.where(seen, 1.0, 0.0), jnp.float32
                    )
        return carry

    lax.fori_loop(0, shape.n_slots, fill_masks, 0, unroll=shape.n_slots <= 8)


def own_kernel(shape, mask_ref, q_ref, own_ref, peak_ref, acc_ref):
    for h in range(shape.heads):
        for b, start in tiles_of(shape):
            rows = pl.ds(b * shape.rows_unit + start, ROW_TILE)
            width = (b + 1) * BLOCK
            s = scores(q_ref[h, rows, :], own_ref[h, :width, :]) * shape.factor
            columns = []
            for j in range(b):
                seen = mask_ref[h, b, pl.ds(j, 1), :]
                columns.append(jnp.where(seen > 0.0, s[:, j * BLOCK:(j + 1) * BLOCK], HIDDEN))
            diagonal = s[:, b * BLOCK:]
            row = start + lax.broadcasted_iota(jnp.int32, diagonal.shape, 0)
            column = lax.broadcasted_iota(jnp.int32, diagonal.shape, 1)
            columns.append(jnp.where(column * shape.group <= row, diagonal, HIDDEN))
            s = jnp.concatenate(columns, axis=1)
            m = jnp.max(s, axis=1, keepdims=True)
            peak_ref[h, rows, :] = jnp.broadcast_to(m, (ROW_TILE, BLOCK))
            p = jnp.exp2(s - m).astype(jnp.bfloat16)
            vals = with_ones(own_ref[shape.heads + h, :width, :])
            acc_ref[h, rows, :] = jnp.dot(p, vals, preferred_element_type=jnp.float32)


def parts_of(shape, slots, h, mask_ref, piece_refs):
    parts = []
    for at in range(0, len(slots), PIECES_AT_ONCE):
        some_slots = slots[at:at + PIECES_AT_ONCE]
        some_refs = piece_refs[at:at + PIECES_AT_ONCE]
        vals = jnp.concatenate([ref[shape.heads + h] for ref in some_refs], axis=0)
        seen_vals = []
        for b in range(shape.blocks_here):
            masks = jnp.concatenate(
                [
                    jnp.broadcast_to(
                        mask_ref[h, b, pl.ds(slot * shape.blocks_here + j, 1), :],
                        (BLOCK, shape.head_dim),
                    )
                    for slot in some_slots for j in range(shape.blocks_here)
                ],
                axis=0,
            ).astype(jnp.bfloat16)
            seen_vals.append(jnp.concatenate([vals * masks, masks], axis=1))
        parts.append((jnp.concatenate([ref[h] for ref in some_refs], axis=0), seen_vals))
    return parts


def mixed_tile(shape, parts, h, b, rows, q_ref, peak_ref):
    q = q_ref[h, rows, :]
    m = peak_ref[h, rows, :]
    mixed = None
    for keys, seen_vals in parts:
        s = scores(q, keys) * shape.factor
        p = jnp.exp2(s - jnp.concatenate([m] * (s.shape[1] // m.shape[1]), axis=1))
        part = jnp.dot(p.astype(jnp.bfloat16), seen_vals[b], preferred_element_type=jnp.float32)
        mixed = part if mixed is None else mixed + part
    return mixed


def for_each_form(shape, slots, work):
    line = lax.axis_index("seq") // INNER
    spans = [
        slot[1:] if isinstance(slot, tuple) else (shape.away(slot), shape.outer)
        for slot in slots
    ]
    steps = sorted({0, shape.outer}.union(*spans))
    for least, below in zip(steps, steps[1:]):
        here = [i for i, span in enumerate(spans) if span[0] <= least < span[1]]
        pl.when((line >= least) & (line < below))(functools.partial(work, here))


def slot_numbers(slots):
    return [slot[0] if isinstance(slot, tuple) else slot for slot in slots]


def middle_kernel(shape, slots, mask_ref, q_ref, peak_ref, acc_in, *refs):
    del acc_in
    piece_refs, acc_ref = refs[:-1], refs[-1]
    numbers = slot_numbers(slots)

    def work(here):
        for h in range(shape.heads if here else 0):
            parts = parts_of(
                shape, [numbers[i] for i in here], h, mask_ref, [piece_refs[i] for i in here]
            )
            for b, start in tiles_of(shape):
                rows = pl.ds(b * shape.rows_unit + start, ROW_TILE)
                acc_ref[h, rows, :] += mixed_tile(shape, parts, h, b, rows, q_ref, peak_ref)

    for_each_form(shape, slots, work)


def last_kernel(shape, slots, n_lists, mask_ref, q_ref, peak_in, acc_in, *refs):
    del peak_in, acc_in
    heads, head_dim = shape.heads, shape.head_dim
    n, n_all = len(slots), shape.n_slots
    piece_refs, all_refs, list_refs = refs[:n], refs[n:n + n_all], refs[n + n_all:][:n_lists]
    out_ref, peak_ref, acc_ref, *scratch = refs[n + n_all + n_lists:]
    out_rows, out_tiles, worst, kv, allowed_ref, *lists, sems, out_sems = scratch
    seq_pos = lax.axis_index("seq")
    first_block = seq_pos * shape.blocks_here

    def finish(h, at, sums):
        total = sums[:, head_dim:]
        inverse = pl.reciprocal(total, approx=True)
        inverse = inverse * (2.0 - total * inverse)
        result = sums[:, :head_dim] * inverse
        if h + 1 < heads:
            out_rows[h, at] = result
        else:
            result = jnp.concatenate([out_rows[k, at] for k in range(h)] + [result], axis=1)
            out_tiles[at] = result.reshape(ROW_TILE * heads, head_dim).astype(out_tiles.dtype)
        bad = jnp.where(total < SAFE_TOTAL, 0.0, 1.0)
        worst[...] = jnp.maximum(
            worst[...], jnp.max(bad.reshape(ROW_TILE // 8, 8, head_dim), axis=0)
        )

    def finish_all(parts):
        copies = []
        for h in range(heads):
            for at, (b, start) in enumerate(tiles_of(shape)):
                rows = pl.ds(b * shape.rows_unit + start, ROW_TILE)
                sums = acc_ref[h, rows, :]
                if parts:
                    sums = sums + mixed_tile(shape, parts[h], h, b, rows, q_ref, peak_ref)
                finish(h, at, sums)
                if h + 1 < heads:
                    continue
                copies.append(
                    pltpu.make_async_copy(
                        out_tiles.at[at],
                        out_ref.at[pl.ds(rows.start * heads, ROW_TILE * heads), :],
                        out_sems.at[at],
                    )
                )
                copies[-1].start()
        for copy in copies:
            copy.wait()

    worst[...] = jnp.zeros_like(worst)
    numbers = slot_numbers(slots)
    for_each_form(
        shape, slots,
        lambda here: finish_all([
            parts_of(shape, [numbers[i] for i in here], h, mask_ref, [piece_refs[i] for i in here])
            for h in range(heads)
        ] if here else []),
    )

    @pl.when(jnp.max(worst[...]) > 0.0)
    def _():
        copies = read_lists(list_refs, lists, sems) + [
            pltpu.make_async_copy(all_refs[i], kv.at[i], sems.at[n_lists + i])
            for i in range(n_all)
        ]
        for copy in copies:
            copy.start()
        for copy in copies:
            copy.wait()
        mark_allowed(shape, *lists, allowed_ref)

        def every_tile(step):
            def slot_step(i, carry):
                owner = owner_of(shape, seq_pos, i)

                @pl.when((owner >= 0) & (owner <= seq_pos))
                def _():
                    for h in range(heads):
                        for b, start in tiles_of(shape):
                            rows = pl.ds(b * shape.rows_unit + start, ROW_TILE)
                            s = scores(q_ref[h, rows, :], kv[i, h]) * shape.factor
                            columns = []
                            for j in range(shape.blocks_here):
                                block = owner * shape.blocks_here + j
                                part = s[:, j * BLOCK:(j + 1) * BLOCK]
                                row = start + lax.broadcasted_iota(jnp.int32, part.shape, 0)
                                column = lax.broadcasted_iota(jnp.int32, part.shape, 1)
                                ahead = (first_block + b - block) * BLOCK
                                part = jnp.where(
                                    (column - ahead) * shape.group <= row, part, HIDDEN
                                )
                                seen = allowed_ref[h, b, block] > 0
                                columns.append(part + jnp.where(seen, 0.0, HIDDEN))
                            step(h, rows, jnp.concatenate(columns, axis=1), i)

                return carry

            lax.fori_loop(0, n_all, slot_step, 0)

        def widen(h, rows, s, i):
            m = jnp.max(s, axis=1, keepdims=True)
            peak_ref[h, rows, :] = jnp.maximum(peak_ref[h, rows, :], m)

        def collect(h, rows, s, i):
            m = peak_ref[h, rows, :]
            p = jnp.exp2(s - jnp.concatenate([m] * shape.blocks_here, axis=1))
            acc_ref[h, rows, :] += jnp.dot(
                p.astype(jnp.bfloat16), with_ones(kv[i, heads + h]),
                preferred_element_type=jnp.float32,
            )

        every_tile(widen)
        acc_ref[...] = jnp.zeros_like(acc_ref)
        every_tile(collect)
        finish_all([])


def per_device(
    n_seq, queries, keys, values, retrieval_ids, vertical_blocks, slash_offsets, sink_blocks,
    window_blocks,
):
    tokens_here, heads, width = queries.shape
    head_dim = keys.shape[2]
    group = width // head_dim
    blocks_here = tokens_here // BLOCK
    shape = Shape(heads, blocks_here, n_seq * blocks_here, group, head_dim, n_seq)
    outer = shape.outer

    vmem = pl.BlockSpec(memory_space=pltpu.VMEM)
    hbm = pl.BlockSpec(memory_space=pltpu.HBM)
    anywhere = pl.BlockSpec(memory_space=pl.ANY)
    mask_shape = jax.ShapeDtypeStruct(
        (heads, blocks_here, shape.block_total, head_dim), jnp.float32
    )
    q_shape = jax.ShapeDtypeStruct((heads, shape.rows, head_dim), jnp.bfloat16)
    peak_shape = jax.ShapeDtypeStruct((heads, shape.rows, head_dim), jnp.float32)
    acc_shape = jax.ShapeDtypeStruct((heads, shape.rows, 2 * head_dim), jnp.float32)
    allowed_scratch = pltpu.SMEM((heads, blocks_here, shape.block_total), jnp.int32)
    params = pltpu.CompilerParams(vmem_limit_bytes=16 << 20)
    cost = pl.CostEstimate(flops=1 << 20, transcendentals=0, bytes_accessed=1 << 10)

    own = jnp.concatenate(
        [jnp.transpose(keys, (1, 0, 2)), jnp.transpose(values, (1, 0, 2))], axis=0
    )
    q_raw = queries.reshape(tokens_here, heads, group, head_dim)
    q_raw = jnp.transpose(q_raw, (0, 2, 1, 3)).reshape(heads * shape.rows, head_dim)
    q_raw = pltpu.with_memory_space_constraint(q_raw, pltpu.HBM)
    lists = tuple(
        pltpu.with_memory_space_constraint(x, pltpu.HBM)
        for x in (retrieval_ids, vertical_blocks, slash_offsets, sink_blocks, window_blocks)
    )
    n_lists = len(lists)
    list_scratch = [pltpu.SMEM(x.shape, jnp.int32) for x in lists]

    def prepare(q_raw):
        return pl.pallas_call(
            functools.partial(prepare_kernel, shape, n_lists),
            out_shape=(mask_shape, q_shape),
            in_specs=[hbm] * (n_lists + 1),
            out_specs=(vmem, vmem),
            scratch_shapes=[
                pltpu.VMEM((heads * shape.rows, head_dim), jnp.bfloat16),
                pltpu.VMEM((heads * shape.rows, head_dim), jnp.float32),
                allowed_scratch,
                *list_scratch,
                pltpu.SemaphoreType.DMA((n_lists + 1,)),
            ],
            compiler_params=params,
            cost_estimate=cost,
        )(*lists, q_raw)

    def start_sums():
        return pl.pallas_call(
            functools.partial(own_kernel, shape),
            out_shape=(peak_shape, acc_shape),
            in_specs=[vmem] * 3,
            out_specs=(vmem, vmem),
            compiler_params=params,
            cost_estimate=cost,
        )(mask, q, own)

    def add(acc, slots, cost=cost):
        return pl.pallas_call(
            functools.partial(middle_kernel, shape, slots),
            out_shape=acc_shape,
            in_specs=[vmem] * (4 + len(slots)),
            out_specs=vmem,
            input_output_aliases={3: 0},
            compiler_params=params,
            cost_estimate=cost,
        )(mask, q, peak, acc, *[piece[slot] for slot in slot_numbers(slots)])

    def send(x, pairs):
        return lax.ppermute(x, "seq", pairs)

    def along(x, least, step=1, most=outer):
        return send(x, [
            (s, s + step * INNER) for s in range(n_seq)
            if least <= s // INNER < min(most, outer - step)
        ])

    def across(x, least):
        return send(x, [
            (s, s ^ 1) for s in range(n_seq)
            if s // INNER >= least and (least > 0 or s % INNER == 0)
        ])

    piece = {0: own}
    if outer == 4:
        first = [along(own, k, most=k + 1) for k in range(3)]
        piece[4] = send(own, [(s, s ^ 1) for s in range(n_seq) if s % INNER == 0 or s == 1])
        second = [None, along(first[0], 1, most=2), along(first[1], 2)]
        q_raw, first[0] = lax.optimization_barrier((q_raw, first[0]))
        mask, q = prepare(q_raw)
        piece[1] = first[0] + first[1] + first[2]
        piece[1], q = lax.optimization_barrier((piece[1], q))
        piece[5] = across(piece[1], 1)
        piece[7] = along(piece[4], 0, step=3, most=1)
        q, second[1], piece[4] = lax.optimization_barrier((q, second[1], piece[4]))
        piece[3] = along(second[1], 2)
        peak, acc = start_sums()
        piece[2] = second[1] + second[2]
        piece[6] = across(piece[2], 2)
        heavy = pl.CostEstimate(flops=1 << 36, transcendentals=0, bytes_accessed=1 << 10)
        acc = add(acc, [1, 4], heavy)
        acc = add(acc, [2, 5])
        acc = add(acc, [7])
        acc = add(acc, [(6, 3, 4)])
        last_slots = [3, (6, 2, 3)]
    else:
        mask, q = prepare(q_raw)
        peak, acc = start_sums()
        for step in range(outer):
            if step + 1 < outer:
                piece[step + 1] = along(piece[step], step)
            piece[outer + step] = across(piece[step], step)
            if step > 0:
                acc = add(acc, [step, outer + step - 1])
            if step + 1 < outer:
                piece[step + 1], acc = lax.optimization_barrier((piece[step + 1], acc))
        last_slots = [n_seq - 1]

    out, _, _ = pl.pallas_call(
        functools.partial(last_kernel, shape, last_slots, n_lists),
        out_shape=(
            jax.ShapeDtypeStruct((heads * shape.rows, head_dim), jnp.bfloat16),
            peak_shape,
            acc_shape,
        ),
        in_specs=[vmem] * (4 + len(last_slots)) + [anywhere] * n_seq + [hbm] * n_lists,
        out_specs=(hbm, vmem, vmem),
        input_output_aliases={2: 1, 3: 2},
        scratch_shapes=[
            pltpu.VMEM((heads - 1, shape.rows // ROW_TILE, ROW_TILE, head_dim), jnp.float32),
            pltpu.VMEM((shape.rows // ROW_TILE, heads * ROW_TILE, head_dim), jnp.bfloat16),
            pltpu.VMEM((8, head_dim), jnp.float32),
            pltpu.VMEM((n_seq,) + own.shape, jnp.bfloat16),
            allowed_scratch,
            *list_scratch,
            pltpu.SemaphoreType.DMA((n_lists + n_seq,)),
            pltpu.SemaphoreType.DMA((shape.rows // ROW_TILE,)),
        ],
        compiler_params=pltpu.CompilerParams(
            vmem_limit_bytes=(16 << 20) + 2 * n_seq * own.size
        ),
        cost_estimate=cost,
    )(
        mask, q, peak, acc, *[piece[slot] for slot in slot_numbers(last_slots)],
        *[piece[slot] for slot in range(n_seq)], *lists,
    )
    out = out.reshape(tokens_here, group, heads, head_dim)
    return jnp.transpose(out, (0, 2, 1, 3)).reshape(tokens_here, heads, width)


def solution(mesh):
    in_specs = (
        P("seq", "head", None),
        P("seq", "head", None),
        P("seq", "head", None),
        P(),
        P("seq", None, None),
        P("seq", None, None),
        P(),
        P(),
    )
    out_specs = P("seq", "head", None)
    return jax.shard_map(
        functools.partial(per_device, mesh.shape["seq"]),
        mesh=mesh, in_specs=in_specs, out_specs=out_specs, check_vma=False,
    )
```

```python
import functools
import math

import jax
import jax.numpy as jnp
from jax import lax
from jax.experimental import pallas as pl
from jax.experimental.pallas import tpu as pltpu
from jax.sharding import PartitionSpec as P

KV_HEADS = 8
BLOCK = 128
INNER = 2
ROW_TILE = 256
PIECES_AT_ONCE = 2
HIDDEN = -1e30
SAFE_TOTAL = 1e30


class Shape:
    def __init__(self, heads, blocks_here, block_total, group, head_dim, n_slots):
        self.heads = heads
        self.blocks_here = blocks_here
        self.block_total = block_total
        self.group = group
        self.head_dim = head_dim
        self.n_slots = n_slots
        self.outer = n_slots // INNER
        self.rows_unit = BLOCK * group
        self.rows = blocks_here * self.rows_unit
        self.factor = head_dim ** -0.5 * math.log2(math.e)

    def away(self, slot):
        return slot % self.outer


def owner_of(shape, seq_pos, slot):
    crossed = slot >= shape.outer
    line = seq_pos // INNER - jnp.where(crossed, slot - shape.outer, slot)
    place = seq_pos % INNER
    return line * INNER + jnp.where(crossed, 1 - place, place)


def scores(q, keys):
    return lax.dot_general(q, keys, (((1,), (1,)), ((), ())), preferred_element_type=jnp.float32)


def with_ones(vals):
    return jnp.concatenate([vals, jnp.ones_like(vals)], axis=1)


def tiles_of(shape):
    return [(b, r * ROW_TILE) for b in range(shape.blocks_here)
            for r in range(shape.rows_unit // ROW_TILE)]


def mark_allowed(shape, retr_ref, vert_ref, slash_ref, sink_ref, window_ref, allowed_ref):
    first_block = lax.axis_index("seq") * shape.blocks_here
    first_head = lax.axis_index("head") * shape.heads
    n_retr = retr_ref.shape[0]
    for h in range(shape.heads):
        head_id = first_head + h
        is_retr = functools.reduce(
            jnp.logical_or, [retr_ref[i] == head_id for i in range(n_retr)]
        )
        for b in range(shape.blocks_here):
            query_block = first_block + b
            sinks = jnp.where(is_retr, 0, sink_ref[head_id])
            lowest = query_block - jnp.where(is_retr, 1, window_ref[head_id])

            def clear(c, carry):
                read = ((c < sinks) | (c > lowest)) & (c <= query_block)
                allowed_ref[h, b, c] = read.astype(jnp.int32)
                return carry

            lax.fori_loop(0, shape.block_total, clear, 0, unroll=shape.block_total <= 16)
            for j in range(vert_ref.shape[2]):
                c = vert_ref[b, head_id, j]
                allowed_ref[h, b, jnp.where(is_retr, c, query_block)] = 1
            for j in range(slash_ref.shape[2]):
                c = query_block - slash_ref[b, head_id, j]
                allowed_ref[h, b, jnp.where(is_retr, c, query_block)] = 1


def read_lists(list_refs, lists, sems):
    return [pltpu.make_async_copy(list_refs[i], lists[i], sems.at[i]) for i in range(len(lists))]


def prepare_kernel(shape, n_lists, *refs):
    list_refs, q_raw_ref, mask_ref, q_ref = refs[:n_lists], *refs[n_lists:n_lists + 3]
    q_raw, wide, allowed_ref, *lists, sems = refs[n_lists + 3:]
    seq_pos = lax.axis_index("seq")
    copies = read_lists(list_refs, lists, sems)
    for copy in copies:
        copy.start()
    q_copy = pltpu.make_async_copy(q_raw_ref, q_raw, sems.at[n_lists])
    q_copy.start()
    for copy in copies + [q_copy]:
        copy.wait()
    mark_allowed(shape, *lists, allowed_ref)
    wide[...] = q_raw[...].astype(jnp.float32)
    for h in range(shape.heads):
        q_ref[h] = wide[pl.ds(h, shape.rows, stride=shape.heads), :].astype(q_ref.dtype)

    def fill_masks(slot, carry):
        owner = owner_of(shape, seq_pos, slot)
        there = (owner >= 0) & (owner <= seq_pos)
        base = jnp.where(there, owner, 0) * shape.blocks_here
        for h in range(shape.heads):
            for b in range(shape.blocks_here):
                for j in range(shape.blocks_here):
                    seen = there & (allowed_ref[h, b, base + j] > 0)
                    mask_ref[h, b, pl.ds(slot * shape.blocks_here + j, 1), :] = jnp.full(
                        (1, shape.head_dim), jnp.where(seen, 1.0, 0.0), jnp.float32
                    )
        return carry

    lax.fori_loop(0, shape.n_slots, fill_masks, 0, unroll=shape.n_slots <= 8)


def parts_of(shape, slots, h, mask_ref, piece_refs):
    parts = []
    for at in range(0, len(slots), PIECES_AT_ONCE):
        some_slots = slots[at:at + PIECES_AT_ONCE]
        some_refs = piece_refs[at:at + PIECES_AT_ONCE]
        vals = jnp.concatenate([ref[shape.heads + h] for ref in some_refs], axis=0)
        seen_vals = []
        for b in range(shape.blocks_here):
            masks = jnp.concatenate(
                [
                    jnp.broadcast_to(
                        mask_ref[h, b, pl.ds(slot * shape.blocks_here + j, 1), :],
                        (BLOCK, shape.head_dim),
                    )
                    for slot in some_slots for j in range(shape.blocks_here)
                ],
                axis=0,
            ).astype(jnp.bfloat16)
            seen_vals.append(jnp.concatenate([vals * masks, masks], axis=1))
        parts.append((jnp.concatenate([ref[h] for ref in some_refs], axis=0), seen_vals))
    return parts


def mixed_tile(shape, parts, h, b, rows, q_ref, peak_ref):
    q = q_ref[h, rows, :]
    m = peak_ref[h, rows, :]
    mixed = None
    for keys, seen_vals in parts:
        s = scores(q, keys) * shape.factor
        p = jnp.exp2(s - jnp.concatenate([m] * (s.shape[1] // m.shape[1]), axis=1))
        part = jnp.dot(p.astype(jnp.bfloat16), seen_vals[b], preferred_element_type=jnp.float32)
        mixed = part if mixed is None else mixed + part
    return mixed


def for_each_form(shape, slots, work):
    line = lax.axis_index("seq") // INNER
    spans = [
        slot[1:] if isinstance(slot, tuple) else (shape.away(slot), shape.outer)
        for slot in slots
    ]
    steps = sorted({0, shape.outer}.union(*spans))
    for least, below in zip(steps, steps[1:]):
        here = [i for i, span in enumerate(spans) if span[0] <= least < span[1]]
        pl.when((line >= least) & (line < below))(functools.partial(work, here))


def slot_numbers(slots):
    return [slot[0] if isinstance(slot, tuple) else slot for slot in slots]


def own_kernel(shape, slots, mask_ref, q_ref, own_ref, *refs):
    piece_refs, peak_ref, acc_ref = refs[:-2], refs[-2], refs[-1]

    def work(here):
        for h in range(shape.heads):
            parts = parts_of(
                shape, [slots[i] for i in here], h, mask_ref, [piece_refs[i] for i in here]
            )
            for b, start in tiles_of(shape):
                rows = pl.ds(b * shape.rows_unit + start, ROW_TILE)
                width = (b + 1) * BLOCK
                s = scores(q_ref[h, rows, :], own_ref[h, :width, :]) * shape.factor
                columns = []
                for j in range(b):
                    seen = mask_ref[h, b, pl.ds(j, 1), :]
                    columns.append(
                        jnp.where(seen > 0.0, s[:, j * BLOCK:(j + 1) * BLOCK], HIDDEN)
                    )
                diagonal = s[:, b * BLOCK:]
                row = start + lax.broadcasted_iota(jnp.int32, diagonal.shape, 0)
                column = lax.broadcasted_iota(jnp.int32, diagonal.shape, 1)
                columns.append(jnp.where(column * shape.group <= row, diagonal, HIDDEN))
                s = jnp.concatenate(columns, axis=1)
                m = jnp.max(s, axis=1, keepdims=True)
                peak_ref[h, rows, :] = jnp.broadcast_to(m, (ROW_TILE, BLOCK))
                p = jnp.exp2(s - m).astype(jnp.bfloat16)
                vals = with_ones(own_ref[shape.heads + h, :width, :])
                sums = jnp.dot(p, vals, preferred_element_type=jnp.float32)
                if parts:
                    sums += mixed_tile(shape, parts, h, b, rows, q_ref, peak_ref)
                acc_ref[h, rows, :] = sums

    for_each_form(shape, slots, work)


def middle_kernel(shape, slots, mask_ref, q_ref, peak_ref, acc_in, *refs):
    del acc_in
    piece_refs, acc_ref = refs[:-1], refs[-1]
    numbers = slot_numbers(slots)

    def work(here):
        for h in range(shape.heads if here else 0):
            parts = parts_of(
                shape, [numbers[i] for i in here], h, mask_ref, [piece_refs[i] for i in here]
            )
            for b, start in tiles_of(shape):
                rows = pl.ds(b * shape.rows_unit + start, ROW_TILE)
                acc_ref[h, rows, :] += mixed_tile(shape, parts, h, b, rows, q_ref, peak_ref)

    for_each_form(shape, slots, work)


def last_kernel(shape, slots, n_lists, mask_ref, q_ref, peak_in, acc_in, *refs):
    del peak_in, acc_in
    heads, head_dim = shape.heads, shape.head_dim
    n, n_all = len(slots), shape.n_slots
    piece_refs, all_refs, list_refs = refs[:n], refs[n:n + n_all], refs[n + n_all:][:n_lists]
    out_ref, peak_ref, acc_ref, *scratch = refs[n + n_all + n_lists:]
    out_rows, out_tiles, worst, kv, allowed_ref, *lists, sems, out_sems = scratch
    seq_pos = lax.axis_index("seq")
    first_block = seq_pos * shape.blocks_here

    def finish(h, at, sums):
        total = sums[:, head_dim:]
        inverse = pl.reciprocal(total, approx=True)
        inverse = inverse * (2.0 - total * inverse)
        result = sums[:, :head_dim] * inverse
        if h + 1 < heads:
            out_rows[h, at] = result
        else:
            result = jnp.concatenate([out_rows[k, at] for k in range(h)] + [result], axis=1)
            out_tiles[at] = result.reshape(ROW_TILE * heads, head_dim).astype(out_tiles.dtype)
        bad = jnp.where(total < SAFE_TOTAL, 0.0, 1.0)
        worst[...] = jnp.maximum(
            worst[...], jnp.max(bad.reshape(ROW_TILE // 8, 8, head_dim), axis=0)
        )

    def finish_all(parts):
        copies = []
        for h in range(heads):
            for at, (b, start) in enumerate(tiles_of(shape)):
                rows = pl.ds(b * shape.rows_unit + start, ROW_TILE)
                sums = acc_ref[h, rows, :]
                if parts:
                    sums = sums + mixed_tile(shape, parts[h], h, b, rows, q_ref, peak_ref)
                finish(h, at, sums)
                if h + 1 < heads:
                    continue
                copies.append(
                    pltpu.make_async_copy(
                        out_tiles.at[at],
                        out_ref.at[pl.ds(rows.start * heads, ROW_TILE * heads), :],
                        out_sems.at[at],
                    )
                )
                copies[-1].start()
        for copy in copies:
            copy.wait()

    worst[...] = jnp.zeros_like(worst)
    numbers = slot_numbers(slots)
    for_each_form(
        shape, slots,
        lambda here: finish_all([
            parts_of(shape, [numbers[i] for i in here], h, mask_ref, [piece_refs[i] for i in here])
            for h in range(heads)
        ] if here else []),
    )

    @pl.when(jnp.max(worst[...]) > 0.0)
    def _():
        copies = read_lists(list_refs, lists, sems) + [
            pltpu.make_async_copy(all_refs[i], kv.at[i], sems.at[n_lists + i])
            for i in range(n_all)
        ]
        for copy in copies:
            copy.start()
        for copy in copies:
            copy.wait()
        mark_allowed(shape, *lists, allowed_ref)

        def every_tile(step):
            def slot_step(i, carry):
                owner = owner_of(shape, seq_pos, i)

                @pl.when((owner >= 0) & (owner <= seq_pos))
                def _():
                    for h in range(heads):
                        for b, start in tiles_of(shape):
                            rows = pl.ds(b * shape.rows_unit + start, ROW_TILE)
                            s = scores(q_ref[h, rows, :], kv[i, h]) * shape.factor
                            columns = []
                            for j in range(shape.blocks_here):
                                block = owner * shape.blocks_here + j
                                part = s[:, j * BLOCK:(j + 1) * BLOCK]
                                row = start + lax.broadcasted_iota(jnp.int32, part.shape, 0)
                                column = lax.broadcasted_iota(jnp.int32, part.shape, 1)
                                ahead = (first_block + b - block) * BLOCK
                                part = jnp.where(
                                    (column - ahead) * shape.group <= row, part, HIDDEN
                                )
                                seen = allowed_ref[h, b, block] > 0
                                columns.append(part + jnp.where(seen, 0.0, HIDDEN))
                            step(h, rows, jnp.concatenate(columns, axis=1), i)

                return carry

            lax.fori_loop(0, n_all, slot_step, 0)

        def widen(h, rows, s, i):
            m = jnp.max(s, axis=1, keepdims=True)
            peak_ref[h, rows, :] = jnp.maximum(peak_ref[h, rows, :], m)

        def collect(h, rows, s, i):
            m = peak_ref[h, rows, :]
            p = jnp.exp2(s - jnp.concatenate([m] * shape.blocks_here, axis=1))
            acc_ref[h, rows, :] += jnp.dot(
                p.astype(jnp.bfloat16), with_ones(kv[i, heads + h]),
                preferred_element_type=jnp.float32,
            )

        every_tile(widen)
        acc_ref[...] = jnp.zeros_like(acc_ref)
        every_tile(collect)
        finish_all([])


def per_device(
    n_seq, queries, keys, values, retrieval_ids, vertical_blocks, slash_offsets, sink_blocks,
    window_blocks,
):
    tokens_here, heads, width = queries.shape
    head_dim = keys.shape[2]
    group = width // head_dim
    blocks_here = tokens_here // BLOCK
    shape = Shape(heads, blocks_here, n_seq * blocks_here, group, head_dim, n_seq)
    outer = shape.outer

    vmem = pl.BlockSpec(memory_space=pltpu.VMEM)
    hbm = pl.BlockSpec(memory_space=pltpu.HBM)
    anywhere = pl.BlockSpec(memory_space=pl.ANY)
    mask_shape = jax.ShapeDtypeStruct(
        (heads, blocks_here, shape.block_total, head_dim), jnp.float32
    )
    q_shape = jax.ShapeDtypeStruct((heads, shape.rows, head_dim), jnp.bfloat16)
    peak_shape = jax.ShapeDtypeStruct((heads, shape.rows, head_dim), jnp.float32)
    acc_shape = jax.ShapeDtypeStruct((heads, shape.rows, 2 * head_dim), jnp.float32)
    allowed_scratch = pltpu.SMEM((heads, blocks_here, shape.block_total), jnp.int32)
    params = pltpu.CompilerParams(vmem_limit_bytes=16 << 20)
    cost = pl.CostEstimate(flops=1 << 20, transcendentals=0, bytes_accessed=1 << 10)

    own = jnp.concatenate(
        [jnp.transpose(keys, (1, 0, 2)), jnp.transpose(values, (1, 0, 2))], axis=0
    )
    q_raw = queries.reshape(tokens_here, heads, group, head_dim)
    q_raw = jnp.transpose(q_raw, (0, 2, 1, 3)).reshape(heads * shape.rows, head_dim)
    q_raw = pltpu.with_memory_space_constraint(q_raw, pltpu.HBM)
    lists = tuple(
        pltpu.with_memory_space_constraint(x, pltpu.HBM)
        for x in (retrieval_ids, vertical_blocks, slash_offsets, sink_blocks, window_blocks)
    )
    n_lists = len(lists)
    list_scratch = [pltpu.SMEM(x.shape, jnp.int32) for x in lists]

    def prepare(q_raw):
        return pl.pallas_call(
            functools.partial(prepare_kernel, shape, n_lists),
            out_shape=(mask_shape, q_shape),
            in_specs=[hbm] * (n_lists + 1),
            out_specs=(vmem, vmem),
            scratch_shapes=[
                pltpu.VMEM((heads * shape.rows, head_dim), jnp.bfloat16),
                pltpu.VMEM((heads * shape.rows, head_dim), jnp.float32),
                allowed_scratch,
                *list_scratch,
                pltpu.SemaphoreType.DMA((n_lists + 1,)),
            ],
            compiler_params=params,
            cost_estimate=cost,
        )(*lists, q_raw)

    def start_sums(slots=(), cost=cost):
        return pl.pallas_call(
            functools.partial(own_kernel, shape, slots),
            out_shape=(peak_shape, acc_shape),
            in_specs=[vmem] * (3 + len(slots)),
            out_specs=(vmem, vmem),
            compiler_params=params,
            cost_estimate=cost,
        )(mask, q, own, *[piece[slot] for slot in slots])

    def add(acc, slots, cost=cost):
        return pl.pallas_call(
            functools.partial(middle_kernel, shape, slots),
            out_shape=acc_shape,
            in_specs=[vmem] * (4 + len(slots)),
            out_specs=vmem,
            input_output_aliases={3: 0},
            compiler_params=params,
            cost_estimate=cost,
        )(mask, q, peak, acc, *[piece[slot] for slot in slot_numbers(slots)])

    def send(x, pairs):
        return lax.ppermute(x, "seq", pairs)

    def along(x, least, step=1, most=outer):
        return send(x, [
            (s, s + step * INNER) for s in range(n_seq)
            if least <= s // INNER < min(most, outer - step)
        ])

    def across(x, least):
        return send(x, [
            (s, s ^ 1) for s in range(n_seq)
            if s // INNER >= least and (least > 0 or s % INNER == 0)
        ])

    piece = {0: own}
    if outer == 4:
        first = [along(own, k, most=k + 1) for k in range(3)]
        piece[4] = send(own, [(s, s ^ 1) for s in range(n_seq) if s % INNER == 0 or s == 1])
        second = [None, along(first[0], 1, most=2), along(first[1], 2)]
        q_raw, first[0] = lax.optimization_barrier((q_raw, first[0]))
        mask, q = prepare(q_raw)
        piece[1] = first[0] + first[1] + first[2]
        piece[1], q = lax.optimization_barrier((piece[1], q))
        piece[5] = across(piece[1], 1)
        piece[7] = along(piece[4], 0, step=3, most=1)
        q, second[1], piece[4] = lax.optimization_barrier((q, second[1], piece[4]))
        piece[3] = along(second[1], 2)
        piece[2] = second[1] + second[2]
        piece[6] = across(piece[2], 2)
        heavy = pl.CostEstimate(flops=1 << 36, transcendentals=0, bytes_accessed=1 << 10)
        peak, acc = start_sums([1, 4], heavy)
        acc = add(acc, [2, 5])
        acc = add(acc, [7, (6, 3, 4)])
        last_slots = [3, (6, 2, 3)]
    else:
        mask, q = prepare(q_raw)
        peak, acc = start_sums()
        for step in range(outer):
            if step + 1 < outer:
                piece[step + 1] = along(piece[step], step)
            piece[outer + step] = across(piece[step], step)
            if step > 0:
                acc = add(acc, [step, outer + step - 1])
            if step + 1 < outer:
                piece[step + 1], acc = lax.optimization_barrier((piece[step + 1], acc))
        last_slots = [n_seq - 1]

    out, _, _ = pl.pallas_call(
        functools.partial(last_kernel, shape, last_slots, n_lists),
        out_shape=(
            jax.ShapeDtypeStruct((heads * shape.rows, head_dim), jnp.bfloat16),
            peak_shape,
            acc_shape,
        ),
        in_specs=[vmem] * (4 + len(last_slots)) + [anywhere] * n_seq + [hbm] * n_lists,
        out_specs=(hbm, vmem, vmem),
        input_output_aliases={2: 1, 3: 2},
        scratch_shapes=[
            pltpu.VMEM((heads - 1, shape.rows // ROW_TILE, ROW_TILE, head_dim), jnp.float32),
            pltpu.VMEM((shape.rows // ROW_TILE, heads * ROW_TILE, head_dim), jnp.bfloat16),
            pltpu.VMEM((8, head_dim), jnp.float32),
            pltpu.VMEM((n_seq,) + own.shape, jnp.bfloat16),
            allowed_scratch,
            *list_scratch,
            pltpu.SemaphoreType.DMA((n_lists + n_seq,)),
            pltpu.SemaphoreType.DMA((shape.rows // ROW_TILE,)),
        ],
        compiler_params=pltpu.CompilerParams(
            vmem_limit_bytes=(16 << 20) + 2 * n_seq * own.size
        ),
        cost_estimate=cost,
    )(
        mask, q, peak, acc, *[piece[slot] for slot in slot_numbers(last_slots)],
        *[piece[slot] for slot in range(n_seq)], *lists,
    )
    out = out.reshape(tokens_here, group, heads, head_dim)
    return jnp.transpose(out, (0, 2, 1, 3)).reshape(tokens_here, heads, width)


def solution(mesh):
    in_specs = (
        P("seq", "head", None),
        P("seq", "head", None),
        P("seq", "head", None),
        P(),
        P("seq", None, None),
        P("seq", None, None),
        P(),
        P(),
    )
    out_specs = P("seq", "head", None)
    return jax.shard_map(
        functools.partial(per_device, mesh.shape["seq"]),
        mesh=mesh, in_specs=in_specs, out_specs=out_specs, check_vma=False,
    )
```

```python
import functools
import math

import jax
import jax.numpy as jnp
from jax import lax
from jax.experimental import pallas as pl
from jax.experimental.pallas import tpu as pltpu
from jax.sharding import PartitionSpec as P

KV_HEADS = 8
BLOCK = 128
INNER = 2
ROW_TILE = 512
PIECES_AT_ONCE = 2
HIDDEN = -1e30
SAFE_TOTAL = 1e30


class Shape:
    def __init__(self, heads, blocks_here, block_total, group, head_dim, n_slots):
        self.heads = heads
        self.blocks_here = blocks_here
        self.block_total = block_total
        self.group = group
        self.head_dim = head_dim
        self.n_slots = n_slots
        self.outer = n_slots // INNER
        self.rows_unit = BLOCK * group
        self.rows = blocks_here * self.rows_unit
        self.factor = head_dim ** -0.5 * math.log2(math.e)

    def away(self, slot):
        return slot % self.outer


def owner_of(shape, seq_pos, slot):
    crossed = slot >= shape.outer
    line = seq_pos // INNER - jnp.where(crossed, slot - shape.outer, slot)
    place = seq_pos % INNER
    return line * INNER + jnp.where(crossed, 1 - place, place)


def scores(q, keys):
    return lax.dot_general(q, keys, (((1,), (1,)), ((), ())), preferred_element_type=jnp.float32)


def with_ones(vals):
    return jnp.concatenate([vals, jnp.ones_like(vals)], axis=1)


def tiles_of(shape):
    return [(b, r * ROW_TILE) for b in range(shape.blocks_here)
            for r in range(shape.rows_unit // ROW_TILE)]


def mark_allowed(shape, retr_ref, vert_ref, slash_ref, sink_ref, window_ref, allowed_ref):
    first_block = lax.axis_index("seq") * shape.blocks_here
    first_head = lax.axis_index("head") * shape.heads
    n_retr = retr_ref.shape[0]
    for h in range(shape.heads):
        head_id = first_head + h
        is_retr = functools.reduce(
            jnp.logical_or, [retr_ref[i] == head_id for i in range(n_retr)]
        )
        for b in range(shape.blocks_here):
            query_block = first_block + b
            sinks = jnp.where(is_retr, 0, sink_ref[head_id])
            lowest = query_block - jnp.where(is_retr, 1, window_ref[head_id])

            def clear(c, carry):
                read = ((c < sinks) | (c > lowest)) & (c <= query_block)
                allowed_ref[h, b, c] = read.astype(jnp.int32)
                return carry

            lax.fori_loop(0, shape.block_total, clear, 0, unroll=shape.block_total <= 16)
            for j in range(vert_ref.shape[2]):
                c = vert_ref[b, head_id, j]
                allowed_ref[h, b, jnp.where(is_retr, c, query_block)] = 1
            for j in range(slash_ref.shape[2]):
                c = query_block - slash_ref[b, head_id, j]
                allowed_ref[h, b, jnp.where(is_retr, c, query_block)] = 1


def read_lists(list_refs, lists, sems):
    return [pltpu.make_async_copy(list_refs[i], lists[i], sems.at[i]) for i in range(len(lists))]


def prepare_kernel(shape, n_lists, *refs):
    list_refs, q_raw_ref, mask_ref, q_ref = refs[:n_lists], *refs[n_lists:n_lists + 3]
    q_raw, wide, allowed_ref, *lists, sems = refs[n_lists + 3:]
    seq_pos = lax.axis_index("seq")
    copies = read_lists(list_refs, lists, sems)
    for copy in copies:
        copy.start()
    q_copy = pltpu.make_async_copy(q_raw_ref, q_raw, sems.at[n_lists])
    q_copy.start()
    for copy in copies + [q_copy]:
        copy.wait()
    mark_allowed(shape, *lists, allowed_ref)
    wide[...] = q_raw[...].astype(jnp.float32)
    for h in range(shape.heads):
        q_ref[h] = wide[pl.ds(h, shape.rows, stride=shape.heads), :].astype(q_ref.dtype)

    def fill_masks(slot, carry):
        owner = owner_of(shape, seq_pos, slot)
        there = (owner >= 0) & (owner <= seq_pos)
        base = jnp.where(there, owner, 0) * shape.blocks_here
        for h in range(shape.heads):
            for b in range(shape.blocks_here):
                for j in range(shape.blocks_here):
                    seen = there & (allowed_ref[h, b, base + j] > 0)
                    mask_ref[h, b, pl.ds(slot * shape.blocks_here + j, 1), :] = jnp.full(
                        (1, shape.head_dim), jnp.where(seen, 1.0, 0.0), jnp.float32
                    )
        return carry

    lax.fori_loop(0, shape.n_slots, fill_masks, 0, unroll=shape.n_slots <= 8)


def parts_of(shape, slots, h, mask_ref, piece_refs):
    parts = []
    for at in range(0, len(slots), PIECES_AT_ONCE):
        some_slots = slots[at:at + PIECES_AT_ONCE]
        some_refs = piece_refs[at:at + PIECES_AT_ONCE]
        vals = jnp.concatenate([ref[shape.heads + h] for ref in some_refs], axis=0)
        seen_vals = []
        for b in range(shape.blocks_here):
            masks = jnp.concatenate(
                [
                    jnp.broadcast_to(
                        mask_ref[h, b, pl.ds(slot * shape.blocks_here + j, 1), :],
                        (BLOCK, shape.head_dim),
                    )
                    for slot in some_slots for j in range(shape.blocks_here)
                ],
                axis=0,
            ).astype(jnp.bfloat16)
            seen_vals.append(jnp.concatenate([vals * masks, masks], axis=1))
        parts.append((jnp.concatenate([ref[h] for ref in some_refs], axis=0), seen_vals))
    return parts


def mixed_tile(shape, parts, h, b, rows, q_ref, peak_ref):
    q = q_ref[h, rows, :]
    m = peak_ref[h, rows, :]
    mixed = None
    for keys, seen_vals in parts:
        s = scores(q, keys) * shape.factor
        p = jnp.exp2(s - jnp.concatenate([m] * (s.shape[1] // m.shape[1]), axis=1))
        part = jnp.dot(p.astype(jnp.bfloat16), seen_vals[b], preferred_element_type=jnp.float32)
        mixed = part if mixed is None else mixed + part
    return mixed


def for_each_form(shape, slots, work):
    line = lax.axis_index("seq") // INNER
    spans = [
        slot[1:] if isinstance(slot, tuple) else (shape.away(slot), shape.outer)
        for slot in slots
    ]
    steps = sorted({0, shape.outer}.union(*spans))
    for least, below in zip(steps, steps[1:]):
        here = [i for i, span in enumerate(spans) if span[0] <= least < span[1]]
        pl.when((line >= least) & (line < below))(functools.partial(work, here))


def slot_numbers(slots):
    return [slot[0] if isinstance(slot, tuple) else slot for slot in slots]


def own_kernel(shape, slots, mask_ref, q_ref, own_ref, *refs):
    piece_refs, peak_ref, acc_ref = refs[:-2], refs[-2], refs[-1]

    def work(here):
        for h in range(shape.heads):
            parts = parts_of(
                shape, [slots[i] for i in here], h, mask_ref, [piece_refs[i] for i in here]
            )
            for b, start in tiles_of(shape):
                rows = pl.ds(b * shape.rows_unit + start, ROW_TILE)
                width = (b + 1) * BLOCK
                s = scores(q_ref[h, rows, :], own_ref[h, :width, :]) * shape.factor
                columns = []
                for j in range(b):
                    seen = mask_ref[h, b, pl.ds(j, 1), :]
                    columns.append(
                        jnp.where(seen > 0.0, s[:, j * BLOCK:(j + 1) * BLOCK], HIDDEN)
                    )
                diagonal = s[:, b * BLOCK:]
                row = start + lax.broadcasted_iota(jnp.int32, diagonal.shape, 0)
                column = lax.broadcasted_iota(jnp.int32, diagonal.shape, 1)
                columns.append(jnp.where(column * shape.group <= row, diagonal, HIDDEN))
                s = jnp.concatenate(columns, axis=1)
                m = jnp.max(s, axis=1, keepdims=True)
                peak_ref[h, rows, :] = jnp.broadcast_to(m, (ROW_TILE, BLOCK))
                p = jnp.exp2(s - m).astype(jnp.bfloat16)
                vals = with_ones(own_ref[shape.heads + h, :width, :])
                sums = jnp.dot(p, vals, preferred_element_type=jnp.float32)
                if parts:
                    sums += mixed_tile(shape, parts, h, b, rows, q_ref, peak_ref)
                acc_ref[h, rows, :] = sums

    for_each_form(shape, slots, work)


def middle_kernel(shape, slots, mask_ref, q_ref, peak_ref, acc_in, *refs):
    del acc_in
    piece_refs, acc_ref = refs[:-1], refs[-1]
    numbers = slot_numbers(slots)

    def work(here):
        for h in range(shape.heads if here else 0):
            parts = parts_of(
                shape, [numbers[i] for i in here], h, mask_ref, [piece_refs[i] for i in here]
            )
            for b, start in tiles_of(shape):
                rows = pl.ds(b * shape.rows_unit + start, ROW_TILE)
                acc_ref[h, rows, :] += mixed_tile(shape, parts, h, b, rows, q_ref, peak_ref)

    for_each_form(shape, slots, work)


def last_kernel(shape, slots, n_lists, mask_ref, q_ref, peak_in, acc_in, *refs):
    del peak_in, acc_in
    heads, head_dim = shape.heads, shape.head_dim
    n, n_all = len(slots), shape.n_slots
    piece_refs, all_refs, list_refs = refs[:n], refs[n:n + n_all], refs[n + n_all:][:n_lists]
    out_ref, peak_ref, acc_ref, *scratch = refs[n + n_all + n_lists:]
    out_rows, out_tiles, worst, kv, allowed_ref, *lists, sems, out_sems = scratch
    seq_pos = lax.axis_index("seq")
    first_block = seq_pos * shape.blocks_here

    def finish(h, at, sums):
        total = sums[:, head_dim:]
        inverse = pl.reciprocal(total, approx=True)
        inverse = inverse * (2.0 - total * inverse)
        result = sums[:, :head_dim] * inverse
        if h + 1 < heads:
            out_rows[h, at] = result
        else:
            result = jnp.concatenate([out_rows[k, at] for k in range(h)] + [result], axis=1)
            out_tiles[at] = result.reshape(ROW_TILE * heads, head_dim).astype(out_tiles.dtype)
        bad = jnp.where(total < SAFE_TOTAL, 0.0, 1.0)
        worst[...] = jnp.maximum(
            worst[...], jnp.max(bad.reshape(ROW_TILE // 8, 8, head_dim), axis=0)
        )

    def finish_all(parts):
        copies = []
        for h in range(heads):
            for at, (b, start) in enumerate(tiles_of(shape)):
                rows = pl.ds(b * shape.rows_unit + start, ROW_TILE)
                sums = acc_ref[h, rows, :]
                if parts:
                    sums = sums + mixed_tile(shape, parts[h], h, b, rows, q_ref, peak_ref)
                finish(h, at, sums)
                if h + 1 < heads:
                    continue
                copies.append(
                    pltpu.make_async_copy(
                        out_tiles.at[at],
                        out_ref.at[pl.ds(rows.start * heads, ROW_TILE * heads), :],
                        out_sems.at[at],
                    )
                )
                copies[-1].start()
        for copy in copies:
            copy.wait()

    worst[...] = jnp.zeros_like(worst)
    numbers = slot_numbers(slots)
    for_each_form(
        shape, slots,
        lambda here: finish_all([
            parts_of(shape, [numbers[i] for i in here], h, mask_ref, [piece_refs[i] for i in here])
            for h in range(heads)
        ] if here else []),
    )

    @pl.when(jnp.max(worst[...]) > 0.0)
    def _():
        copies = read_lists(list_refs, lists, sems) + [
            pltpu.make_async_copy(all_refs[i], kv.at[i], sems.at[n_lists + i])
            for i in range(n_all)
        ]
        for copy in copies:
            copy.start()
        for copy in copies:
            copy.wait()
        mark_allowed(shape, *lists, allowed_ref)

        def every_tile(step):
            def slot_step(i, carry):
                owner = owner_of(shape, seq_pos, i)

                @pl.when((owner >= 0) & (owner <= seq_pos))
                def _():
                    for h in range(heads):
                        for b, start in tiles_of(shape):
                            rows = pl.ds(b * shape.rows_unit + start, ROW_TILE)
                            s = scores(q_ref[h, rows, :], kv[i, h]) * shape.factor
                            columns = []
                            for j in range(shape.blocks_here):
                                block = owner * shape.blocks_here + j
                                part = s[:, j * BLOCK:(j + 1) * BLOCK]
                                row = start + lax.broadcasted_iota(jnp.int32, part.shape, 0)
                                column = lax.broadcasted_iota(jnp.int32, part.shape, 1)
                                ahead = (first_block + b - block) * BLOCK
                                part = jnp.where(
                                    (column - ahead) * shape.group <= row, part, HIDDEN
                                )
                                seen = allowed_ref[h, b, block] > 0
                                columns.append(part + jnp.where(seen, 0.0, HIDDEN))
                            step(h, rows, jnp.concatenate(columns, axis=1), i)

                return carry

            lax.fori_loop(0, n_all, slot_step, 0)

        def widen(h, rows, s, i):
            m = jnp.max(s, axis=1, keepdims=True)
            peak_ref[h, rows, :] = jnp.maximum(peak_ref[h, rows, :], m)

        def collect(h, rows, s, i):
            m = peak_ref[h, rows, :]
            p = jnp.exp2(s - jnp.concatenate([m] * shape.blocks_here, axis=1))
            acc_ref[h, rows, :] += jnp.dot(
                p.astype(jnp.bfloat16), with_ones(kv[i, heads + h]),
                preferred_element_type=jnp.float32,
            )

        every_tile(widen)
        acc_ref[...] = jnp.zeros_like(acc_ref)
        every_tile(collect)
        finish_all([])


def per_device(
    n_seq, queries, keys, values, retrieval_ids, vertical_blocks, slash_offsets, sink_blocks,
    window_blocks,
):
    tokens_here, heads, width = queries.shape
    head_dim = keys.shape[2]
    group = width // head_dim
    blocks_here = tokens_here // BLOCK
    shape = Shape(heads, blocks_here, n_seq * blocks_here, group, head_dim, n_seq)
    outer = shape.outer

    vmem = pl.BlockSpec(memory_space=pltpu.VMEM)
    hbm = pl.BlockSpec(memory_space=pltpu.HBM)
    anywhere = pl.BlockSpec(memory_space=pl.ANY)
    mask_shape = jax.ShapeDtypeStruct(
        (heads, blocks_here, shape.block_total, head_dim), jnp.float32
    )
    q_shape = jax.ShapeDtypeStruct((heads, shape.rows, head_dim), jnp.bfloat16)
    peak_shape = jax.ShapeDtypeStruct((heads, shape.rows, head_dim), jnp.float32)
    acc_shape = jax.ShapeDtypeStruct((heads, shape.rows, 2 * head_dim), jnp.float32)
    allowed_scratch = pltpu.SMEM((heads, blocks_here, shape.block_total), jnp.int32)
    params = pltpu.CompilerParams(vmem_limit_bytes=16 << 20)
    cost = pl.CostEstimate(flops=1 << 20, transcendentals=0, bytes_accessed=1 << 10)

    own = jnp.concatenate(
        [jnp.transpose(keys, (1, 0, 2)), jnp.transpose(values, (1, 0, 2))], axis=0
    )
    q_raw = queries.reshape(tokens_here, heads, group, head_dim)
    q_raw = jnp.transpose(q_raw, (0, 2, 1, 3)).reshape(heads * shape.rows, head_dim)
    q_raw = pltpu.with_memory_space_constraint(q_raw, pltpu.HBM)
    lists = tuple(
        pltpu.with_memory_space_constraint(x, pltpu.HBM)
        for x in (retrieval_ids, vertical_blocks, slash_offsets, sink_blocks, window_blocks)
    )
    n_lists = len(lists)
    list_scratch = [pltpu.SMEM(x.shape, jnp.int32) for x in lists]

    def prepare(q_raw):
        return pl.pallas_call(
            functools.partial(prepare_kernel, shape, n_lists),
            out_shape=(mask_shape, q_shape),
            in_specs=[hbm] * (n_lists + 1),
            out_specs=(vmem, vmem),
            scratch_shapes=[
                pltpu.VMEM((heads * shape.rows, head_dim), jnp.bfloat16),
                pltpu.VMEM((heads * shape.rows, head_dim), jnp.float32),
                allowed_scratch,
                *list_scratch,
                pltpu.SemaphoreType.DMA((n_lists + 1,)),
            ],
            compiler_params=params,
            cost_estimate=cost,
        )(*lists, q_raw)

    def start_sums(slots=(), cost=cost):
        return pl.pallas_call(
            functools.partial(own_kernel, shape, slots),
            out_shape=(peak_shape, acc_shape),
            in_specs=[vmem] * (3 + len(slots)),
            out_specs=(vmem, vmem),
            compiler_params=params,
            cost_estimate=cost,
        )(mask, q, own, *[piece[slot] for slot in slots])

    def add(acc, slots, cost=cost):
        return pl.pallas_call(
            functools.partial(middle_kernel, shape, slots),
            out_shape=acc_shape,
            in_specs=[vmem] * (4 + len(slots)),
            out_specs=vmem,
            input_output_aliases={3: 0},
            compiler_params=params,
            cost_estimate=cost,
        )(mask, q, peak, acc, *[piece[slot] for slot in slot_numbers(slots)])

    def send(x, pairs):
        return lax.ppermute(x, "seq", pairs)

    def along(x, least, step=1, most=outer):
        return send(x, [
            (s, s + step * INNER) for s in range(n_seq)
            if least <= s // INNER < min(most, outer - step)
        ])

    def across(x, least):
        return send(x, [
            (s, s ^ 1) for s in range(n_seq)
            if s // INNER >= least and (least > 0 or s % INNER == 0)
        ])

    piece = {0: own}
    if outer == 4:
        first = [along(own, k, most=k + 1) for k in range(3)]
        piece[4] = send(own, [(s, s ^ 1) for s in range(n_seq) if s % INNER == 0 or s == 1])
        second = [None, along(first[0], 1, most=2), along(first[1], 2)]
        q_raw, first[0] = lax.optimization_barrier((q_raw, first[0]))
        mask, q = prepare(q_raw)
        piece[1] = first[0] + first[1] + first[2]
        piece[1], q = lax.optimization_barrier((piece[1], q))
        piece[5] = across(piece[1], 1)
        piece[7] = along(piece[4], 0, step=3, most=1)
        q, second[1], piece[4] = lax.optimization_barrier((q, second[1], piece[4]))
        piece[3] = along(second[1], 2)
        piece[2] = second[1] + second[2]
        piece[6] = across(piece[2], 2)
        heavy = pl.CostEstimate(flops=1 << 36, transcendentals=0, bytes_accessed=1 << 10)
        peak, acc = start_sums([1, 4], heavy)
        acc = add(acc, [2, 5])
        acc = add(acc, [7, (6, 3, 4)])
        last_slots = [3, (6, 2, 3)]
    else:
        mask, q = prepare(q_raw)
        peak, acc = start_sums()
        for step in range(outer):
            if step + 1 < outer:
                piece[step + 1] = along(piece[step], step)
            piece[outer + step] = across(piece[step], step)
            if step > 0:
                acc = add(acc, [step, outer + step - 1])
            if step + 1 < outer:
                piece[step + 1], acc = lax.optimization_barrier((piece[step + 1], acc))
        last_slots = [n_seq - 1]

    out, _, _ = pl.pallas_call(
        functools.partial(last_kernel, shape, last_slots, n_lists),
        out_shape=(
            jax.ShapeDtypeStruct((heads * shape.rows, head_dim), jnp.bfloat16),
            peak_shape,
            acc_shape,
        ),
        in_specs=[vmem] * (4 + len(last_slots)) + [anywhere] * n_seq + [hbm] * n_lists,
        out_specs=(hbm, vmem, vmem),
        input_output_aliases={2: 1, 3: 2},
        scratch_shapes=[
            pltpu.VMEM((heads - 1, shape.rows // ROW_TILE, ROW_TILE, head_dim), jnp.float32),
            pltpu.VMEM((shape.rows // ROW_TILE, heads * ROW_TILE, head_dim), jnp.bfloat16),
            pltpu.VMEM((8, head_dim), jnp.float32),
            pltpu.VMEM((n_seq,) + own.shape, jnp.bfloat16),
            allowed_scratch,
            *list_scratch,
            pltpu.SemaphoreType.DMA((n_lists + n_seq,)),
            pltpu.SemaphoreType.DMA((shape.rows // ROW_TILE,)),
        ],
        compiler_params=pltpu.CompilerParams(
            vmem_limit_bytes=(16 << 20) + 2 * n_seq * own.size
        ),
        cost_estimate=cost,
    )(
        mask, q, peak, acc, *[piece[slot] for slot in slot_numbers(last_slots)],
        *[piece[slot] for slot in range(n_seq)], *lists,
    )
    out = out.reshape(tokens_here, group, heads, head_dim)
    return jnp.transpose(out, (0, 2, 1, 3)).reshape(tokens_here, heads, width)


def solution(mesh):
    in_specs = (
        P("seq", "head", None),
        P("seq", "head", None),
        P("seq", "head", None),
        P(),
        P("seq", None, None),
        P("seq", None, None),
        P(),
        P(),
    )
    out_specs = P("seq", "head", None)
    return jax.shard_map(
        functools.partial(per_device, mesh.shape["seq"]),
        mesh=mesh, in_specs=in_specs, out_specs=out_specs, check_vma=False,
    )
```

```python
import functools
import math

import jax
import jax.numpy as jnp
from jax import lax
from jax.experimental import pallas as pl
from jax.experimental.pallas import tpu as pltpu
from jax.sharding import PartitionSpec as P

KV_HEADS = 8
BLOCK = 128
INNER = 2
ROW_TILE = 1024
PIECES_AT_ONCE = 2
HIDDEN = -1e30
SAFE_TOTAL = 1e30


class Shape:
    def __init__(self, heads, blocks_here, block_total, group, head_dim, n_slots):
        self.heads = heads
        self.blocks_here = blocks_here
        self.block_total = block_total
        self.group = group
        self.head_dim = head_dim
        self.n_slots = n_slots
        self.outer = n_slots // INNER
        self.rows_unit = BLOCK * group
        self.rows = blocks_here * self.rows_unit
        self.factor = head_dim ** -0.5 * math.log2(math.e)

    def away(self, slot):
        return slot % self.outer


def owner_of(shape, seq_pos, slot):
    crossed = slot >= shape.outer
    line = seq_pos // INNER - jnp.where(crossed, slot - shape.outer, slot)
    place = seq_pos % INNER
    return line * INNER + jnp.where(crossed, 1 - place, place)


def scores(q, keys):
    return lax.dot_general(q, keys, (((1,), (1,)), ((), ())), preferred_element_type=jnp.float32)


def with_ones(vals):
    return jnp.concatenate([vals, jnp.ones_like(vals)], axis=1)


def tiles_of(shape):
    return [(b, r * ROW_TILE) for b in range(shape.blocks_here)
            for r in range(shape.rows_unit // ROW_TILE)]


def mark_allowed(shape, retr_ref, vert_ref, slash_ref, sink_ref, window_ref, allowed_ref):
    first_block = lax.axis_index("seq") * shape.blocks_here
    first_head = lax.axis_index("head") * shape.heads
    n_retr = retr_ref.shape[0]
    for h in range(shape.heads):
        head_id = first_head + h
        is_retr = functools.reduce(
            jnp.logical_or, [retr_ref[i] == head_id for i in range(n_retr)]
        )
        for b in range(shape.blocks_here):
            query_block = first_block + b
            sinks = jnp.where(is_retr, 0, sink_ref[head_id])
            lowest = query_block - jnp.where(is_retr, 1, window_ref[head_id])

            def clear(c, carry):
                read = ((c < sinks) | (c > lowest)) & (c <= query_block)
                allowed_ref[h, b, c] = read.astype(jnp.int32)
                return carry

            lax.fori_loop(0, shape.block_total, clear, 0, unroll=shape.block_total <= 16)
            for j in range(vert_ref.shape[2]):
                c = vert_ref[b, head_id, j]
                allowed_ref[h, b, jnp.where(is_retr, c, query_block)] = 1
            for j in range(slash_ref.shape[2]):
                c = query_block - slash_ref[b, head_id, j]
                allowed_ref[h, b, jnp.where(is_retr, c, query_block)] = 1


def read_lists(list_refs, lists, sems):
    return [pltpu.make_async_copy(list_refs[i], lists[i], sems.at[i]) for i in range(len(lists))]


def prepare_kernel(shape, n_lists, *refs):
    list_refs, q_raw_ref, mask_ref, q_ref = refs[:n_lists], *refs[n_lists:n_lists + 3]
    q_raw, wide, allowed_ref, *lists, sems = refs[n_lists + 3:]
    seq_pos = lax.axis_index("seq")
    copies = read_lists(list_refs, lists, sems)
    for copy in copies:
        copy.start()
    q_copy = pltpu.make_async_copy(q_raw_ref, q_raw, sems.at[n_lists])
    q_copy.start()
    for copy in copies + [q_copy]:
        copy.wait()
    mark_allowed(shape, *lists, allowed_ref)
    wide[...] = q_raw[...].astype(jnp.float32)
    for h in range(shape.heads):
        q_ref[h] = wide[pl.ds(h, shape.rows, stride=shape.heads), :].astype(q_ref.dtype)

    def fill_masks(slot, carry):
        owner = owner_of(shape, seq_pos, slot)
        there = (owner >= 0) & (owner <= seq_pos)
        base = jnp.where(there, owner, 0) * shape.blocks_here
        for h in range(shape.heads):
            for b in range(shape.blocks_here):
                for j in range(shape.blocks_here):
                    seen = there & (allowed_ref[h, b, base + j] > 0)
                    mask_ref[h, b, pl.ds(slot * shape.blocks_here + j, 1), :] = jnp.full(
                        (1, shape.head_dim), jnp.where(seen, 1.0, 0.0), jnp.float32
                    )
        return carry

    lax.fori_loop(0, shape.n_slots, fill_masks, 0, unroll=shape.n_slots <= 8)


def parts_of(shape, slots, h, mask_ref, piece_refs):
    parts = []
    for at in range(0, len(slots), PIECES_AT_ONCE):
        some_slots = slots[at:at + PIECES_AT_ONCE]
        some_refs = piece_refs[at:at + PIECES_AT_ONCE]
        vals = jnp.concatenate([ref[shape.heads + h] for ref in some_refs], axis=0)
        seen_vals = []
        for b in range(shape.blocks_here):
            masks = jnp.concatenate(
                [
                    jnp.broadcast_to(
                        mask_ref[h, b, pl.ds(slot * shape.blocks_here + j, 1), :],
                        (BLOCK, shape.head_dim),
                    )
                    for slot in some_slots for j in range(shape.blocks_here)
                ],
                axis=0,
            ).astype(jnp.bfloat16)
            seen_vals.append(jnp.concatenate([vals * masks, masks], axis=1))
        parts.append((jnp.concatenate([ref[h] for ref in some_refs], axis=0), seen_vals))
    return parts


def mixed_tile(shape, parts, h, b, rows, q_ref, peak_ref):
    q = q_ref[h, rows, :]
    m = peak_ref[h, rows, :]
    mixed = None
    for keys, seen_vals in parts:
        s = scores(q, keys) * shape.factor
        p = jnp.exp2(s - jnp.concatenate([m] * (s.shape[1] // m.shape[1]), axis=1))
        part = jnp.dot(p.astype(jnp.bfloat16), seen_vals[b], preferred_element_type=jnp.float32)
        mixed = part if mixed is None else mixed + part
    return mixed


def for_each_form(shape, slots, work):
    line = lax.axis_index("seq") // INNER
    spans = [
        slot[1:] if isinstance(slot, tuple) else (shape.away(slot), shape.outer)
        for slot in slots
    ]
    steps = sorted({0, shape.outer}.union(*spans))
    for least, below in zip(steps, steps[1:]):
        here = [i for i, span in enumerate(spans) if span[0] <= least < span[1]]
        pl.when((line >= least) & (line < below))(functools.partial(work, here))


def slot_numbers(slots):
    return [slot[0] if isinstance(slot, tuple) else slot for slot in slots]


def own_kernel(shape, slots, mask_ref, q_ref, own_ref, *refs):
    piece_refs, peak_ref, acc_ref = refs[:-2], refs[-2], refs[-1]

    def work(here):
        for h in range(shape.heads):
            parts = parts_of(
                shape, [slots[i] for i in here], h, mask_ref, [piece_refs[i] for i in here]
            )
            for b, start in tiles_of(shape):
                rows = pl.ds(b * shape.rows_unit + start, ROW_TILE)
                width = (b + 1) * BLOCK
                s = scores(q_ref[h, rows, :], own_ref[h, :width, :]) * shape.factor
                columns = []
                for j in range(b):
                    seen = mask_ref[h, b, pl.ds(j, 1), :]
                    columns.append(
                        jnp.where(seen > 0.0, s[:, j * BLOCK:(j + 1) * BLOCK], HIDDEN)
                    )
                diagonal = s[:, b * BLOCK:]
                row = start + lax.broadcasted_iota(jnp.int32, diagonal.shape, 0)
                column = lax.broadcasted_iota(jnp.int32, diagonal.shape, 1)
                columns.append(jnp.where(column * shape.group <= row, diagonal, HIDDEN))
                s = jnp.concatenate(columns, axis=1)
                m = jnp.max(s, axis=1, keepdims=True)
                peak_ref[h, rows, :] = jnp.broadcast_to(m, (ROW_TILE, BLOCK))
                p = jnp.exp2(s - m).astype(jnp.bfloat16)
                vals = with_ones(own_ref[shape.heads + h, :width, :])
                sums = jnp.dot(p, vals, preferred_element_type=jnp.float32)
                if parts:
                    sums += mixed_tile(shape, parts, h, b, rows, q_ref, peak_ref)
                acc_ref[h, rows, :] = sums

    for_each_form(shape, slots, work)


def middle_kernel(shape, slots, mask_ref, q_ref, peak_ref, acc_in, *refs):
    del acc_in
    piece_refs, acc_ref = refs[:-1], refs[-1]
    numbers = slot_numbers(slots)

    def work(here):
        for h in range(shape.heads if here else 0):
            parts = parts_of(
                shape, [numbers[i] for i in here], h, mask_ref, [piece_refs[i] for i in here]
            )
            for b, start in tiles_of(shape):
                rows = pl.ds(b * shape.rows_unit + start, ROW_TILE)
                acc_ref[h, rows, :] += mixed_tile(shape, parts, h, b, rows, q_ref, peak_ref)

    for_each_form(shape, slots, work)


def last_kernel(shape, slots, n_lists, mask_ref, q_ref, peak_in, acc_in, *refs):
    del peak_in, acc_in
    heads, head_dim = shape.heads, shape.head_dim
    n, n_all = len(slots), shape.n_slots
    piece_refs, all_refs, list_refs = refs[:n], refs[n:n + n_all], refs[n + n_all:][:n_lists]
    out_ref, peak_ref, acc_ref, *scratch = refs[n + n_all + n_lists:]
    out_rows, out_tiles, worst, kv, allowed_ref, *lists, sems, out_sems = scratch
    seq_pos = lax.axis_index("seq")
    first_block = seq_pos * shape.blocks_here

    def finish(h, at, sums):
        total = sums[:, head_dim:]
        inverse = pl.reciprocal(total, approx=True)
        inverse = inverse * (2.0 - total * inverse)
        result = sums[:, :head_dim] * inverse
        if h + 1 < heads:
            out_rows[h, at] = result
        else:
            result = jnp.concatenate([out_rows[k, at] for k in range(h)] + [result], axis=1)
            out_tiles[at] = result.reshape(ROW_TILE * heads, head_dim).astype(out_tiles.dtype)
        bad = jnp.where(total < SAFE_TOTAL, 0.0, 1.0)
        worst[...] = jnp.maximum(
            worst[...], jnp.max(bad.reshape(ROW_TILE // 8, 8, head_dim), axis=0)
        )

    def finish_all(parts):
        copies = []
        for h in range(heads):
            for at, (b, start) in enumerate(tiles_of(shape)):
                rows = pl.ds(b * shape.rows_unit + start, ROW_TILE)
                sums = acc_ref[h, rows, :]
                if parts:
                    sums = sums + mixed_tile(shape, parts[h], h, b, rows, q_ref, peak_ref)
                finish(h, at, sums)
                if h + 1 < heads:
                    continue
                copies.append(
                    pltpu.make_async_copy(
                        out_tiles.at[at],
                        out_ref.at[pl.ds(rows.start * heads, ROW_TILE * heads), :],
                        out_sems.at[at],
                    )
                )
                copies[-1].start()
        for copy in copies:
            copy.wait()

    worst[...] = jnp.zeros_like(worst)
    numbers = slot_numbers(slots)
    for_each_form(
        shape, slots,
        lambda here: finish_all([
            parts_of(shape, [numbers[i] for i in here], h, mask_ref, [piece_refs[i] for i in here])
            for h in range(heads)
        ] if here else []),
    )

    @pl.when(jnp.max(worst[...]) > 0.0)
    def _():
        copies = read_lists(list_refs, lists, sems) + [
            pltpu.make_async_copy(all_refs[i], kv.at[i], sems.at[n_lists + i])
            for i in range(n_all)
        ]
        for copy in copies:
            copy.start()
        for copy in copies:
            copy.wait()
        mark_allowed(shape, *lists, allowed_ref)

        def every_tile(step):
            def slot_step(i, carry):
                owner = owner_of(shape, seq_pos, i)

                @pl.when((owner >= 0) & (owner <= seq_pos))
                def _():
                    for h in range(heads):
                        for b, start in tiles_of(shape):
                            rows = pl.ds(b * shape.rows_unit + start, ROW_TILE)
                            s = scores(q_ref[h, rows, :], kv[i, h]) * shape.factor
                            columns = []
                            for j in range(shape.blocks_here):
                                block = owner * shape.blocks_here + j
                                part = s[:, j * BLOCK:(j + 1) * BLOCK]
                                row = start + lax.broadcasted_iota(jnp.int32, part.shape, 0)
                                column = lax.broadcasted_iota(jnp.int32, part.shape, 1)
                                ahead = (first_block + b - block) * BLOCK
                                part = jnp.where(
                                    (column - ahead) * shape.group <= row, part, HIDDEN
                                )
                                seen = allowed_ref[h, b, block] > 0
                                columns.append(part + jnp.where(seen, 0.0, HIDDEN))
                            step(h, rows, jnp.concatenate(columns, axis=1), i)

                return carry

            lax.fori_loop(0, n_all, slot_step, 0)

        def widen(h, rows, s, i):
            m = jnp.max(s, axis=1, keepdims=True)
            peak_ref[h, rows, :] = jnp.maximum(peak_ref[h, rows, :], m)

        def collect(h, rows, s, i):
            m = peak_ref[h, rows, :]
            p = jnp.exp2(s - jnp.concatenate([m] * shape.blocks_here, axis=1))
            acc_ref[h, rows, :] += jnp.dot(
                p.astype(jnp.bfloat16), with_ones(kv[i, heads + h]),
                preferred_element_type=jnp.float32,
            )

        every_tile(widen)
        acc_ref[...] = jnp.zeros_like(acc_ref)
        every_tile(collect)
        finish_all([])


def per_device(
    n_seq, queries, keys, values, retrieval_ids, vertical_blocks, slash_offsets, sink_blocks,
    window_blocks,
):
    tokens_here, heads, width = queries.shape
    head_dim = keys.shape[2]
    group = width // head_dim
    blocks_here = tokens_here // BLOCK
    shape = Shape(heads, blocks_here, n_seq * blocks_here, group, head_dim, n_seq)
    outer = shape.outer

    vmem = pl.BlockSpec(memory_space=pltpu.VMEM)
    hbm = pl.BlockSpec(memory_space=pltpu.HBM)
    anywhere = pl.BlockSpec(memory_space=pl.ANY)
    mask_shape = jax.ShapeDtypeStruct(
        (heads, blocks_here, shape.block_total, head_dim), jnp.float32
    )
    q_shape = jax.ShapeDtypeStruct((heads, shape.rows, head_dim), jnp.bfloat16)
    peak_shape = jax.ShapeDtypeStruct((heads, shape.rows, head_dim), jnp.float32)
    acc_shape = jax.ShapeDtypeStruct((heads, shape.rows, 2 * head_dim), jnp.float32)
    allowed_scratch = pltpu.SMEM((heads, blocks_here, shape.block_total), jnp.int32)
    params = pltpu.CompilerParams(vmem_limit_bytes=16 << 20)
    cost = pl.CostEstimate(flops=1 << 20, transcendentals=0, bytes_accessed=1 << 10)

    own = jnp.concatenate(
        [jnp.transpose(keys, (1, 0, 2)), jnp.transpose(values, (1, 0, 2))], axis=0
    )
    q_raw = queries.reshape(tokens_here, heads, group, head_dim)
    q_raw = jnp.transpose(q_raw, (0, 2, 1, 3)).reshape(heads * shape.rows, head_dim)
    q_raw = pltpu.with_memory_space_constraint(q_raw, pltpu.HBM)
    lists = tuple(
        pltpu.with_memory_space_constraint(x, pltpu.HBM)
        for x in (retrieval_ids, vertical_blocks, slash_offsets, sink_blocks, window_blocks)
    )
    n_lists = len(lists)
    list_scratch = [pltpu.SMEM(x.shape, jnp.int32) for x in lists]

    def prepare(q_raw):
        return pl.pallas_call(
            functools.partial(prepare_kernel, shape, n_lists),
            out_shape=(mask_shape, q_shape),
            in_specs=[hbm] * (n_lists + 1),
            out_specs=(vmem, vmem),
            scratch_shapes=[
                pltpu.VMEM((heads * shape.rows, head_dim), jnp.bfloat16),
                pltpu.VMEM((heads * shape.rows, head_dim), jnp.float32),
                allowed_scratch,
                *list_scratch,
                pltpu.SemaphoreType.DMA((n_lists + 1,)),
            ],
            compiler_params=params,
            cost_estimate=cost,
        )(*lists, q_raw)

    def start_sums(slots=(), cost=cost):
        return pl.pallas_call(
            functools.partial(own_kernel, shape, slots),
            out_shape=(peak_shape, acc_shape),
            in_specs=[vmem] * (3 + len(slots)),
            out_specs=(vmem, vmem),
            compiler_params=params,
            cost_estimate=cost,
        )(mask, q, own, *[piece[slot] for slot in slots])

    def add(acc, slots, cost=cost):
        return pl.pallas_call(
            functools.partial(middle_kernel, shape, slots),
            out_shape=acc_shape,
            in_specs=[vmem] * (4 + len(slots)),
            out_specs=vmem,
            input_output_aliases={3: 0},
            compiler_params=params,
            cost_estimate=cost,
        )(mask, q, peak, acc, *[piece[slot] for slot in slot_numbers(slots)])

    def send(x, pairs):
        return lax.ppermute(x, "seq", pairs)

    def along(x, least, step=1, most=outer):
        return send(x, [
            (s, s + step * INNER) for s in range(n_seq)
            if least <= s // INNER < min(most, outer - step)
        ])

    def across(x, least):
        return send(x, [
            (s, s ^ 1) for s in range(n_seq)
            if s // INNER >= least and (least > 0 or s % INNER == 0)
        ])

    piece = {0: own}
    if outer == 4:
        first = [along(own, k, most=k + 1) for k in range(3)]
        piece[4] = send(own, [(s, s ^ 1) for s in range(n_seq) if s % INNER == 0 or s == 1])
        second = [None, along(first[0], 1, most=2), along(first[1], 2)]
        q_raw, first[0] = lax.optimization_barrier((q_raw, first[0]))
        mask, q = prepare(q_raw)
        piece[1] = first[0] + first[1] + first[2]
        piece[1], q = lax.optimization_barrier((piece[1], q))
        piece[5] = across(piece[1], 1)
        piece[7] = along(piece[4], 0, step=3, most=1)
        q, second[1], piece[4] = lax.optimization_barrier((q, second[1], piece[4]))
        piece[3] = along(second[1], 2)
        piece[2] = second[1] + second[2]
        piece[6] = across(piece[2], 2)
        heavy = pl.CostEstimate(flops=1 << 36, transcendentals=0, bytes_accessed=1 << 10)
        peak, acc = start_sums([1, 4], heavy)
        acc = add(acc, [2, 5])
        acc = add(acc, [7, (6, 3, 4)])
        last_slots = [3, (6, 2, 3)]
    else:
        mask, q = prepare(q_raw)
        peak, acc = start_sums()
        for step in range(outer):
            if step + 1 < outer:
                piece[step + 1] = along(piece[step], step)
            piece[outer + step] = across(piece[step], step)
            if step > 0:
                acc = add(acc, [step, outer + step - 1])
            if step + 1 < outer:
                piece[step + 1], acc = lax.optimization_barrier((piece[step + 1], acc))
        last_slots = [n_seq - 1]

    out, _, _ = pl.pallas_call(
        functools.partial(last_kernel, shape, last_slots, n_lists),
        out_shape=(
            jax.ShapeDtypeStruct((heads * shape.rows, head_dim), jnp.bfloat16),
            peak_shape,
            acc_shape,
        ),
        in_specs=[vmem] * (4 + len(last_slots)) + [anywhere] * n_seq + [hbm] * n_lists,
        out_specs=(hbm, vmem, vmem),
        input_output_aliases={2: 1, 3: 2},
        scratch_shapes=[
            pltpu.VMEM((heads - 1, shape.rows // ROW_TILE, ROW_TILE, head_dim), jnp.float32),
            pltpu.VMEM((shape.rows // ROW_TILE, heads * ROW_TILE, head_dim), jnp.bfloat16),
            pltpu.VMEM((8, head_dim), jnp.float32),
            pltpu.VMEM((n_seq,) + own.shape, jnp.bfloat16),
            allowed_scratch,
            *list_scratch,
            pltpu.SemaphoreType.DMA((n_lists + n_seq,)),
            pltpu.SemaphoreType.DMA((shape.rows // ROW_TILE,)),
        ],
        compiler_params=pltpu.CompilerParams(
            vmem_limit_bytes=(16 << 20) + 2 * n_seq * own.size
        ),
        cost_estimate=cost,
    )(
        mask, q, peak, acc, *[piece[slot] for slot in slot_numbers(last_slots)],
        *[piece[slot] for slot in range(n_seq)], *lists,
    )
    out = out.reshape(tokens_here, group, heads, head_dim)
    return jnp.transpose(out, (0, 2, 1, 3)).reshape(tokens_here, heads, width)


def solution(mesh):
    in_specs = (
        P("seq", "head", None),
        P("seq", "head", None),
        P("seq", "head", None),
        P(),
        P("seq", None, None),
        P("seq", None, None),
        P(),
        P(),
    )
    out_specs = P("seq", "head", None)
    return jax.shard_map(
        functools.partial(per_device, mesh.shape["seq"]),
        mesh=mesh, in_specs=in_specs, out_specs=out_specs, check_vma=False,
    )
```

```python
import functools
import math

import jax
import jax.numpy as jnp
from jax import lax
from jax.experimental import pallas as pl
from jax.experimental.pallas import tpu as pltpu
from jax.sharding import PartitionSpec as P

KV_HEADS = 8
BLOCK = 128
INNER = 2
ROW_TILE = 512
PIECES_AT_ONCE = 1
HIDDEN = -1e30
SAFE_TOTAL = 1e30


class Shape:
    def __init__(self, heads, blocks_here, block_total, group, head_dim, n_slots):
        self.heads = heads
        self.blocks_here = blocks_here
        self.block_total = block_total
        self.group = group
        self.head_dim = head_dim
        self.n_slots = n_slots
        self.outer = n_slots // INNER
        self.rows_unit = BLOCK * group
        self.rows = blocks_here * self.rows_unit
        self.factor = head_dim ** -0.5 * math.log2(math.e)

    def away(self, slot):
        return slot % self.outer


def owner_of(shape, seq_pos, slot):
    crossed = slot >= shape.outer
    line = seq_pos // INNER - jnp.where(crossed, slot - shape.outer, slot)
    place = seq_pos % INNER
    return line * INNER + jnp.where(crossed, 1 - place, place)


def scores(q, keys):
    return lax.dot_general(q, keys, (((1,), (1,)), ((), ())), preferred_element_type=jnp.float32)


def with_ones(vals):
    return jnp.concatenate([vals, jnp.ones_like(vals)], axis=1)


def tiles_of(shape):
    return [(b, r * ROW_TILE) for b in range(shape.blocks_here)
            for r in range(shape.rows_unit // ROW_TILE)]


def mark_allowed(shape, retr_ref, vert_ref, slash_ref, sink_ref, window_ref, allowed_ref):
    first_block = lax.axis_index("seq") * shape.blocks_here
    first_head = lax.axis_index("head") * shape.heads
    n_retr = retr_ref.shape[0]
    for h in range(shape.heads):
        head_id = first_head + h
        is_retr = functools.reduce(
            jnp.logical_or, [retr_ref[i] == head_id for i in range(n_retr)]
        )
        for b in range(shape.blocks_here):
            query_block = first_block + b
            sinks = jnp.where(is_retr, 0, sink_ref[head_id])
            lowest = query_block - jnp.where(is_retr, 1, window_ref[head_id])

            def clear(c, carry):
                read = ((c < sinks) | (c > lowest)) & (c <= query_block)
                allowed_ref[h, b, c] = read.astype(jnp.int32)
                return carry

            lax.fori_loop(0, shape.block_total, clear, 0, unroll=shape.block_total <= 16)
            for j in range(vert_ref.shape[2]):
                c = vert_ref[b, head_id, j]
                allowed_ref[h, b, jnp.where(is_retr, c, query_block)] = 1
            for j in range(slash_ref.shape[2]):
                c = query_block - slash_ref[b, head_id, j]
                allowed_ref[h, b, jnp.where(is_retr, c, query_block)] = 1


def read_lists(list_refs, lists, sems):
    return [pltpu.make_async_copy(list_refs[i], lists[i], sems.at[i]) for i in range(len(lists))]


def prepare_kernel(shape, n_lists, *refs):
    list_refs, q_raw_ref, mask_ref, q_ref = refs[:n_lists], *refs[n_lists:n_lists + 3]
    q_raw, wide, allowed_ref, *lists, sems = refs[n_lists + 3:]
    seq_pos = lax.axis_index("seq")
    copies = read_lists(list_refs, lists, sems)
    for copy in copies:
        copy.start()
    q_copy = pltpu.make_async_copy(q_raw_ref, q_raw, sems.at[n_lists])
    q_copy.start()
    for copy in copies + [q_copy]:
        copy.wait()
    mark_allowed(shape, *lists, allowed_ref)
    wide[...] = q_raw[...].astype(jnp.float32)
    for h in range(shape.heads):
        q_ref[h] = wide[pl.ds(h, shape.rows, stride=shape.heads), :].astype(q_ref.dtype)

    def fill_masks(slot, carry):
        owner = owner_of(shape, seq_pos, slot)
        there = (owner >= 0) & (owner <= seq_pos)
        base = jnp.where(there, owner, 0) * shape.blocks_here
        for h in range(shape.heads):
            for b in range(shape.blocks_here):
                for j in range(shape.blocks_here):
                    seen = there & (allowed_ref[h, b, base + j] > 0)
                    mask_ref[h, b, pl.ds(slot * shape.blocks_here + j, 1), :] = jnp.full(
                        (1, shape.head_dim), jnp.where(seen, 1.0, 0.0), jnp.float32
                    )
        return carry

    lax.fori_loop(0, shape.n_slots, fill_masks, 0, unroll=shape.n_slots <= 8)


def parts_of(shape, slots, h, mask_ref, piece_refs):
    parts = []
    for at in range(0, len(slots), PIECES_AT_ONCE):
        some_slots = slots[at:at + PIECES_AT_ONCE]
        some_refs = piece_refs[at:at + PIECES_AT_ONCE]
        vals = jnp.concatenate([ref[shape.heads + h] for ref in some_refs], axis=0)
        seen_vals = []
        for b in range(shape.blocks_here):
            masks = jnp.concatenate(
                [
                    jnp.broadcast_to(
                        mask_ref[h, b, pl.ds(slot * shape.blocks_here + j, 1), :],
                        (BLOCK, shape.head_dim),
                    )
                    for slot in some_slots for j in range(shape.blocks_here)
                ],
                axis=0,
            ).astype(jnp.bfloat16)
            seen_vals.append(jnp.concatenate([vals * masks, masks], axis=1))
        parts.append((jnp.concatenate([ref[h] for ref in some_refs], axis=0), seen_vals))
    return parts


def mixed_tile(shape, parts, h, b, rows, q_ref, peak_ref):
    q = q_ref[h, rows, :]
    m = peak_ref[h, rows, :]
    mixed = None
    for keys, seen_vals in parts:
        s = scores(q, keys) * shape.factor
        p = jnp.exp2(s - jnp.concatenate([m] * (s.shape[1] // m.shape[1]), axis=1))
        part = jnp.dot(p.astype(jnp.bfloat16), seen_vals[b], preferred_element_type=jnp.float32)
        mixed = part if mixed is None else mixed + part
    return mixed


def for_each_form(shape, slots, work):
    line = lax.axis_index("seq") // INNER
    spans = [
        slot[1:] if isinstance(slot, tuple) else (shape.away(slot), shape.outer)
        for slot in slots
    ]
    steps = sorted({0, shape.outer}.union(*spans))
    for least, below in zip(steps, steps[1:]):
        here = [i for i, span in enumerate(spans) if span[0] <= least < span[1]]
        pl.when((line >= least) & (line < below))(functools.partial(work, here))


def slot_numbers(slots):
    return [slot[0] if isinstance(slot, tuple) else slot for slot in slots]


def own_kernel(shape, slots, mask_ref, q_ref, own_ref, *refs):
    piece_refs, peak_ref, acc_ref = refs[:-2], refs[-2], refs[-1]

    def work(here):
        for h in range(shape.heads):
            parts = parts_of(
                shape, [slots[i] for i in here], h, mask_ref, [piece_refs[i] for i in here]
            )
            for b, start in tiles_of(shape):
                rows = pl.ds(b * shape.rows_unit + start, ROW_TILE)
                width = (b + 1) * BLOCK
                s = scores(q_ref[h, rows, :], own_ref[h, :width, :]) * shape.factor
                columns = []
                for j in range(b):
                    seen = mask_ref[h, b, pl.ds(j, 1), :]
                    columns.append(
                        jnp.where(seen > 0.0, s[:, j * BLOCK:(j + 1) * BLOCK], HIDDEN)
                    )
                diagonal = s[:, b * BLOCK:]
                row = start + lax.broadcasted_iota(jnp.int32, diagonal.shape, 0)
                column = lax.broadcasted_iota(jnp.int32, diagonal.shape, 1)
                columns.append(jnp.where(column * shape.group <= row, diagonal, HIDDEN))
                s = jnp.concatenate(columns, axis=1)
                m = jnp.max(s, axis=1, keepdims=True)
                peak_ref[h, rows, :] = jnp.broadcast_to(m, (ROW_TILE, BLOCK))
                p = jnp.exp2(s - m).astype(jnp.bfloat16)
                vals = with_ones(own_ref[shape.heads + h, :width, :])
                sums = jnp.dot(p, vals, preferred_element_type=jnp.float32)
                if parts:
                    sums += mixed_tile(shape, parts, h, b, rows, q_ref, peak_ref)
                acc_ref[h, rows, :] = sums

    for_each_form(shape, slots, work)


def middle_kernel(shape, slots, mask_ref, q_ref, peak_ref, acc_in, *refs):
    del acc_in
    piece_refs, acc_ref = refs[:-1], refs[-1]
    numbers = slot_numbers(slots)

    def work(here):
        for h in range(shape.heads if here else 0):
            parts = parts_of(
                shape, [numbers[i] for i in here], h, mask_ref, [piece_refs[i] for i in here]
            )
            for b, start in tiles_of(shape):
                rows = pl.ds(b * shape.rows_unit + start, ROW_TILE)
                acc_ref[h, rows, :] += mixed_tile(shape, parts, h, b, rows, q_ref, peak_ref)

    for_each_form(shape, slots, work)


def last_kernel(shape, slots, n_lists, mask_ref, q_ref, peak_in, acc_in, *refs):
    del peak_in, acc_in
    heads, head_dim = shape.heads, shape.head_dim
    n, n_all = len(slots), shape.n_slots
    piece_refs, all_refs, list_refs = refs[:n], refs[n:n + n_all], refs[n + n_all:][:n_lists]
    out_ref, peak_ref, acc_ref, *scratch = refs[n + n_all + n_lists:]
    out_rows, out_tiles, worst, kv, allowed_ref, *lists, sems, out_sems = scratch
    seq_pos = lax.axis_index("seq")
    first_block = seq_pos * shape.blocks_here

    def finish(h, at, sums):
        total = sums[:, head_dim:]
        inverse = pl.reciprocal(total, approx=True)
        inverse = inverse * (2.0 - total * inverse)
        result = sums[:, :head_dim] * inverse
        if h + 1 < heads:
            out_rows[h, at] = result
        else:
            result = jnp.concatenate([out_rows[k, at] for k in range(h)] + [result], axis=1)
            out_tiles[at] = result.reshape(ROW_TILE * heads, head_dim).astype(out_tiles.dtype)
        bad = jnp.where(total < SAFE_TOTAL, 0.0, 1.0)
        worst[...] = jnp.maximum(
            worst[...], jnp.max(bad.reshape(ROW_TILE // 8, 8, head_dim), axis=0)
        )

    def finish_all(parts):
        copies = []
        for h in range(heads):
            for at, (b, start) in enumerate(tiles_of(shape)):
                rows = pl.ds(b * shape.rows_unit + start, ROW_TILE)
                sums = acc_ref[h, rows, :]
                if parts:
                    sums = sums + mixed_tile(shape, parts[h], h, b, rows, q_ref, peak_ref)
                finish(h, at, sums)
                if h + 1 < heads:
                    continue
                copies.append(
                    pltpu.make_async_copy(
                        out_tiles.at[at],
                        out_ref.at[pl.ds(rows.start * heads, ROW_TILE * heads), :],
                        out_sems.at[at],
                    )
                )
                copies[-1].start()
        for copy in copies:
            copy.wait()

    worst[...] = jnp.zeros_like(worst)
    numbers = slot_numbers(slots)
    for_each_form(
        shape, slots,
        lambda here: finish_all([
            parts_of(shape, [numbers[i] for i in here], h, mask_ref, [piece_refs[i] for i in here])
            for h in range(heads)
        ] if here else []),
    )

    @pl.when(jnp.max(worst[...]) > 0.0)
    def _():
        copies = read_lists(list_refs, lists, sems) + [
            pltpu.make_async_copy(all_refs[i], kv.at[i], sems.at[n_lists + i])
            for i in range(n_all)
        ]
        for copy in copies:
            copy.start()
        for copy in copies:
            copy.wait()
        mark_allowed(shape, *lists, allowed_ref)

        def every_tile(step):
            def slot_step(i, carry):
                owner = owner_of(shape, seq_pos, i)

                @pl.when((owner >= 0) & (owner <= seq_pos))
                def _():
                    for h in range(heads):
                        for b, start in tiles_of(shape):
                            rows = pl.ds(b * shape.rows_unit + start, ROW_TILE)
                            s = scores(q_ref[h, rows, :], kv[i, h]) * shape.factor
                            columns = []
                            for j in range(shape.blocks_here):
                                block = owner * shape.blocks_here + j
                                part = s[:, j * BLOCK:(j + 1) * BLOCK]
                                row = start + lax.broadcasted_iota(jnp.int32, part.shape, 0)
                                column = lax.broadcasted_iota(jnp.int32, part.shape, 1)
                                ahead = (first_block + b - block) * BLOCK
                                part = jnp.where(
                                    (column - ahead) * shape.group <= row, part, HIDDEN
                                )
                                seen = allowed_ref[h, b, block] > 0
                                columns.append(part + jnp.where(seen, 0.0, HIDDEN))
                            step(h, rows, jnp.concatenate(columns, axis=1), i)

                return carry

            lax.fori_loop(0, n_all, slot_step, 0)

        def widen(h, rows, s, i):
            m = jnp.max(s, axis=1, keepdims=True)
            peak_ref[h, rows, :] = jnp.maximum(peak_ref[h, rows, :], m)

        def collect(h, rows, s, i):
            m = peak_ref[h, rows, :]
            p = jnp.exp2(s - jnp.concatenate([m] * shape.blocks_here, axis=1))
            acc_ref[h, rows, :] += jnp.dot(
                p.astype(jnp.bfloat16), with_ones(kv[i, heads + h]),
                preferred_element_type=jnp.float32,
            )

        every_tile(widen)
        acc_ref[...] = jnp.zeros_like(acc_ref)
        every_tile(collect)
        finish_all([])


def per_device(
    n_seq, queries, keys, values, retrieval_ids, vertical_blocks, slash_offsets, sink_blocks,
    window_blocks,
):
    tokens_here, heads, width = queries.shape
    head_dim = keys.shape[2]
    group = width // head_dim
    blocks_here = tokens_here // BLOCK
    shape = Shape(heads, blocks_here, n_seq * blocks_here, group, head_dim, n_seq)
    outer = shape.outer

    vmem = pl.BlockSpec(memory_space=pltpu.VMEM)
    hbm = pl.BlockSpec(memory_space=pltpu.HBM)
    anywhere = pl.BlockSpec(memory_space=pl.ANY)
    mask_shape = jax.ShapeDtypeStruct(
        (heads, blocks_here, shape.block_total, head_dim), jnp.float32
    )
    q_shape = jax.ShapeDtypeStruct((heads, shape.rows, head_dim), jnp.bfloat16)
    peak_shape = jax.ShapeDtypeStruct((heads, shape.rows, head_dim), jnp.float32)
    acc_shape = jax.ShapeDtypeStruct((heads, shape.rows, 2 * head_dim), jnp.float32)
    allowed_scratch = pltpu.SMEM((heads, blocks_here, shape.block_total), jnp.int32)
    params = pltpu.CompilerParams(vmem_limit_bytes=16 << 20)
    cost = pl.CostEstimate(flops=1 << 20, transcendentals=0, bytes_accessed=1 << 10)

    own = jnp.concatenate(
        [jnp.transpose(keys, (1, 0, 2)), jnp.transpose(values, (1, 0, 2))], axis=0
    )
    q_raw = queries.reshape(tokens_here, heads, group, head_dim)
    q_raw = jnp.transpose(q_raw, (0, 2, 1, 3)).reshape(heads * shape.rows, head_dim)
    q_raw = pltpu.with_memory_space_constraint(q_raw, pltpu.HBM)
    lists = tuple(
        pltpu.with_memory_space_constraint(x, pltpu.HBM)
        for x in (retrieval_ids, vertical_blocks, slash_offsets, sink_blocks, window_blocks)
    )
    n_lists = len(lists)
    list_scratch = [pltpu.SMEM(x.shape, jnp.int32) for x in lists]

    def prepare(q_raw):
        return pl.pallas_call(
            functools.partial(prepare_kernel, shape, n_lists),
            out_shape=(mask_shape, q_shape),
            in_specs=[hbm] * (n_lists + 1),
            out_specs=(vmem, vmem),
            scratch_shapes=[
                pltpu.VMEM((heads * shape.rows, head_dim), jnp.bfloat16),
                pltpu.VMEM((heads * shape.rows, head_dim), jnp.float32),
                allowed_scratch,
                *list_scratch,
                pltpu.SemaphoreType.DMA((n_lists + 1,)),
            ],
            compiler_params=params,
            cost_estimate=cost,
        )(*lists, q_raw)

    def start_sums(slots=(), cost=cost):
        return pl.pallas_call(
            functools.partial(own_kernel, shape, slots),
            out_shape=(peak_shape, acc_shape),
            in_specs=[vmem] * (3 + len(slots)),
            out_specs=(vmem, vmem),
            compiler_params=params,
            cost_estimate=cost,
        )(mask, q, own, *[piece[slot] for slot in slots])

    def add(acc, slots, cost=cost):
        return pl.pallas_call(
            functools.partial(middle_kernel, shape, slots),
            out_shape=acc_shape,
            in_specs=[vmem] * (4 + len(slots)),
            out_specs=vmem,
            input_output_aliases={3: 0},
            compiler_params=params,
            cost_estimate=cost,
        )(mask, q, peak, acc, *[piece[slot] for slot in slot_numbers(slots)])

    def send(x, pairs):
        return lax.ppermute(x, "seq", pairs)

    def along(x, least, step=1, most=outer):
        return send(x, [
            (s, s + step * INNER) for s in range(n_seq)
            if least <= s // INNER < min(most, outer - step)
        ])

    def across(x, least):
        return send(x, [
            (s, s ^ 1) for s in range(n_seq)
            if s // INNER >= least and (least > 0 or s % INNER == 0)
        ])

    piece = {0: own}
    if outer == 4:
        first = [along(own, k, most=k + 1) for k in range(3)]
        piece[4] = send(own, [(s, s ^ 1) for s in range(n_seq) if s % INNER == 0 or s == 1])
        second = [None, along(first[0], 1, most=2), along(first[1], 2)]
        q_raw, first[0] = lax.optimization_barrier((q_raw, first[0]))
        mask, q = prepare(q_raw)
        piece[1] = first[0] + first[1] + first[2]
        piece[1], q = lax.optimization_barrier((piece[1], q))
        piece[5] = across(piece[1], 1)
        piece[7] = along(piece[4], 0, step=3, most=1)
        q, second[1], piece[4] = lax.optimization_barrier((q, second[1], piece[4]))
        piece[3] = along(second[1], 2)
        piece[2] = second[1] + second[2]
        piece[6] = across(piece[2], 2)
        heavy = pl.CostEstimate(flops=1 << 36, transcendentals=0, bytes_accessed=1 << 10)
        peak, acc = start_sums([1, 4], heavy)
        acc = add(acc, [2, 5])
        acc = add(acc, [7, (6, 3, 4)])
        last_slots = [3, (6, 2, 3)]
    else:
        mask, q = prepare(q_raw)
        peak, acc = start_sums()
        for step in range(outer):
            if step + 1 < outer:
                piece[step + 1] = along(piece[step], step)
            piece[outer + step] = across(piece[step], step)
            if step > 0:
                acc = add(acc, [step, outer + step - 1])
            if step + 1 < outer:
                piece[step + 1], acc = lax.optimization_barrier((piece[step + 1], acc))
        last_slots = [n_seq - 1]

    out, _, _ = pl.pallas_call(
        functools.partial(last_kernel, shape, last_slots, n_lists),
        out_shape=(
            jax.ShapeDtypeStruct((heads * shape.rows, head_dim), jnp.bfloat16),
            peak_shape,
            acc_shape,
        ),
        in_specs=[vmem] * (4 + len(last_slots)) + [anywhere] * n_seq + [hbm] * n_lists,
        out_specs=(hbm, vmem, vmem),
        input_output_aliases={2: 1, 3: 2},
        scratch_shapes=[
            pltpu.VMEM((heads - 1, shape.rows // ROW_TILE, ROW_TILE, head_dim), jnp.float32),
            pltpu.VMEM((shape.rows // ROW_TILE, heads * ROW_TILE, head_dim), jnp.bfloat16),
            pltpu.VMEM((8, head_dim), jnp.float32),
            pltpu.VMEM((n_seq,) + own.shape, jnp.bfloat16),
            allowed_scratch,
            *list_scratch,
            pltpu.SemaphoreType.DMA((n_lists + n_seq,)),
            pltpu.SemaphoreType.DMA((shape.rows // ROW_TILE,)),
        ],
        compiler_params=pltpu.CompilerParams(
            vmem_limit_bytes=(16 << 20) + 2 * n_seq * own.size
        ),
        cost_estimate=cost,
    )(
        mask, q, peak, acc, *[piece[slot] for slot in slot_numbers(last_slots)],
        *[piece[slot] for slot in range(n_seq)], *lists,
    )
    out = out.reshape(tokens_here, group, heads, head_dim)
    return jnp.transpose(out, (0, 2, 1, 3)).reshape(tokens_here, heads, width)


def solution(mesh):
    in_specs = (
        P("seq", "head", None),
        P("seq", "head", None),
        P("seq", "head", None),
        P(),
        P("seq", None, None),
        P("seq", None, None),
        P(),
        P(),
    )
    out_specs = P("seq", "head", None)
    return jax.shard_map(
        functools.partial(per_device, mesh.shape["seq"]),
        mesh=mesh, in_specs=in_specs, out_specs=out_specs, check_vma=False,
    )
```
